32 devices in a mesh: section: 2 (over core), dp: 8 (over z, y), tensor: 2 (over x).
Axes of the slice: x: 2, y: 2, z: 4, core: 2. Of those that a mesh axis runs over, the one named last changes fastest.
Arguments:
- inputs: bfloat16 [16, 512, 768], P('dp'), may hold values from -6 to 6
- segments: int32 [16, 512], P('dp'), may hold values from 0 to 15, never falling along the last dimension, each value on 1 to 64 neighbouring positions
- partner: int32 [16, 16], P('dp'), may hold values from 0 to 15, as said below
- grad_output: bfloat16 [16, 512, 768], P('dp'), may hold values from -6 to 6
- w_qkv: bfloat16 [2, 768, 3, 768], P('section', 'dp', None, 'tensor'), may hold values from -0.21875 to 0.21875
- w_out: bfloat16 [2, 768, 768], P('section', 'tensor', 'dp'), may hold values from -0.875 to 0.875
- w_up: bfloat16 [2, 768, 3072], P('section', 'dp', 'tensor'), may hold values from -0.21875 to 0.21875
- w_down: bfloat16 [2, 3072, 768], P('section', 'tensor', 'dp'), may hold values from -0.109375 to 0.109375
- norm_gain: bfloat16 [2, 2, 768], P('section', None, 'dp'), may hold values from 0.25 to 1.75
- norm_shift: bfloat16 [2, 2, 768], P('section', None, 'dp'), may hold values from -3 to 3
Outputs:
- layer_outputs: bfloat16 [2, 16, 512, 768], P('section', 'dp')
- input_grads: bfloat16 [2, 16, 512, 768], P('section', 'dp')
- grad_qkv: float32 [2, 768, 3, 768], P('section', 'dp', None, 'tensor')
- grad_out: float32 [2, 768, 768], P('section', 'tensor', 'dp')
- grad_up: float32 [2, 768, 3072], P('section', 'dp', 'tensor')
- grad_down: float32 [2, 3072, 768], P('section', 'tensor', 'dp')
- grad_gain: float32 [2, 2, 768], P('section', None, 'dp')
- grad_shift: float32 [2, 2, 768], P('section', None, 'dp')
The draws below stay inside these ranges and needn't reach their ends.
Inputs may be any that keep to these rules, and one draw needn't show every extreme that they name: partner pairs the segments of a row: an even segment maps to an odd one and back, and partner of partner is the segment itself. Each row holds all 16 segments in order, of 1 to 64 tokens, at least one of exactly 64.
All inputs are finite; a program needn't handle non-finite values.
Results may differ from the reference program's by a relative error of at most 0.028.
Values may be sent and summed in bfloat16 or wider, within the bound.
A program may use at most 192 MiB of HBM per device.

```python
import math
import jax
import jax.numpy as jnp
import numpy as np
from jax import lax

D = 768
HEADS = 12
HEAD = 64
FF = 3072
L = 512
SEGS = 16
SEG_MOST = 64
PAIRS = 8
BATCH = 16


def draw_partner(key, part):
    key = jax.random.fold_in(key, 7)
    row_keys = jax.random.split(key, BATCH)

    def one_row(row_key):
        order = jax.random.permutation(row_key, PAIRS)
        back = jnp.argsort(order)
        even = 2 * order + 1
        odd = 2 * back
        return jnp.stack([even, odd], -1).reshape(-1).astype(jnp.int32)
    return jax.vmap(one_row)(row_keys)


def block_levels(own_key, dims, shards, least, top_value):
    def one(position, parts):
        steps = jax.random.uniform(jax.random.fold_in(jax.random.fold_in(own_key, 6), position), (parts,), jnp.float32, least / len(shards), top_value / len(shards))
        return jnp.repeat(jnp.exp(steps), dims[position] // parts).reshape((-1,) + (1,) * (len(dims) - position - 1))

    level = one(*shards[0])
    for cut in shards[1:]:
        level = level * one(*cut)
    return level


def profile(count, total, most, skew):
    weights = [(1 << 20) // math.isqrt(standing ** skew) + 1 for standing in range(2, count + 1)]
    rest, given = total - most - (count - 1), [1] * (count - 1)
    while rest > 0:
        free = [i for i in range(count - 1) if given[i] < most]
        whole, remaining = sum([weights[i] for i in free]), rest
        for i in free:
            extra = min(most - given[i], max(1, remaining * weights[i] // whole), rest)
            given[i] = given[i] + extra
            rest = rest - extra
    return np.array([most] + given)


def ragged(rng, count, total, most, slope):
    if count == 2:
        one = jax.random.randint(rng, (), max(1, total - most), min(most, total - 1) + 1)
        return jnp.stack([one, total - one])
    lengths = jnp.asarray(profile(count, total, most, slope), jnp.int32)
    twos = (count - 1) // 2
    donor, receiver = lengths[1:1 + 2 * twos:2], lengths[2:2 + 2 * twos:2]
    room = jnp.minimum(donor - 1, most - receiver)
    moved = jax.random.randint(jax.random.fold_in(rng, 1), (twos,), 0, 1 << 20) % (room + 1)
    lengths = lengths.at[1:1 + 2 * twos:2].set(donor - moved).at[2:2 + 2 * twos:2].set(receiver + moved)
    return lengths[jax.random.permutation(jax.random.fold_in(rng, 2), count)]


def centred(rng, extent, deviation, most, shards=(), kind=jnp.bfloat16):
    array = deviation * jax.random.normal(rng, extent, jnp.float32)
    if shards:
        array = array * block_levels(rng, extent, shards, -0.22, 0.18)
    return jnp.clip(array, -most, most).astype(kind)


def setup_inputs(seed: int = 0) -> dict:
    splits = jax.random.split(jax.random.key(seed), 11)
    inputs = centred(splits[0], (BATCH, L, D), 1.0, 6.0, ((0, 8),))
    segments = jax.vmap(lambda own: jnp.searchsorted(jnp.cumsum(ragged(own, SEGS, L, SEG_MOST, 0)), jnp.arange(L), side="right"))(jax.random.split(splits[1], BATCH)).reshape((BATCH, L)).astype(jnp.int32)
    partner = draw_partner(jax.random.fold_in(splits[10], 71), 0)
    grad_output = centred(splits[3], (BATCH, L, D), 1.0, 6.0, ((0, 8),))
    w_qkv = centred(splits[4], (2, D, 3, D), D ** -0.5, 0.21875, ((0, 2), (1, 8), (3, 2)))
    w_out = centred(splits[5], (2, D, D), (D // 16) ** -0.5, 0.875, ((0, 2), (1, 2), (2, 8)))
    w_up = centred(splits[6], (2, D, FF), D ** -0.5, 0.21875, ((0, 2), (1, 8), (2, 2)))
    w_down = centred(splits[7], (2, FF, D), FF ** -0.5, 0.109375, ((0, 2), (1, 2), (2, 8)))
    norm_gain = jnp.clip(1.0 + 0.15 * jax.random.normal(splits[8], (2, 2, D), jnp.float32), 0.25, 1.75).astype(jnp.bfloat16)
    norm_shift = centred(splits[9], (2, 2, D), 0.5, 3.0, ((0, 2), (2, 8)))
    return {"inputs": inputs, "segments": segments, "partner": partner, "grad_output": grad_output, "w_qkv": w_qkv, "w_out": w_out, "w_up": w_up, "w_down": w_down, "norm_gain": norm_gain, "norm_shift": norm_shift}


@jax.custom_vjp
def low(v):
    return lax.optimization_barrier(v.astype(jnp.bfloat16)).astype(jnp.float32)

@jax.custom_vjp
def low_back(v):
    return v

def low_keep(v):
    return (low(v), None)

def low_pass(kept, grad):
    return (grad,)

def back_keep(v):
    return (v, None)

def back_low(kept, grad):
    return (low(grad),)
low.defvjp(low_keep, low_pass)
low_back.defvjp(back_keep, back_low)
norm_eps = 1e-06
score_scale = 0.125
masked_value = -1000000000.0
best = lax.Precision.HIGHEST

def partner_of(segment_ids, partner):
    table = jnp.arange(partner.shape[-1], dtype=jnp.int32)
    hits = segment_ids[..., None] == table
    return lax.optimization_barrier(jnp.sum(jnp.where(hits, partner[:, None, :], 0), -1)).astype(jnp.int32)

def layer_norm(values, gain, shift):
    center = values - lax.optimization_barrier(jnp.mean(values, -1, keepdims=True))
    inverse = lax.rsqrt(lax.optimization_barrier(jnp.mean(center * center, -1, keepdims=True)) + norm_eps)
    return center * inverse * gain + shift

def attend(query, key, value, query_groups, key_groups):
    scores = low_back(jnp.einsum('qhd,khd->hqk', query, key, precision=best) * score_scale)
    allowed = query_groups[:, None] == key_groups[None, :]
    scores = jnp.where(allowed[None], scores, masked_value)
    probs = low(jax.nn.softmax(scores, -1))
    return jnp.einsum('hqk,khd->qhd', probs, value, precision=best)

def layer(inputs, w_qkv, w_out, w_up, w_down, gains, shifts, query_groups, key_groups):
    rows, length, width = inputs.shape
    flat = inputs.reshape(rows * length, width)
    packed = low_back(low(jnp.einsum('nd,dcm->ncm', flat, w_qkv, precision=best)))
    heads = packed.reshape(rows, length, 3, HEADS, HEAD)
    mixed = lax.map(jax.checkpoint(lambda item: attend(*item)), (heads[:, :, 0], heads[:, :, 1], heads[:, :, 2], query_groups, key_groups))
    mixed = low_back(low(mixed.reshape(rows * length, width)))
    attn_out = low_back(jnp.dot(mixed, w_out, precision=best))
    hidden = layer_norm(flat + attn_out, gains[0], shifts[0])
    hidden_low = low(hidden)
    pre = low_back(jnp.dot(hidden_low, w_up, precision=best))
    act = low(jax.nn.gelu(pre, approximate=False))
    ffn_out = low_back(jnp.dot(act, w_down, precision=best))
    out = layer_norm(hidden + ffn_out, gains[1], shifts[1])
    return out.reshape(rows, length, width)

def reference(inputs, segments, partner, grad_output, w_qkv, w_out, w_up, w_down, norm_gain, norm_shift):
    mapped = partner_of(segments, partner)

    def forward(first_in, nudge, wq, wo, wu, wd, gains, shifts):
        first = low(layer(first_in, wq[0], wo[0], wu[0], wd[0], gains[0], shifts[0], segments, segments))
        middle = low_back(first) + nudge
        second = layer(middle, wq[1], wo[1], wu[1], wd[1], gains[1], shifts[1], mapped, segments)
        return (first, second)
    primals = (inputs.astype(jnp.float32), jnp.zeros(inputs.shape, jnp.float32), w_qkv.astype(jnp.float32), w_out.astype(jnp.float32), w_up.astype(jnp.float32), w_down.astype(jnp.float32), norm_gain.astype(jnp.float32), norm_shift.astype(jnp.float32))
    (first, second), pullback = jax.vjp(forward, *primals)
    grads = pullback((jnp.zeros_like(first), grad_output.astype(jnp.float32)))
    layer_outputs = jnp.stack([first, second]).astype(jnp.bfloat16)
    input_grads = jnp.stack([grads[0], grads[1]]).astype(jnp.bfloat16)
    return (layer_outputs, input_grads, grads[2], grads[3], grads[4], grads[5], grads[6], grads[7])
```

```python
import jax
import jax.numpy as jnp
from jax import lax
from jax.sharding import PartitionSpec as P

HEAD = 64


norm_eps = 1e-06
score_scale = 0.125
masked_value = -1000000000.0


def partner_of(segment_ids, partner):
    table = jnp.arange(partner.shape[-1], dtype=jnp.int32)
    hits = segment_ids[..., None] == table
    return jnp.sum(jnp.where(hits, partner[None, :], 0), -1)


def layer_norm(values, gain, shift):
    center = values - jnp.mean(values, -1, keepdims=True)
    inverse = lax.rsqrt(jnp.mean(center * center, -1, keepdims=True) + norm_eps)
    normed = center * inverse
    return (normed * gain + shift, normed, inverse)


def norm_back(grad, normed, inverse, gain):
    scaled = grad * gain
    inner = (
        scaled
        - jnp.mean(scaled, -1, keepdims=True)
        - normed * jnp.mean(scaled * normed, -1, keepdims=True)
    )
    return inner * inverse


def gelu_slope(values):
    lower = 0.5 * (1.0 + lax.erf(values * 0.7071067811865476))
    density = jnp.exp(-0.5 * values * values) * 0.3989422804014327
    return lower + values * density


def swapped(value, axis):
    size = lax.axis_size(axis)
    return lax.ppermute(value, axis, [(i, size - 1 - i) for i in range(size)])


def tensor_sum(partial_value):
    low = partial_value.astype(jnp.bfloat16)
    return low.astype(jnp.float32) + swapped(low, "tensor").astype(jnp.float32)


def masked_scores(query, key, query_groups, key_groups):
    scores = (
        jnp.einsum("qhd,khd->hqk", query, key, preferred_element_type=jnp.float32) * score_scale
    )
    allowed = query_groups[:, None] == key_groups[None, :]
    return jnp.where(allowed[None], scores, masked_value)


def attend(query, key, value, query_groups, key_groups):
    scores = masked_scores(query, key, query_groups, key_groups)
    top = jnp.max(scores, -1, keepdims=True)
    expo = jnp.exp(scores - top)
    total = jnp.sum(expo, -1, keepdims=True)
    probs = (expo / total).astype(jnp.bfloat16)
    mixed = jnp.einsum("hqk,khd->qhd", probs, value, preferred_element_type=jnp.float32)
    return (mixed.astype(jnp.bfloat16), (top + jnp.log(total))[..., 0])


def attend_back(query, key, value, query_groups, key_groups, spread, grad_mixed):
    scores = masked_scores(query, key, query_groups, key_groups)
    probs = jnp.exp(scores - spread[..., None])
    probs_low = probs.astype(jnp.bfloat16)
    grad_probs = jnp.einsum("qhd,khd->hqk", grad_mixed, value, preferred_element_type=jnp.float32)
    grad_value = jnp.einsum(
        "hqk,qhd->khd", probs_low, grad_mixed, preferred_element_type=jnp.float32
    )
    row_dot = jnp.sum(probs * grad_probs, -1, keepdims=True)
    grad_scores = (probs * (grad_probs - row_dot)).astype(jnp.bfloat16)
    grad_query = (
        jnp.einsum("hqk,khd->qhd", grad_scores, key, preferred_element_type=jnp.float32)
        * score_scale
    )
    grad_key = (
        jnp.einsum("hqk,qhd->khd", grad_scores, query, preferred_element_type=jnp.float32)
        * score_scale
    )
    return jnp.stack(
        [
            grad_query.astype(jnp.bfloat16),
            grad_key.astype(jnp.bfloat16),
            grad_value.astype(jnp.bfloat16),
        ],
        1,
    )


def layer_forward(flat, weights, query_groups, key_groups):
    w_qkv, w_out, w_up, w_down, gains, shifts = weights
    length = flat.shape[0]
    local = w_qkv.shape[2]
    packed = jnp.einsum("nd,dcm->ncm", flat, w_qkv, preferred_element_type=jnp.float32).astype(
        jnp.bfloat16
    )
    heads = packed.reshape(length, 3, local // HEAD, HEAD)
    mixed, spread = attend(heads[:, 0], heads[:, 1], heads[:, 2], query_groups, key_groups)
    mixed_flat = mixed.reshape(length, local)
    attn_out = tensor_sum(jnp.dot(mixed_flat, w_out, preferred_element_type=jnp.float32))
    hidden, normed_first, inverse_first = layer_norm(
        flat.astype(jnp.float32) + attn_out, gains[0], shifts[0]
    )
    hidden_low = hidden.astype(jnp.bfloat16)
    pre = jnp.dot(hidden_low, w_up, preferred_element_type=jnp.float32)
    act = jax.nn.gelu(pre, approximate=False).astype(jnp.bfloat16)
    ffn_out = tensor_sum(jnp.dot(act, w_down, preferred_element_type=jnp.float32))
    result, normed_second, inverse_second = layer_norm(hidden + ffn_out, gains[1], shifts[1])
    kept = (
        flat,
        heads,
        spread,
        mixed_flat,
        normed_first,
        inverse_first,
        hidden_low,
        pre,
        act,
        normed_second,
        inverse_second,
    )
    return (result.astype(jnp.bfloat16), kept)


def layer_backward(grad_result, kept, weights, query_groups, key_groups):
    w_qkv, w_out, w_up, w_down, gains, shifts = weights
    (
        flat,
        heads,
        spread,
        mixed_flat,
        normed_first,
        inverse_first,
        hidden_low,
        pre,
        act,
        normed_second,
        inverse_second,
    ) = kept
    length = flat.shape[0]
    local = w_qkv.shape[2]
    gain_second = jnp.sum(grad_result * normed_second, 0)
    shift_second = jnp.sum(grad_result, 0)
    grad_sum2 = norm_back(grad_result, normed_second, inverse_second, gains[1])
    grad_ffn = grad_sum2.astype(jnp.bfloat16)
    grad_down = jnp.einsum("nf,nd->fd", act, grad_ffn, preferred_element_type=jnp.float32)
    grad_act = jnp.einsum("nd,fd->nf", grad_ffn, w_down, preferred_element_type=jnp.float32)
    grad_pre = (grad_act * gelu_slope(pre)).astype(jnp.bfloat16)
    grad_up = jnp.einsum("nd,nf->df", hidden_low, grad_pre, preferred_element_type=jnp.float32)
    grad_hidden = grad_sum2 + tensor_sum(
        jnp.einsum("nf,df->nd", grad_pre, w_up, preferred_element_type=jnp.float32)
    )
    gain_first = jnp.sum(grad_hidden * normed_first, 0)
    shift_first = jnp.sum(grad_hidden, 0)
    grad_resid = norm_back(grad_hidden, normed_first, inverse_first, gains[0])
    grad_attn = grad_resid.astype(jnp.bfloat16)
    grad_out = jnp.einsum("nm,nd->md", mixed_flat, grad_attn, preferred_element_type=jnp.float32)
    grad_mixed = jnp.einsum(
        "nd,md->nm", grad_attn, w_out, preferred_element_type=jnp.float32
    ).astype(jnp.bfloat16)
    grad_mixed = grad_mixed.reshape(length, local // HEAD, HEAD)
    grad_heads = attend_back(
        heads[:, 0], heads[:, 1], heads[:, 2], query_groups, key_groups, spread, grad_mixed
    )
    grad_packed = grad_heads.reshape(length, 3, local)
    grad_qkv = jnp.einsum("nd,ncm->dcm", flat, grad_packed, preferred_element_type=jnp.float32)
    grad_input = grad_resid + tensor_sum(
        jnp.einsum("ncm,dcm->nd", grad_packed, w_qkv, preferred_element_type=jnp.float32)
    )
    grads = (
        grad_qkv.astype(jnp.bfloat16),
        grad_out.astype(jnp.bfloat16),
        grad_up.astype(jnp.bfloat16),
        grad_down.astype(jnp.bfloat16),
        jnp.stack([gain_first, gain_second]),
        jnp.stack([shift_first, shift_second]),
    )
    return (grads, grad_input.astype(jnp.bfloat16))


def shards(
    inputs, segments, partner, grad_output, w_qkv, w_out, w_up, w_down, norm_gain, norm_shift
):
    core = lax.axis_index("section")
    rows = inputs.shape[0] // lax.axis_size("section")

    def per_row(row):
        key_groups = lax.dynamic_index_in_dim(segments, row, 0, False)
        mapped = partner_of(key_groups, lax.dynamic_index_in_dim(partner, row, 0, False))
        flat = lax.dynamic_index_in_dim(inputs, row, 0, False)
        first, kept_first = layer_forward(flat, layers[0], key_groups, key_groups)
        second, kept_second = layer_forward(first, layers[1], mapped, key_groups)
        grad_top = lax.dynamic_index_in_dim(grad_output, row, 0, False).astype(jnp.float32)
        grads_second, grad_mid = layer_backward(
            grad_top, kept_second, layers[1], mapped, key_groups
        )
        grads_first, grad_low = layer_backward(
            grad_mid.astype(jnp.float32), kept_first, layers[0], key_groups, key_groups
        )
        return (first, second, grad_low, grad_mid, grads_first, grads_second)

    def gathered(shard, axis):
        own = lax.all_gather(shard[0], "dp", axis=axis, tiled=True)
        other = swapped(own, "section")
        return (jnp.where(core == 0, own, other), jnp.where(core == 0, other, own))

    pairs = [
        gathered(w_qkv, 0),
        gathered(w_out, 1),
        gathered(w_up, 0),
        gathered(w_down, 1),
        gathered(norm_gain, 1),
        gathered(norm_shift, 1),
    ]
    layers = [
        [pair[layer].astype(jnp.float32) if place > 3 else pair[layer] for place, pair in enumerate(pairs)]
        for layer in range(2)
    ]
    done = [per_row(core * rows + step) for step in range(rows)]

    def summed(first, second, axis):
        mine = jnp.where(core == 0, first, second)
        away = jnp.where(core == 0, second, first)
        both = mine.astype(jnp.float32) + swapped(away, "section").astype(jnp.float32)
        return lax.psum_scatter(both.astype(first.dtype), "dp", scatter_dimension=axis, tiled=True).astype(jnp.float32)

    def total(layer, place):
        value = done[0][4 + layer][place]
        for item in done[1:]:
            value = (value.astype(jnp.float32) + item[4 + layer][place].astype(jnp.float32)).astype(value.dtype)
        return value

    axes = (0, 1, 0, 1, 1, 1)
    sums = [summed(total(0, place), total(1, place), axis) for place, axis in enumerate(axes)]

    def regrouped(first, second):
        mine = jnp.where(core == 0, first, second)
        other = swapped(jnp.where(core == 0, second, first), "section")
        return jnp.where(
            core == 0, jnp.concatenate([mine, other]), jnp.concatenate([other, mine])
        )

    layer_outputs = regrouped(
        jnp.stack([item[0] for item in done]), jnp.stack([item[1] for item in done])
    )
    input_grads = regrouped(
        jnp.stack([item[2] for item in done]), jnp.stack([item[3] for item in done])
    )
    return (layer_outputs[None], input_grads[None]) + tuple(value[None] for value in sums)


def solution(mesh):
    placed = (
        P("dp", None, None),
        P("dp", None),
        P("dp", None),
        P("dp", None, None),
        P("section", "dp", None, "tensor"),
        P("section", "tensor", "dp"),
        P("section", "dp", "tensor"),
        P("section", "tensor", "dp"),
        P("section", None, "dp"),
        P("section", None, "dp"),
    )
    return jax.shard_map(
        shards,
        mesh=mesh,
        in_specs=placed,
        out_specs=(
            P("section", "dp", None, None),
            P("section", "dp", None, None),
            P("section", "dp", None, "tensor"),
            P("section", "tensor", "dp"),
            P("section", "dp", "tensor"),
            P("section", "tensor", "dp"),
            P("section", None, "dp"),
            P("section", None, "dp"),
        ),
        check_vma=False,
    )
```

```python
import functools

import jax
import jax.numpy as jnp
from jax import lax
from jax.experimental import pallas as pl
from jax.experimental.pallas import tpu as pltpu
from jax.sharding import PartitionSpec as P

HEAD = 64
WIDTH = 768


norm_eps = 1e-06
score_scale = 0.125
masked_value = -1000000000.0


def partner_of(segment_ids, partner):
    table = jnp.arange(partner.shape[-1], dtype=jnp.int32)
    hits = segment_ids[..., None] == table
    return jnp.sum(jnp.where(hits, partner[None, :], 0), -1)


def layer_norm(values, gain, shift):
    center = values - jnp.mean(values, -1, keepdims=True)
    inverse = lax.rsqrt(jnp.mean(center * center, -1, keepdims=True) + norm_eps)
    normed = center * inverse
    return (normed * gain + shift, normed, inverse)


def norm_back(grad, normed, inverse, gain):
    scaled = grad * gain
    inner = (
        scaled
        - jnp.mean(scaled, -1, keepdims=True)
        - normed * jnp.mean(scaled * normed, -1, keepdims=True)
    )
    return inner * inverse


def gelu_slope(values):
    lower = 0.5 * (1.0 + lax.erf(values * 0.7071067811865476))
    density = jnp.exp(-0.5 * values * values) * 0.3989422804014327
    return lower + values * density


def swapped(value, axis):
    size = lax.axis_size(axis)
    return lax.ppermute(value, axis, [(i, size - 1 - i) for i in range(size)])


def tensor_sum(partial_value):
    low = partial_value.astype(jnp.bfloat16)
    return low.astype(jnp.float32) + swapped(low, "tensor").astype(jnp.float32)


def masked_scores(query, key, query_groups, key_groups):
    scores = (
        jnp.einsum("qhd,khd->hqk", query, key, preferred_element_type=jnp.float32) * score_scale
    )
    allowed = query_groups[:, None] == key_groups[None, :]
    return jnp.where(allowed[None], scores, masked_value)


def attend(query, key, value, query_groups, key_groups):
    scores = masked_scores(query, key, query_groups, key_groups)
    top = jnp.max(scores, -1, keepdims=True)
    expo = jnp.exp(scores - top)
    total = jnp.sum(expo, -1, keepdims=True)
    probs = (expo / total).astype(jnp.bfloat16)
    mixed = jnp.einsum("hqk,khd->qhd", probs, value, preferred_element_type=jnp.float32)
    return (mixed.astype(jnp.bfloat16), (top + jnp.log(total))[..., 0])


def attend_back(query, key, value, query_groups, key_groups, spread, grad_mixed):
    scores = masked_scores(query, key, query_groups, key_groups)
    probs = jnp.exp(scores - spread[..., None])
    probs_low = probs.astype(jnp.bfloat16)
    grad_probs = jnp.einsum("qhd,khd->hqk", grad_mixed, value, preferred_element_type=jnp.float32)
    grad_value = jnp.einsum(
        "hqk,qhd->khd", probs_low, grad_mixed, preferred_element_type=jnp.float32
    )
    row_dot = jnp.sum(probs * grad_probs, -1, keepdims=True)
    grad_scores = (probs * (grad_probs - row_dot)).astype(jnp.bfloat16)
    grad_query = (
        jnp.einsum("hqk,khd->qhd", grad_scores, key, preferred_element_type=jnp.float32)
        * score_scale
    )
    grad_key = (
        jnp.einsum("hqk,qhd->khd", grad_scores, query, preferred_element_type=jnp.float32)
        * score_scale
    )
    return jnp.stack(
        [
            grad_query.astype(jnp.bfloat16),
            grad_key.astype(jnp.bfloat16),
            grad_value.astype(jnp.bfloat16),
        ],
        1,
    )


def layer_forward(flat, weights, query_groups, key_groups):
    w_qkv, w_out, w_up, w_down, gains, shifts = weights
    length = flat.shape[0]
    local = w_qkv.shape[2]
    packed = jnp.einsum("nd,dcm->ncm", flat, w_qkv, preferred_element_type=jnp.float32).astype(
        jnp.bfloat16
    )
    heads = packed.reshape(length, 3, local // HEAD, HEAD)
    mixed, spread = attend(heads[:, 0], heads[:, 1], heads[:, 2], query_groups, key_groups)
    mixed_flat = mixed.reshape(length, local)
    attn_out = tensor_sum(jnp.dot(mixed_flat, w_out, preferred_element_type=jnp.float32))
    hidden, normed_first, inverse_first = layer_norm(
        flat.astype(jnp.float32) + attn_out, gains[0], shifts[0]
    )
    hidden_low = hidden.astype(jnp.bfloat16)
    pre = jnp.dot(hidden_low, w_up, preferred_element_type=jnp.float32)
    act = jax.nn.gelu(pre, approximate=False).astype(jnp.bfloat16)
    ffn_out = tensor_sum(jnp.dot(act, w_down, preferred_element_type=jnp.float32))
    result, normed_second, inverse_second = layer_norm(hidden + ffn_out, gains[1], shifts[1])
    kept = (
        flat,
        heads,
        spread,
        mixed_flat,
        normed_first,
        inverse_first,
        hidden_low,
        pre,
        act,
        normed_second,
        inverse_second,
    )
    return (result.astype(jnp.bfloat16), kept)


def layer_backward(grad_result, kept, weights, query_groups, key_groups):
    w_qkv, w_out, w_up, w_down, gains, shifts = weights
    (
        flat,
        heads,
        spread,
        mixed_flat,
        normed_first,
        inverse_first,
        hidden_low,
        pre,
        act,
        normed_second,
        inverse_second,
    ) = kept
    length = flat.shape[0]
    local = w_qkv.shape[2]
    gain_second = jnp.sum(grad_result * normed_second, 0)
    shift_second = jnp.sum(grad_result, 0)
    grad_sum2 = norm_back(grad_result, normed_second, inverse_second, gains[1])
    grad_ffn = grad_sum2.astype(jnp.bfloat16)
    grad_down = jnp.einsum("nf,nd->fd", act, grad_ffn, preferred_element_type=jnp.float32)
    grad_act = jnp.einsum("nd,fd->nf", grad_ffn, w_down, preferred_element_type=jnp.float32)
    grad_pre = (grad_act * gelu_slope(pre)).astype(jnp.bfloat16)
    grad_up = jnp.einsum("nd,nf->df", hidden_low, grad_pre, preferred_element_type=jnp.float32)
    grad_hidden = grad_sum2 + tensor_sum(
        jnp.einsum("nf,df->nd", grad_pre, w_up, preferred_element_type=jnp.float32)
    )
    gain_first = jnp.sum(grad_hidden * normed_first, 0)
    shift_first = jnp.sum(grad_hidden, 0)
    grad_resid = norm_back(grad_hidden, normed_first, inverse_first, gains[0])
    grad_attn = grad_resid.astype(jnp.bfloat16)
    grad_out = jnp.einsum("nm,nd->md", mixed_flat, grad_attn, preferred_element_type=jnp.float32)
    grad_mixed = jnp.einsum(
        "nd,md->nm", grad_attn, w_out, preferred_element_type=jnp.float32
    ).astype(jnp.bfloat16)
    grad_mixed = grad_mixed.reshape(length, local // HEAD, HEAD)
    grad_heads = attend_back(
        heads[:, 0], heads[:, 1], heads[:, 2], query_groups, key_groups, spread, grad_mixed
    )
    grad_packed = grad_heads.reshape(length, 3, local)
    grad_qkv = jnp.einsum("nd,ncm->dcm", flat, grad_packed, preferred_element_type=jnp.float32)
    grad_input = grad_resid + tensor_sum(
        jnp.einsum("ncm,dcm->nd", grad_packed, w_qkv, preferred_element_type=jnp.float32)
    )
    grads = (
        grad_qkv.astype(jnp.bfloat16),
        grad_out.astype(jnp.bfloat16),
        grad_up.astype(jnp.bfloat16),
        grad_down.astype(jnp.bfloat16),
        jnp.stack([gain_first, gain_second]),
        jnp.stack([shift_first, shift_second]),
    )
    return (grads, grad_input.astype(jnp.bfloat16))


def shards(
    inputs, segments, partner, grad_output, w_qkv, w_out, w_up, w_down, norm_gain, norm_shift
):
    core = lax.axis_index("section")
    rows = inputs.shape[0] // lax.axis_size("section")

    def per_row(row):
        key_groups = lax.dynamic_index_in_dim(segments, row, 0, False)
        mapped = partner_of(key_groups, lax.dynamic_index_in_dim(partner, row, 0, False))
        flat = lax.dynamic_index_in_dim(inputs, row, 0, False)
        first, kept_first = layer_forward(flat, layers[0], key_groups, key_groups)
        second, kept_second = layer_forward(first, layers[1], mapped, key_groups)
        grad_top = lax.dynamic_index_in_dim(grad_output, row, 0, False).astype(jnp.float32)
        grads_second, grad_mid = layer_backward(
            grad_top, kept_second, layers[1], mapped, key_groups
        )
        grads_first, grad_low = layer_backward(
            grad_mid.astype(jnp.float32), kept_first, layers[0], key_groups, key_groups
        )
        return (first, second, grad_low, grad_mid, grads_first, grads_second)

    def gathered(shard, axis):
        own = lax.all_gather(shard[0], "dp", axis=axis, tiled=True)
        other = swapped(own, "section")
        return (jnp.where(core == 0, own, other), jnp.where(core == 0, other, own))

    pairs = [
        gathered(w_qkv, 0),
        gathered(w_out, 1),
        gathered(w_up, 0),
        gathered(w_down, 1),
        gathered(norm_gain, 1),
        gathered(norm_shift, 1),
    ]
    layers = [
        [pair[layer].astype(jnp.float32) if place > 3 else pair[layer] for place, pair in enumerate(pairs)]
        for layer in range(2)
    ]
    done = [per_row(core * rows + step) for step in range(rows)]

    def summed(first, second, axis):
        mine = jnp.where(core == 0, first, second)
        away = jnp.where(core == 0, second, first)
        both = mine.astype(jnp.float32) + swapped(away, "section").astype(jnp.float32)
        return lax.psum_scatter(both.astype(first.dtype), "dp", scatter_dimension=axis, tiled=True).astype(jnp.float32)

    def total(layer, place):
        value = done[0][4 + layer][place]
        for item in done[1:]:
            value = (value.astype(jnp.float32) + item[4 + layer][place].astype(jnp.float32)).astype(value.dtype)
        return value

    axes = (0, 1, 0, 1, 1, 1)
    sums = [summed(total(0, place), total(1, place), axis) for place, axis in enumerate(axes)]

    def regrouped(first, second):
        mine = jnp.where(core == 0, first, second)
        other = swapped(jnp.where(core == 0, second, first), "section")
        return jnp.where(
            core == 0, jnp.concatenate([mine, other]), jnp.concatenate([other, mine])
        )

    layer_outputs = regrouped(
        jnp.stack([item[0] for item in done]), jnp.stack([item[1] for item in done])
    )
    input_grads = regrouped(
        jnp.stack([item[2] for item in done]), jnp.stack([item[3] for item in done])
    )
    return (layer_outputs[None], input_grads[None]) + tuple(value[None] for value in sums)


MESH = pl.DeviceIdType.MESH
BF = jnp.bfloat16
F32 = jnp.float32
CHUNK = 256
SUB = 32
LANES = 128
NT = (((1,), (1,)), ((), ()))


def dot(left, right):
    return jnp.dot(left, right, preferred_element_type=F32)


def dot_nt(left, right):
    return lax.dot_general(left, right, NT, preferred_element_type=F32)


def flat_rows(value):
    return value.reshape(-1, value.shape[-1])


def kernel(
    sizes,
    x_ref,
    go_ref,
    keys_ref,
    groups_ref,
    sq,
    so,
    su,
    sd,
    sn,
    lo_ref,
    ig_ref,
    oq,
    oo,
    ou,
    od,
    on,
    wq,
    wo,
    wu,
    wd,
    wn,
    rq,
    ro,
    ru,
    rd,
    yq,
    yo,
    yu,
    yd,
    vq,
    vo,
    vu,
    vd,
    rn,
    yn,
    vn,
    ng,
    zin,
    packed,
    prob,
    mixed,
    norm1,
    inv1,
    hid,
    act,
    slope,
    norm2,
    inv2,
    gsum,
    gtok,
    gmix,
    turned,
    gtop,
    gin,
    work,
    norms,
    xs,
    xr,
    local_sem,
    out_send,
    out_recv,
    xs_sem,
    xr_sem,
    az_s,
    az_r,
    ay_s,
    ay_r,
    ac_s,
    ac_r,
    gc_s,
    gc_r,
    gy_s,
    gy_r,
    gz_s,
    gz_r,
):
    nz, ny, length, width, local, units, eps, scale = sizes
    chunks = length // CHUNK
    core = lax.axis_index("section")
    place = lax.axis_index("dp")
    side = lax.axis_index("tensor")
    z, y = place // ny, lax.rem(place, ny)
    other_y = 1 - y
    to_x = {"tensor": 1 - side}
    to_core = {"section": 1 - core}
    to_y = {"dp": z * ny + other_y}

    def turn(k):
        return lax.rem(z + k + nz, nz)

    def to_z(k):
        return {"dp": turn(k) * ny + y}

    shard = (sq, so, su, sd, sn)
    full = (wq, wo, wu, wd, wn)
    summed = (rq, ro, ru, rd)
    from_y = (yq, yo, yu, yd)
    from_z = (vq, vo, vu, vd)
    result = (oq, oo, ou, od)

    def remote(src, dst, send, recv, target):
        return pltpu.make_async_remote_copy(
            src_ref=src,
            dst_ref=dst,
            send_sem=send,
            recv_sem=recv,
            device_id=target,
            device_id_type=MESH,
        )

    def each(count, body):
        lax.fori_loop(0, count, lambda i, none: (body(i), none)[1], 0)


    def gather_z(l, m, k):
        return remote(
            shard[m], full[m].at[l, z, y], az_s.at[m, k - 1], az_r.at[m, k - 1], to_z(k)
        )

    def gather_y(l, m, k, src=None):
        ref = full[m].at[l, turn(-k), y]
        return remote(ref if src is None else src, ref, ay_s.at[m, k], ay_r.at[m, k], to_y)

    def gather_core(l, m, k, column, src=None):
        ref = full[m].at[l, turn(-k), column]
        slot = k if column is y else nz + k
        return remote(
            ref if src is None else src, ref, ac_s.at[m, slot], ac_r.at[m, slot], to_core
        )

    def gather_start(l, *mats):
        @pl.when(core == l)
        def _():
            for m in mats:
                for k in range(1, nz):
                    gather_z(l, m, k).start()
                gather_y(l, m, 0, shard[m]).start()
                gather_core(l, m, 0, y, shard[m]).start()
                full[m][l, z, y] = shard[m][...]

    def gather_pass(l, *mats):
        @pl.when(core == l)
        def _():
            for m in mats:

                def one(k):
                    gather_z(l, m, k).wait_recv()
                    gather_y(l, m, k).start()
                    gather_core(l, m, k, y).start()

                lax.fori_loop(1, nz, lambda k, none: (one(k), none)[1], 0)

    def gather_end(l, *mats):
        @pl.when(core == l)
        def _():
            for m in mats:

                def one(k):
                    gather_y(l, m, k).wait_recv()
                    gather_core(l, m, k, other_y).start()

                each(nz, one)

        @pl.when(core != l)
        def _():
            for m in mats:

                def one(k):
                    gather_core(l, m, k, y).wait_recv()
                    gather_core(l, m, k, other_y).wait_recv()

                each(nz, one)

    def gather_drain(l, m):
        @pl.when(core == l)
        def _():
            lax.fori_loop(1, nz, lambda k, none: (gather_z(l, m, k).wait_send(), none)[1], 0)

            def one(k):
                gather_y(l, m, k).wait_send()
                gather_core(l, m, k, y).wait_send()
                gather_core(l, m, k, other_y).wait_send()

            each(nz, one)


    def sum_core(l, m, part):
        column = (other_y, y)[part]
        return remote(
            full[m].at[l, :, column],
            summed[m].at[:, column],
            gc_s.at[m, part],
            gc_r.at[m, part],
            to_core,
        )

    def sum_y(l, m, k):
        return remote(
            full[m].at[l, k, other_y], from_y[m].at[k], gy_s.at[m, k], gy_r.at[m, k], to_y
        )

    def sum_z(l, m, k):
        return remote(
            full[m].at[l, turn(k), y],
            from_z[m].at[k - 1],
            gz_s.at[m, k - 1],
            gz_r.at[m, k - 1],
            to_z(k),
        )

    def sum_start(l, m):
        @pl.when(core != l)
        def _():
            sum_core(l, m, 0).start()
            sum_core(l, m, 1).start()

    def sum_first(l, m):
        @pl.when(core == l)
        def _():
            sum_core(l, m, 0).wait_recv()

            def one(k):
                both = full[m][l, k, other_y].astype(F32) + summed[m][k, other_y].astype(F32)
                full[m][l, k, other_y] = both.astype(BF)
                sum_y(l, m, k).start()

            each(nz, one)

    def sum_second(l, m):
        @pl.when(core == l)
        def _():
            sum_core(l, m, 1).wait_recv()

            def total(k):
                at = turn(k)
                sum_y(l, m, at).wait_recv()
                both = full[m][l, at, y].astype(F32) + summed[m][at, y].astype(F32)
                return both + from_y[m][at].astype(F32)

            def one(k, none):
                full[m][l, turn(k), y] = total(k).astype(BF)
                sum_z(l, m, k).start()
                return none

            lax.fori_loop(1, nz, one, 0)
            result[m][...] = total(0)

    def sum_last(l, m):
        @pl.when(core == l)
        def _():
            def one(k, none):
                sum_z(l, m, k).wait_recv()
                result[m][...] += from_z[m][k - 1].astype(F32)
                return none

            lax.fori_loop(1, nz, one, 0)

    def sum_drain(l, m):
        @pl.when(core != l)
        def _():
            sum_core(l, m, 0).wait_send()
            sum_core(l, m, 1).wait_send()

        @pl.when(core == l)
        def _():
            each(nz, lambda k: sum_y(l, m, k).wait_send())
            lax.fori_loop(1, nz, lambda k, none: (sum_z(l, m, k).wait_send(), none)[1], 0)


    def vec_core(l):
        return remote(ng.at[l], rn, gc_s.at[4, 0], gc_r.at[4, 0], to_core)

    def vec_y(l):
        return remote(ng.at[2], yn, gy_s.at[4, 0], gy_r.at[4, 0], to_y)

    def vec_z(l, k):
        return remote(
            ng.at[3], vn.at[k - 1], gz_s.at[4, k - 1], gz_r.at[4, k - 1], to_z(k)
        )

    def vec_start(l):
        @pl.when(core != l)
        def _():
            vec_core(l).start()

    def vec_first(l):
        @pl.when(core == l)
        def _():
            vec_core(l).wait_recv()
            ng[2] = ng[l] + rn[...]
            vec_y(l).start()

    def vec_second(l):
        @pl.when(core == l)
        def _():
            vec_y(l).wait_recv()
            ng[3] = ng[2] + yn[...]
            for k in range(1, nz):
                vec_z(l, k).start()

    def vec_last(l):
        @pl.when(core == l)
        def _():
            total = ng[3]
            for k in range(1, nz):
                vec_z(l, k).wait_recv()
                total = total + vn[k - 1]
            on[...] = total

    def vec_drain(l):
        @pl.when(core != l)
        def _():
            vec_core(l).wait_send()

        @pl.when(core == l)
        def _():
            vec_y(l).wait_send()
            for k in range(1, nz):
                vec_z(l, k).wait_send()


    def exchange(i, c):
        return remote(xs.at[c], xr.at[i % 2, c], xs_sem.at[c], xr_sem.at[i % 2, c], to_x)

    def send(i, c):
        exchange(i, c).start()

    def arrive(i, c):
        exchange(i, c).wait()

    def both(i, c, r):
        rows = pl.ds(r * SUB, SUB)
        return xs[c, rows].astype(F32) + xr[i % 2, c, rows].astype(F32)

    def chunk_rows(c):
        return pl.ds(pl.multiple_of(c * CHUNK, CHUNK), CHUNK)

    def sub_rows(c, r):
        return pl.ds(pl.multiple_of(c * CHUNK + r * SUB, SUB), SUB)

    def columns(j, span):
        return pl.ds(pl.multiple_of(j * span, LANES), span)


    def out_copy(l, which, src, dst):
        def away():
            return remote(src, dst.at[core], out_send.at[which], out_recv.at[which], to_core)

        def here():
            return pltpu.make_async_copy(src, dst.at[core], local_sem.at[which])

        return here, away

    def out_start(l, which, src, dst):
        here, away = out_copy(l, which, src, dst)

        @pl.when(core == l)
        def _():
            here().start()

        @pl.when(core != l)
        def _():
            away().start()

    def out_wait(l, which, src, dst):
        here, away = out_copy(l, which, src, dst)

        @pl.when(core == l)
        def _():
            here().wait()
            remote(
                src, dst.at[1 - core], out_send.at[which], out_recv.at[which], to_core
            ).wait_recv()

        @pl.when(core != l)
        def _():
            away().wait_send()


    def project(l, c):
        rows = chunk_rows(c)

        def one(j):
            cols = columns(j, local)
            packed[l, rows, cols] = dot(
                zin[l, rows], flat_rows(wq[l, :, :, :, cols])
            ).astype(BF)

        each(3, one)

    low_lane = lax.broadcasted_iota(jnp.int32, (1, LANES), 1) < LANES // 2

    def half(value, h):
        keep = low_lane if h == 0 else jnp.logical_not(low_lane)
        return jnp.where(keep, value, jnp.zeros_like(value))

    def attend(l, c):
        rows = chunk_rows(c)
        lanes = columns(c, CHUNK)
        allowed = keys_ref[...] == groups_ref[pl.ds(l, 1), lanes]

        def one(j):
            query = packed[l, rows, columns(j, LANES)]
            key = packed[l, :, pl.ds(pl.multiple_of(local + j * LANES, LANES), LANES)]
            value = packed[l, :, pl.ds(pl.multiple_of(2 * local + j * LANES, LANES), LANES)]
            value_t = value.astype(F32).T.astype(BF)
            parts = []
            for h in range(2):
                scores = dot_nt(key, half(query, h)) * scale
                scores = jnp.where(allowed, scores, -1e9)
                top = jnp.max(scores, 0, keepdims=True)
                expo = jnp.exp(scores - top)
                low = (expo * (1.0 / jnp.sum(expo, 0, keepdims=True))).astype(BF)
                prob[l, 2 * j + h, :, lanes] = low
                parts.append(dot(value_t[h * (LANES // 2) : (h + 1) * (LANES // 2)], low))
            mixed[l, rows, columns(j, LANES)] = jnp.concatenate(parts, 0).T.astype(BF)

        each(local // LANES, one)

    def send_product(i, c, left, right):
        def one(j):
            span = width // 2
            xs[c, :, columns(j, span)] = dot_nt(left(), right(j)).astype(BF)

        each(2, one)
        send(i, c)

    def half_rows(ref, l, j):
        return flat_rows(ref[l, pl.ds(j * (nz // 2), nz // 2)])

    def attend_out(i, l, c):
        attend(l, c)
        send_product(
            i, c, lambda: mixed[l, chunk_rows(c)], lambda j: half_rows(wo, l, j)
        )

    def gather_norms(l):
        norms[l] = jnp.sum(flat_rows(wn[l]).reshape(nz * ny, 8, width), 0)

    def norm_of(l, which):
        return norms[l, which : which + 1], norms[l, 2 + which : 3 + which]

    def normalize(value):
        center = value - jnp.mean(value, -1, keepdims=True)
        inverse = lax.rsqrt(jnp.mean(center * center, -1, keepdims=True) + eps)
        return center * inverse, inverse

    def expand(i, l, c):
        rows = chunk_rows(c)
        arrive(i, c)
        gain, shift = norm_of(l, 0)

        def one(r):
            sub = sub_rows(c, r)
            normed, inverse = normalize(zin[l, sub].astype(F32) + both(i, c, r))
            norm1[l, sub] = normed
            inv1[l, sub] = inverse
            hid[l, sub] = (normed * gain + shift).astype(BF)

        each(CHUNK // SUB, one)

        def tile(j):
            span = units // 3
            cols = columns(j, span)
            work[...] = dot(hid[l, rows], flat_rows(wu[l, :, :, :, cols]))

            def piece(r):
                sub = sub_rows(c, r)
                pre = work[pl.ds(pl.multiple_of(r * SUB, SUB), SUB)]
                lower = 0.5 + 0.5 * lax.erf(pre * 0.7071067811865476)
                density = jnp.exp(-0.5 * pre * pre) * 0.3989422804014327
                act[l, sub, cols] = (pre * lower).astype(BF)
                slope[l, sub, cols] = (lower + pre * density).astype(BF)

            each(CHUNK // SUB, piece)

        each(3, tile)
        send_product(i + 1, c, lambda: act[l, rows], lambda j: half_rows(wd, l, j))

    def second_norm(i, l, c, r):
        sub = sub_rows(c, r)
        gain, shift = norm_of(l, 0)
        hidden = norm1[l, sub] * gain + shift
        return normalize(hidden + both(i, c, r))

    def norm_back(grad, normed, inverse, gain):
        scaled = grad * gain
        inner = (
            scaled
            - jnp.mean(scaled, -1, keepdims=True)
            - normed * jnp.mean(scaled * normed, -1, keepdims=True)
        )
        return inner * inverse

    def count(l, which, grad, normed):
        ng[l, which : which + 1] += jnp.sum(grad * normed, 0, keepdims=True)
        ng[l, 2 + which : 3 + which] += jnp.sum(grad, 0, keepdims=True)

    def top_back(l, c, r, grad, normed, inverse):
        sub = sub_rows(c, r)
        count(l, 1, grad, normed)
        back = norm_back(grad, normed, inverse, norm_of(l, 1)[0])
        gsum[sub] = back
        gtok[sub] = back.astype(BF)

    def expand_back(i, l, c):
        rows = chunk_rows(c)

        def tile(j):
            span = units // 3
            cols = columns(j, span)
            grad = dot(gtok[rows], flat_rows(wd[l, :, :, :, cols]))
            slope[l, rows, cols] = (grad * slope[l, rows, cols].astype(F32)).astype(BF)

        each(3, tile)
        send_product(i, c, lambda: slope[l, rows], lambda j: half_rows(wu, l, j))

    def weight_grad(l, m, source, right, span):
        gather_drain(l, m)
        step = length // 4

        def flip(j):
            rows = pl.ds(pl.multiple_of(j * step, step), step)
            turned[:, columns(j, step)] = source[rows].astype(F32).T.astype(BF)

        each(4, flip)

        def tile(j):
            cols = columns(j, span)
            for part in range(2):
                rows = slice(part * width // 2, (part + 1) * width // 2)
                grad = dot(turned[rows], right(cols)).astype(BF)
                full[m][l, part * nz // 2 : (part + 1) * nz // 2, :, :, cols] = grad.reshape(
                    nz // 2, ny, width // (nz * ny), span
                )

        each(full[m].shape[-1] // span, tile)
        sum_start(l, m)

    def attend_back(l):
        def one(j):
            q_cols = columns(j, LANES)
            k_cols = pl.ds(pl.multiple_of(local + j * LANES, LANES), LANES)
            v_cols = pl.ds(pl.multiple_of(2 * local + j * LANES, LANES), LANES)
            query, key, value = (packed[l, :, cols] for cols in (q_cols, k_cols, v_cols))
            grad = gmix[:, q_cols]
            key_t = key.astype(F32).T.astype(BF)
            queries, keys, values = [], [], []
            for h in range(2):
                low = prob[l, 2 * j + h]
                wide = low.astype(F32)
                product = wide * dot_nt(value, half(grad, h))
                total = jnp.sum(product, 0, keepdims=True)
                back = (product - wide * total).astype(BF)
                values.append(dot(low, grad))
                keys.append(dot(back, query))
                queries.append(dot(key_t[h * (LANES // 2) : (h + 1) * (LANES // 2)], back))
            packed[l, :, q_cols] = (jnp.concatenate(queries, 0).T * scale).astype(BF)
            packed[l, :, k_cols] = (jnp.where(low_lane, keys[0], keys[1]) * scale).astype(BF)
            packed[l, :, v_cols] = jnp.where(low_lane, values[0], values[1]).astype(BF)

        each(local // LANES, one)

    def middle_back(i, l, c):
        rows = chunk_rows(c)
        arrive(i, c)

        def one(r):
            sub = sub_rows(c, r)
            grad = gsum[sub] + both(i, c, r)
            normed = norm1[l, sub]
            count(l, 0, grad, normed)
            back = norm_back(grad, normed, inv1[l, sub], norm_of(l, 0)[0])
            gsum[sub] = back
            gtok[sub] = back.astype(BF)

        each(CHUNK // SUB, one)
        gmix[rows] = dot(gtok[rows], flat_rows(wo[l])).astype(BF)

    def project_back(i, l, c):
        send_product(
            i, c, lambda: packed[l, chunk_rows(c)], lambda j: half_rows(wq, l, j)
        )


    barrier = pltpu.get_barrier_semaphore()
    peers = [to_x, to_core, to_y] + [to_z(k) for k in range(1, nz)]
    for peer in peers:
        pl.semaphore_signal(barrier, inc=1, device_id=peer, device_id_type=MESH)
    first_rows = pltpu.make_async_copy(x_ref.at[core], zin.at[0], local_sem.at[4])
    top_rows = pltpu.make_async_copy(go_ref.at[core], gtop, local_sem.at[5])
    first_rows.start()
    top_rows.start()
    ng[...] = jnp.zeros_like(ng)
    pl.semaphore_wait(barrier, len(peers))

    Q, O, U, D, N = range(5)
    gather_start(0, Q, N)
    gather_start(0, O)
    gather_pass(0, Q, N)
    gather_start(0, U)
    gather_end(0, Q, N)
    first_rows.wait()
    gather_norms(0)
    each(chunks, lambda c: project(0, c))
    gather_pass(0, O)
    gather_end(0, O)
    each(chunks, lambda c: attend_out(0, 0, c))
    gather_pass(0, U)
    gather_start(0, D)
    gather_end(0, U)
    gather_start(1, Q, N)
    gather_pass(0, D)
    gather_end(0, D)
    gather_start(1, O)
    gather_start(1, U)
    each(chunks, lambda c: expand(0, 0, c))

    gather_pass(1, Q, N)
    gather_end(1, Q, N)
    gather_norms(1)

    def into_second(c):
        arrive(1, c)
        gain, shift = norm_of(0, 1)

        def one(r):
            sub = sub_rows(c, r)
            normed, inverse = second_norm(1, 0, c, r)
            norm2[sub] = normed
            inv2[sub] = inverse
            zin[1, sub] = (normed * gain + shift).astype(BF)

        each(CHUNK // SUB, one)
        project(1, c)

    each(chunks, into_second)
    out_start(0, 0, zin.at[1], lo_ref)
    gather_pass(1, O)
    gather_start(1, D)
    gather_end(1, O)
    each(chunks, lambda c: attend_out(2, 1, c))
    gather_pass(1, U)
    gather_end(1, U)
    gather_pass(1, D)
    gather_end(1, D)
    each(chunks, lambda c: expand(2, 1, c))
    top_rows.wait()

    def over_top(c):
        arrive(3, c)
        gain, shift = norm_of(1, 1)

        def one(r):
            sub = sub_rows(c, r)
            normed, inverse = second_norm(3, 1, c, r)
            top_back(1, c, r, gtop[sub].astype(F32), normed, inverse)
            gtop[sub] = (normed * gain + shift).astype(BF)

        each(CHUNK // SUB, one)
        expand_back(4, 1, c)

    each(chunks, over_top)
    out_start(1, 1, gtop, lo_ref)
    third = units // 3
    weight_grad(1, D, gtok, lambda cols: act[1, :, cols], third)
    weight_grad(1, U, hid.at[1], lambda cols: slope[1, :, cols], third)
    each(chunks, lambda c: middle_back(4, 1, c))
    weight_grad(1, O, gtok, lambda cols: mixed[1, :, cols], local)
    attend_back(1)
    each(chunks, lambda c: project_back(5, 1, c))
    weight_grad(1, Q, zin.at[1], lambda cols: packed[1, :, cols], local)
    vec_start(1)
    sum_first(1, D)
    sum_first(1, U)

    def under(c):
        arrive(5, c)

        def one(r):
            sub = sub_rows(c, r)
            low = (gsum[sub] + both(5, c, r)).astype(BF)
            gin[sub] = low
            top_back(0, c, r, low.astype(F32), norm2[sub], inv2[sub])

        each(CHUNK // SUB, one)
        expand_back(6, 0, c)

    each(chunks, under)
    out_start(1, 3, gin, ig_ref)
    weight_grad(0, D, gtok, lambda cols: act[0, :, cols], third)
    weight_grad(0, U, hid.at[0], lambda cols: slope[0, :, cols], third)
    sum_second(1, D)
    sum_second(1, U)
    sum_first(1, O)
    sum_first(1, Q)
    vec_first(1)
    each(chunks, lambda c: middle_back(6, 0, c))
    weight_grad(0, O, gtok, lambda cols: mixed[0, :, cols], local)
    sum_first(0, D)
    sum_first(0, U)
    sum_first(0, O)
    attend_back(0)
    each(chunks, lambda c: project_back(7, 0, c))
    weight_grad(0, Q, zin.at[0], lambda cols: packed[0, :, cols], local)
    vec_start(0)
    sum_second(1, O)
    sum_second(1, Q)
    vec_second(1)
    sum_last(1, D)
    sum_last(1, U)
    sum_second(0, D)
    sum_first(0, Q)
    vec_first(0)
    sum_second(0, U)
    sum_second(0, O)

    def bottom(c):
        arrive(7, c)

        def one(r):
            sub = sub_rows(c, r)
            gtop[sub] = (gsum[sub] + both(7, c, r)).astype(BF)

        each(CHUNK // SUB, one)

    out_wait(1, 1, gtop, lo_ref)
    each(chunks, bottom)
    out_start(0, 2, gtop, ig_ref)
    sum_second(0, Q)
    vec_second(0)
    for l in (1, 0):
        for m in (D, U, O, Q):
            if l == 0 or m in (O, Q):
                sum_last(l, m)
        vec_last(l)
    for l in range(2):
        for m in (Q, O, U, D):
            sum_drain(l, m)
        vec_drain(l)
        gather_drain(l, N)
    out_wait(0, 0, zin.at[1], lo_ref)
    out_wait(0, 2, gtop, ig_ref)
    out_wait(1, 3, gin, ig_ref)


def fused(sizes, x, grad, keys, groups, shards_in):
    nz, ny, length, width, local, units, eps, scale = sizes
    block = width // (nz * ny)
    chunks = length // CHUNK
    spans = (3 * local, local, units, units)
    dma = pltpu.SemaphoreType.DMA
    vmem = pltpu.VMEM
    scratch = [vmem((2, nz, ny, block, span), BF) for span in spans]
    scratch += [vmem((2, nz, ny, 8, width), F32)]
    scratch += [vmem((nz, ny, block, span), BF) for span in spans]
    scratch += [vmem((nz, block, span), BF) for span in spans]
    scratch += [vmem((nz - 1, block, span), BF) for span in spans]
    scratch += [
        vmem((8, width), F32),
        vmem((8, width), F32),
        vmem((nz - 1, 8, width), F32),
        vmem((4, 8, width), F32),
        vmem((2, length, width), BF),
        vmem((2, length, 3 * local), BF),
        vmem((2, local // HEAD, length, length), BF),
        vmem((2, length, local), BF),
        vmem((2, length, width), F32),
        vmem((2, length, 1), F32),
        vmem((2, length, width), BF),
        vmem((2, length, units), BF),
        vmem((2, length, units), BF),
        vmem((length, width), F32),
        vmem((length, 1), F32),
        vmem((length, width), F32),
        vmem((length, width), BF),
        vmem((length, local), BF),
        vmem((width, length), BF),
        vmem((length, width), BF),
        vmem((length, width), BF),
        vmem((CHUNK, units // 3), F32),
        vmem((2, 8, width), F32),
        vmem((chunks, CHUNK, width), BF),
        vmem((2, chunks, CHUNK, width), BF),
        dma((6,)),
        dma((4,)),
        dma((4,)),
        dma((chunks,)),
        dma((2, chunks)),
        dma((5, nz - 1)),
        dma((5, nz - 1)),
        dma((5, nz)),
        dma((5, nz)),
        dma((5, 2 * nz)),
        dma((5, 2 * nz)),
        dma((5, 2)),
        dma((5, 2)),
        dma((5, nz)),
        dma((5, nz)),
        dma((5, nz - 1)),
        dma((5, nz - 1)),
    ]
    anywhere = pl.BlockSpec(memory_space=pl.ANY)
    inside = pl.BlockSpec(memory_space=pltpu.VMEM)
    return pl.pallas_call(
        functools.partial(kernel, sizes),
        out_shape=[jax.ShapeDtypeStruct((2, length, width), BF)] * 2
        + [jax.ShapeDtypeStruct((block, span), F32) for span in spans]
        + [jax.ShapeDtypeStruct((8, width), F32)],
        in_specs=[anywhere] * 2 + [inside] * 7,
        out_specs=[anywhere] * 2 + [inside] * 5,
        scratch_shapes=scratch,
        compiler_params=pltpu.CompilerParams(
            collective_id=0, has_side_effects=True, vmem_limit_bytes=63 << 20
        ),
    )(x, grad, keys, groups, *shards_in)


def kernel_shards(
    inputs, segments, partner, grad_output, w_qkv, w_out, w_up, w_down, norm_gain, norm_shift
):
    core = lax.axis_index("section")
    place = lax.axis_index("dp")
    parts = lax.axis_size("dp")
    length, width = inputs.shape[1:]
    local, units = w_out.shape[1], w_up.shape[2]
    block = width // parts
    sizes = (parts // 2, 2, length, width, local, units, norm_eps, score_scale)
    own = lax.dynamic_index_in_dim(segments, core, 0, False)
    mapped = partner_of(own, lax.dynamic_index_in_dim(partner, core, 0, False))
    keys = jnp.broadcast_to(own[:, None], (length, CHUNK))
    groups = jnp.stack([own, mapped])
    vectors = jnp.concatenate([norm_gain[0], norm_shift[0]]).astype(F32)
    spread = lax.dynamic_update_slice(
        jnp.zeros((8, width), F32), vectors, (0, place * block)
    )
    shards_in = (
        w_qkv[0].reshape(block, 3 * local),
        w_out[0].T,
        w_up[0],
        w_down[0].T,
        spread,
    )
    outs = fused(sizes, inputs, grad_output, keys, groups, shards_in)
    layer_outputs, input_grads, g_qkv, g_out, g_up, g_down, g_norm = outs
    own_norm = lax.dynamic_slice(g_norm, (0, place * block), (8, block))
    return (
        layer_outputs[None],
        input_grads[None],
        g_qkv.reshape(1, block, 3, local),
        g_out.T[None],
        g_up[None],
        g_down.T[None],
        own_norm[None, 0:2],
        own_norm[None, 2:4],
    )


def solution(mesh):
    placed = (
        P("dp", None, None),
        P("dp", None),
        P("dp", None),
        P("dp", None, None),
        P("section", "dp", None, "tensor"),
        P("section", "tensor", "dp"),
        P("section", "dp", "tensor"),
        P("section", "tensor", "dp"),
        P("section", None, "dp"),
        P("section", None, "dp"),
    )
    block = WIDTH // mesh.shape["dp"]
    whole_tiles = block * mesh.shape["dp"] == WIDTH and block % 16 == 0
    return jax.shard_map(
        kernel_shards if whole_tiles else shards,
        mesh=mesh,
        in_specs=placed,
        out_specs=(
            P("section", "dp", None, None),
            P("section", "dp", None, None),
            P("section", "dp", None, "tensor"),
            P("section", "tensor", "dp"),
            P("section", "dp", "tensor"),
            P("section", "tensor", "dp"),
            P("section", None, "dp"),
            P("section", None, "dp"),
        ),
        check_vma=False,
    )
```

```python
import functools

import jax
import jax.numpy as jnp
from jax import lax
from jax.experimental import pallas as pl
from jax.experimental.pallas import tpu as pltpu
from jax.sharding import PartitionSpec as P

HEAD = 64
WIDTH = 768


norm_eps = 1e-06
score_scale = 0.125
masked_value = -1000000000.0


def partner_of(segment_ids, partner):
    table = jnp.arange(partner.shape[-1], dtype=jnp.int32)
    hits = segment_ids[..., None] == table
    return jnp.sum(jnp.where(hits, partner[None, :], 0), -1)


def layer_norm(values, gain, shift):
    center = values - jnp.mean(values, -1, keepdims=True)
    inverse = lax.rsqrt(jnp.mean(center * center, -1, keepdims=True) + norm_eps)
    normed = center * inverse
    return (normed * gain + shift, normed, inverse)


def norm_back(grad, normed, inverse, gain):
    scaled = grad * gain
    inner = (
        scaled
        - jnp.mean(scaled, -1, keepdims=True)
        - normed * jnp.mean(scaled * normed, -1, keepdims=True)
    )
    return inner * inverse


def gelu_slope(values):
    lower = 0.5 * (1.0 + lax.erf(values * 0.7071067811865476))
    density = jnp.exp(-0.5 * values * values) * 0.3989422804014327
    return lower + values * density


def swapped(value, axis):
    size = lax.axis_size(axis)
    return lax.ppermute(value, axis, [(i, size - 1 - i) for i in range(size)])


def tensor_sum(partial_value):
    low = partial_value.astype(jnp.bfloat16)
    return low.astype(jnp.float32) + swapped(low, "tensor").astype(jnp.float32)


def masked_scores(query, key, query_groups, key_groups):
    scores = (
        jnp.einsum("qhd,khd->hqk", query, key, preferred_element_type=jnp.float32) * score_scale
    )
    allowed = query_groups[:, None] == key_groups[None, :]
    return jnp.where(allowed[None], scores, masked_value)


def attend(query, key, value, query_groups, key_groups):
    scores = masked_scores(query, key, query_groups, key_groups)
    top = jnp.max(scores, -1, keepdims=True)
    expo = jnp.exp(scores - top)
    total = jnp.sum(expo, -1, keepdims=True)
    probs = (expo / total).astype(jnp.bfloat16)
    mixed = jnp.einsum("hqk,khd->qhd", probs, value, preferred_element_type=jnp.float32)
    return (mixed.astype(jnp.bfloat16), (top + jnp.log(total))[..., 0])


def attend_back(query, key, value, query_groups, key_groups, spread, grad_mixed):
    scores = masked_scores(query, key, query_groups, key_groups)
    probs = jnp.exp(scores - spread[..., None])
    probs_low = probs.astype(jnp.bfloat16)
    grad_probs = jnp.einsum("qhd,khd->hqk", grad_mixed, value, preferred_element_type=jnp.float32)
    grad_value = jnp.einsum(
        "hqk,qhd->khd", probs_low, grad_mixed, preferred_element_type=jnp.float32
    )
    row_dot = jnp.sum(probs * grad_probs, -1, keepdims=True)
    grad_scores = (probs * (grad_probs - row_dot)).astype(jnp.bfloat16)
    grad_query = (
        jnp.einsum("hqk,khd->qhd", grad_scores, key, preferred_element_type=jnp.float32)
        * score_scale
    )
    grad_key = (
        jnp.einsum("hqk,qhd->khd", grad_scores, query, preferred_element_type=jnp.float32)
        * score_scale
    )
    return jnp.stack(
        [
            grad_query.astype(jnp.bfloat16),
            grad_key.astype(jnp.bfloat16),
            grad_value.astype(jnp.bfloat16),
        ],
        1,
    )


def layer_forward(flat, weights, query_groups, key_groups):
    w_qkv, w_out, w_up, w_down, gains, shifts = weights
    length = flat.shape[0]
    local = w_qkv.shape[2]
    packed = jnp.einsum("nd,dcm->ncm", flat, w_qkv, preferred_element_type=jnp.float32).astype(
        jnp.bfloat16
    )
    heads = packed.reshape(length, 3, local // HEAD, HEAD)
    mixed, spread = attend(heads[:, 0], heads[:, 1], heads[:, 2], query_groups, key_groups)
    mixed_flat = mixed.reshape(length, local)
    attn_out = tensor_sum(jnp.dot(mixed_flat, w_out, preferred_element_type=jnp.float32))
    hidden, normed_first, inverse_first = layer_norm(
        flat.astype(jnp.float32) + attn_out, gains[0], shifts[0]
    )
    hidden_low = hidden.astype(jnp.bfloat16)
    pre = jnp.dot(hidden_low, w_up, preferred_element_type=jnp.float32)
    act = jax.nn.gelu(pre, approximate=False).astype(jnp.bfloat16)
    ffn_out = tensor_sum(jnp.dot(act, w_down, preferred_element_type=jnp.float32))
    result, normed_second, inverse_second = layer_norm(hidden + ffn_out, gains[1], shifts[1])
    kept = (
        flat,
        heads,
        spread,
        mixed_flat,
        normed_first,
        inverse_first,
        hidden_low,
        pre,
        act,
        normed_second,
        inverse_second,
    )
    return (result.astype(jnp.bfloat16), kept)


def layer_backward(grad_result, kept, weights, query_groups, key_groups):
    w_qkv, w_out, w_up, w_down, gains, shifts = weights
    (
        flat,
        heads,
        spread,
        mixed_flat,
        normed_first,
        inverse_first,
        hidden_low,
        pre,
        act,
        normed_second,
        inverse_second,
    ) = kept
    length = flat.shape[0]
    local = w_qkv.shape[2]
    gain_second = jnp.sum(grad_result * normed_second, 0)
    shift_second = jnp.sum(grad_result, 0)
    grad_sum2 = norm_back(grad_result, normed_second, inverse_second, gains[1])
    grad_ffn = grad_sum2.astype(jnp.bfloat16)
    grad_down = jnp.einsum("nf,nd->fd", act, grad_ffn, preferred_element_type=jnp.float32)
    grad_act = jnp.einsum("nd,fd->nf", grad_ffn, w_down, preferred_element_type=jnp.float32)
    grad_pre = (grad_act * gelu_slope(pre)).astype(jnp.bfloat16)
    grad_up = jnp.einsum("nd,nf->df", hidden_low, grad_pre, preferred_element_type=jnp.float32)
    grad_hidden = grad_sum2 + tensor_sum(
        jnp.einsum("nf,df->nd", grad_pre, w_up, preferred_element_type=jnp.float32)
    )
    gain_first = jnp.sum(grad_hidden * normed_first, 0)
    shift_first = jnp.sum(grad_hidden, 0)
    grad_resid = norm_back(grad_hidden, normed_first, inverse_first, gains[0])
    grad_attn = grad_resid.astype(jnp.bfloat16)
    grad_out = jnp.einsum("nm,nd->md", mixed_flat, grad_attn, preferred_element_type=jnp.float32)
    grad_mixed = jnp.einsum(
        "nd,md->nm", grad_attn, w_out, preferred_element_type=jnp.float32
    ).astype(jnp.bfloat16)
    grad_mixed = grad_mixed.reshape(length, local // HEAD, HEAD)
    grad_heads = attend_back(
        heads[:, 0], heads[:, 1], heads[:, 2], query_groups, key_groups, spread, grad_mixed
    )
    grad_packed = grad_heads.reshape(length, 3, local)
    grad_qkv = jnp.einsum("nd,ncm->dcm", flat, grad_packed, preferred_element_type=jnp.float32)
    grad_input = grad_resid + tensor_sum(
        jnp.einsum("ncm,dcm->nd", grad_packed, w_qkv, preferred_element_type=jnp.float32)
    )
    grads = (
        grad_qkv.astype(jnp.bfloat16),
        grad_out.astype(jnp.bfloat16),
        grad_up.astype(jnp.bfloat16),
        grad_down.astype(jnp.bfloat16),
        jnp.stack([gain_first, gain_second]),
        jnp.stack([shift_first, shift_second]),
    )
    return (grads, grad_input.astype(jnp.bfloat16))


def shards(
    inputs, segments, partner, grad_output, w_qkv, w_out, w_up, w_down, norm_gain, norm_shift
):
    core = lax.axis_index("section")
    rows = inputs.shape[0] // lax.axis_size("section")

    def per_row(row):
        key_groups = lax.dynamic_index_in_dim(segments, row, 0, False)
        mapped = partner_of(key_groups, lax.dynamic_index_in_dim(partner, row, 0, False))
        flat = lax.dynamic_index_in_dim(inputs, row, 0, False)
        first, kept_first = layer_forward(flat, layers[0], key_groups, key_groups)
        second, kept_second = layer_forward(first, layers[1], mapped, key_groups)
        grad_top = lax.dynamic_index_in_dim(grad_output, row, 0, False).astype(jnp.float32)
        grads_second, grad_mid = layer_backward(
            grad_top, kept_second, layers[1], mapped, key_groups
        )
        grads_first, grad_low = layer_backward(
            grad_mid.astype(jnp.float32), kept_first, layers[0], key_groups, key_groups
        )
        return (first, second, grad_low, grad_mid, grads_first, grads_second)

    def gathered(shard, axis):
        own = lax.all_gather(shard[0], "dp", axis=axis, tiled=True)
        other = swapped(own, "section")
        return (jnp.where(core == 0, own, other), jnp.where(core == 0, other, own))

    pairs = [
        gathered(w_qkv, 0),
        gathered(w_out, 1),
        gathered(w_up, 0),
        gathered(w_down, 1),
        gathered(norm_gain, 1),
        gathered(norm_shift, 1),
    ]
    layers = [
        [pair[layer].astype(jnp.float32) if place > 3 else pair[layer] for place, pair in enumerate(pairs)]
        for layer in range(2)
    ]
    done = [per_row(core * rows + step) for step in range(rows)]

    def summed(first, second, axis):
        mine = jnp.where(core == 0, first, second)
        away = jnp.where(core == 0, second, first)
        both = mine.astype(jnp.float32) + swapped(away, "section").astype(jnp.float32)
        return lax.psum_scatter(both.astype(first.dtype), "dp", scatter_dimension=axis, tiled=True).astype(jnp.float32)

    def total(layer, place):
        value = done[0][4 + layer][place]
        for item in done[1:]:
            value = (value.astype(jnp.float32) + item[4 + layer][place].astype(jnp.float32)).astype(value.dtype)
        return value

    axes = (0, 1, 0, 1, 1, 1)
    sums = [summed(total(0, place), total(1, place), axis) for place, axis in enumerate(axes)]

    def regrouped(first, second):
        mine = jnp.where(core == 0, first, second)
        other = swapped(jnp.where(core == 0, second, first), "section")
        return jnp.where(
            core == 0, jnp.concatenate([mine, other]), jnp.concatenate([other, mine])
        )

    layer_outputs = regrouped(
        jnp.stack([item[0] for item in done]), jnp.stack([item[1] for item in done])
    )
    input_grads = regrouped(
        jnp.stack([item[2] for item in done]), jnp.stack([item[3] for item in done])
    )
    return (layer_outputs[None], input_grads[None]) + tuple(value[None] for value in sums)


MESH = pl.DeviceIdType.MESH
BF = jnp.bfloat16
F32 = jnp.float32
CHUNK = 256
SUB = 32
LANES = 128
QK, V, O, UA, UB, DA, DB, N = range(8)
PIECES = N
NT = (((1,), (1,)), ((), ()))


def dot(left, right):
    return jnp.dot(left, right, preferred_element_type=F32)


def dot_nt(left, right):
    return lax.dot_general(left, right, NT, preferred_element_type=F32)


def flat_rows(value):
    return value.reshape(-1, value.shape[-1])


def kernel(
    sizes,
    x_ref,
    go_ref,
    keys_ref,
    groups_ref,
    sq,
    so,
    su,
    sd,
    sn,
    lo_ref,
    ig_ref,
    oq,
    oo,
    ou,
    od,
    on,
    *refs,
):
    nz, ny, length, width, local, units, eps, scale = sizes
    full, refs = refs[: PIECES + 1], refs[PIECES + 1 :]
    summed, refs = refs[:PIECES], refs[PIECES:]
    from_y, refs = refs[:PIECES], refs[PIECES:]
    from_z, refs = refs[:PIECES], refs[PIECES:]
    (
        rn,
        yn,
        vn,
        ng,
        zin,
        packed,
        prob,
        mixed,
        norm1,
        inv1,
        hid,
        act,
        slope,
        norm2,
        inv2,
        gsum,
        gtok,
        gmix,
        turned,
        gtop,
        gin,
        work,
        norms,
        xs,
        xr,
        local_sem,
        out_send,
        out_recv,
        xs_sem,
        xr_sem,
        az_s,
        az_r,
        ay_s,
        ay_r,
        ac_s,
        ac_r,
        gc_s,
        gc_r,
        gy_s,
        gy_r,
        gz_s,
        gz_r,
    ) = refs
    chunks = length // CHUNK
    core = lax.axis_index("section")
    place = lax.axis_index("dp")
    side = lax.axis_index("tensor")
    z, y = place // ny, lax.rem(place, ny)
    other_y = 1 - y
    to_x = {"tensor": 1 - side}
    to_core = {"section": 1 - core}
    to_y = {"dp": z * ny + other_y}

    def turn(k):
        return lax.rem(z + k + nz, nz)

    def to_z(k):
        return {"dp": turn(k) * ny + y}

    def pieces(q, o, u, d):
        low, high = slice(0, units // 2), slice(units // 2, units)
        ends = slice(0, 2 * local), slice(2 * local, 3 * local)
        cuts = ((q, ends[0]), (q, ends[1]), (o, slice(0, local)))
        cuts += ((u, low), (u, high), (d, low), (d, high))
        return tuple(ref.at[:, cut] for ref, cut in cuts)

    shard = pieces(sq, so, su, sd) + (sn,)
    result = pieces(oq, oo, ou, od)

    def remote(src, dst, send, recv, target):
        return pltpu.make_async_remote_copy(
            src_ref=src,
            dst_ref=dst,
            send_sem=send,
            recv_sem=recv,
            device_id=target,
            device_id_type=MESH,
        )

    def each(count, body):
        lax.fori_loop(0, count, lambda i, none: (body(i), none)[1], 0)


    def gather_z(l, m, k):
        return remote(
            shard[m], full[m].at[l, z, y], az_s.at[m, k - 1], az_r.at[m, k - 1], to_z(k)
        )

    def gather_y(l, m, k, src=None):
        ref = full[m].at[l, turn(-k), y]
        return remote(ref if src is None else src, ref, ay_s.at[m, k], ay_r.at[m, k], to_y)

    def gather_core(l, m, k, column, src=None):
        ref = full[m].at[l, turn(-k), column]
        slot = k if column is y else nz + k
        return remote(
            ref if src is None else src, ref, ac_s.at[m, slot], ac_r.at[m, slot], to_core
        )

    def gather_own(l, *mats):
        @pl.when(core == l)
        def _():
            for m in mats:
                gather_y(l, m, 0, shard[m]).start()
                gather_core(l, m, 0, y, shard[m]).start()
                full[m][l, z, y] = shard[m][...]

    def gather_far(l, *mats):
        @pl.when(core == l)
        def _():
            for m in mats:
                for k in range(1, nz):
                    gather_z(l, m, k).start()

    def gather_pass(l, *mats):
        @pl.when(core == l)
        def _():
            for m in mats:

                def one(k, none):
                    gather_z(l, m, k).wait_recv()
                    gather_y(l, m, k).start()
                    gather_core(l, m, k, y).start()
                    return none

                lax.fori_loop(1, nz, one, 0)

    def gather_near(l, m):
        @pl.when(core != l)
        def _():
            each(nz, lambda k: gather_core(l, m, k, y).wait_recv())

    def gather_end(l, *mats, near=True):
        @pl.when(core == l)
        def _():
            for m in mats:

                def one(k):
                    gather_y(l, m, k).wait_recv()
                    gather_core(l, m, k, other_y).start()

                each(nz, one)

        for m in mats:
            if near:
                gather_near(l, m)

        @pl.when(core != l)
        def _():
            for m in mats:
                each(nz, lambda k: gather_core(l, m, k, other_y).wait_recv())

    def gather_drain(l, m):
        @pl.when(core == l)
        def _():
            lax.fori_loop(1, nz, lambda k, none: (gather_z(l, m, k).wait_send(), none)[1], 0)

            def one(k):
                gather_y(l, m, k).wait_send()
                gather_core(l, m, k, y).wait_send()
                gather_core(l, m, k, other_y).wait_send()

            each(nz, one)


    def sum_core(l, m, part):
        column = (other_y, y)[part]
        return remote(
            full[m].at[l, :, column],
            summed[m].at[:, column],
            gc_s.at[m, part],
            gc_r.at[m, part],
            to_core,
        )

    def sum_y(l, m, k):
        return remote(
            full[m].at[l, k, other_y], from_y[m].at[k], gy_s.at[m, k], gy_r.at[m, k], to_y
        )

    def sum_z(l, m, k):
        return remote(
            full[m].at[l, turn(k), y],
            from_z[m].at[k - 1],
            gz_s.at[m, k - 1],
            gz_r.at[m, k - 1],
            to_z(k),
        )

    def sum_start(l, m):
        @pl.when(core != l)
        def _():
            sum_core(l, m, 0).start()
            sum_core(l, m, 1).start()

    def sum_first(l, m):
        @pl.when(core == l)
        def _():
            sum_core(l, m, 0).wait_recv()

            def one(k):
                both = full[m][l, k, other_y].astype(F32) + summed[m][k, other_y].astype(F32)
                full[m][l, k, other_y] = both.astype(BF)
                sum_y(l, m, k).start()

            each(nz, one)

    def sum_second(l, m):
        @pl.when(core == l)
        def _():
            sum_core(l, m, 1).wait_recv()

            def total(k):
                at = turn(k)
                sum_y(l, m, at).wait_recv()
                both = full[m][l, at, y].astype(F32) + summed[m][at, y].astype(F32)
                return both + from_y[m][at].astype(F32)

            def one(k, none):
                full[m][l, turn(k), y] = total(k).astype(BF)
                sum_z(l, m, k).start()
                return none

            lax.fori_loop(1, nz, one, 0)
            result[m][...] = total(0)

    def sum_last(l, m):
        @pl.when(core == l)
        def _():
            def one(k, none):
                sum_z(l, m, k).wait_recv()
                result[m][...] += from_z[m][k - 1].astype(F32)
                return none

            lax.fori_loop(1, nz, one, 0)

    def sum_drain(l, m):
        @pl.when(core != l)
        def _():
            sum_core(l, m, 0).wait_send()
            sum_core(l, m, 1).wait_send()

        @pl.when(core == l)
        def _():
            each(nz, lambda k: sum_y(l, m, k).wait_send())
            lax.fori_loop(1, nz, lambda k, none: (sum_z(l, m, k).wait_send(), none)[1], 0)


    def vec_core(l):
        return remote(ng.at[l], rn, gc_s.at[PIECES, 0], gc_r.at[PIECES, 0], to_core)

    def vec_y(l):
        return remote(ng.at[2], yn, gy_s.at[PIECES, 0], gy_r.at[PIECES, 0], to_y)

    def vec_z(l, k):
        return remote(
            ng.at[3], vn.at[k - 1], gz_s.at[PIECES, k - 1], gz_r.at[PIECES, k - 1], to_z(k)
        )

    def vec_start(l):
        @pl.when(core != l)
        def _():
            vec_core(l).start()

    def vec_first(l):
        @pl.when(core == l)
        def _():
            vec_core(l).wait_recv()
            ng[2] = ng[l] + rn[...]
            vec_y(l).start()

    def vec_second(l):
        @pl.when(core == l)
        def _():
            vec_y(l).wait_recv()
            ng[3] = ng[2] + yn[...]
            for k in range(1, nz):
                vec_z(l, k).start()

    def vec_last(l):
        @pl.when(core == l)
        def _():
            total = ng[3]
            for k in range(1, nz):
                vec_z(l, k).wait_recv()
                total = total + vn[k - 1]
            on[...] = total

    def vec_drain(l):
        @pl.when(core != l)
        def _():
            vec_core(l).wait_send()

        @pl.when(core == l)
        def _():
            vec_y(l).wait_send()
            for k in range(1, nz):
                vec_z(l, k).wait_send()


    def exchange(i, c):
        return remote(xs.at[c], xr.at[i % 2, c], xs_sem.at[c], xr_sem.at[i % 2, c], to_x)

    def send(i, c):
        exchange(i, c).start()

    def arrive(i, c):
        exchange(i, c).wait()

    def both(i, c, r):
        rows = pl.ds(r * SUB, SUB)
        return xs[c, rows].astype(F32) + xr[i % 2, c, rows].astype(F32)

    def chunk_rows(c):
        return pl.ds(pl.multiple_of(c * CHUNK, CHUNK), CHUNK)

    def sub_rows(c, r):
        return pl.ds(pl.multiple_of(c * CHUNK + r * SUB, SUB), SUB)

    def columns(j, span):
        return pl.ds(pl.multiple_of(j * span, LANES), span)


    def out_copy(l, which, src, dst):
        def away():
            return remote(src, dst.at[core], out_send.at[which], out_recv.at[which], to_core)

        def here():
            return pltpu.make_async_copy(src, dst.at[core], local_sem.at[which])

        return here, away

    def out_start(l, which, src, dst):
        here, away = out_copy(l, which, src, dst)

        @pl.when(core == l)
        def _():
            here().start()

        @pl.when(core != l)
        def _():
            away().start()

    def out_wait(l, which, src, dst):
        here, away = out_copy(l, which, src, dst)

        @pl.when(core == l)
        def _():
            here().wait()
            remote(
                src, dst.at[1 - core], out_send.at[which], out_recv.at[which], to_core
            ).wait_recv()

        @pl.when(core != l)
        def _():
            away().wait_send()


    def project(l, c):
        rows = chunk_rows(c)
        for m, span in ((QK, slice(0, 2 * local)), (V, slice(2 * local, 3 * local))):
            packed[l, rows, span] = dot(zin[l, rows], flat_rows(full[m][l])).astype(BF)

    low_lane = lax.broadcasted_iota(jnp.int32, (1, LANES), 1) < LANES // 2

    def half(value, h):
        keep = low_lane if h == 0 else jnp.logical_not(low_lane)
        return jnp.where(keep, value, jnp.zeros_like(value))

    def attend(l, c):
        rows = chunk_rows(c)
        lanes = columns(c, CHUNK)
        keys = jnp.concatenate([keys_ref[...]] * (CHUNK // LANES), 1)
        allowed = keys == groups_ref[pl.ds(l, 1), lanes]

        def one(j):
            query = packed[l, rows, columns(j, LANES)]
            key = packed[l, :, pl.ds(pl.multiple_of(local + j * LANES, LANES), LANES)]
            value = packed[l, :, pl.ds(pl.multiple_of(2 * local + j * LANES, LANES), LANES)]
            value_t = value.astype(F32).T.astype(BF)
            parts = []
            for h in range(2):
                scores = dot_nt(key, half(query, h)) * scale
                scores = jnp.where(allowed, scores, -1e9)
                top = jnp.max(scores, 0, keepdims=True)
                expo = jnp.exp(scores - top)
                low = (expo * (1.0 / jnp.sum(expo, 0, keepdims=True))).astype(BF)
                prob[l, 2 * j + h, :, lanes] = low
                parts.append(dot(value_t[h * (LANES // 2) : (h + 1) * (LANES // 2)], low))
            mixed[l, rows, columns(j, LANES)] = jnp.concatenate(parts, 0).T.astype(BF)

        each(local // LANES, one)

    def send_product(i, l, c, *pairs):
        def one(j):
            total = 0.0
            for left, m in pairs:
                right = flat_rows(full[m][l, pl.ds(j * (nz // 2), nz // 2)])
                total = total + dot_nt(left(), right)
            xs[c, :, columns(j, width // 2)] = total.astype(BF)

        each(2, one)
        send(i, c)

    def attend_out(i, l, c):
        send_product(i, l, c, (lambda: mixed[l, chunk_rows(c)], O))

    def gather_norms(l):
        norms[l] = jnp.sum(flat_rows(full[PIECES][l]).reshape(nz * ny, 8, width), 0)

    def norm_of(l, which):
        return norms[l, which : which + 1], norms[l, 2 + which : 3 + which]

    def normalize(value):
        center = value - jnp.mean(value, -1, keepdims=True)
        inverse = lax.rsqrt(jnp.mean(center * center, -1, keepdims=True) + eps)
        return center * inverse, inverse

    def expand(i, l, c):
        rows = chunk_rows(c)
        arrive(i, c)
        gain, shift = norm_of(l, 0)

        def one(r):
            sub = sub_rows(c, r)
            normed, inverse = normalize(zin[l, sub].astype(F32) + both(i, c, r))
            norm1[l, sub] = normed
            inv1[l, sub] = inverse
            hid[l, sub] = (normed * gain + shift).astype(BF)

        each(CHUNK // SUB, one)

        def tile(m):
            cols = slice((m - UA) * units // 2, (m - UA + 1) * units // 2)
            work[...] = dot(hid[l, rows], flat_rows(full[m][l]))

            def piece(r):
                sub = sub_rows(c, r)
                pre = work[pl.ds(pl.multiple_of(r * SUB, SUB), SUB)]
                lower = 0.5 + 0.5 * lax.erf(pre * 0.7071067811865476)
                density = jnp.exp(-0.5 * pre * pre) * 0.3989422804014327
                act[l, sub, cols] = (pre * lower).astype(BF)
                slope[l, sub, cols] = (lower + pre * density).astype(BF)

            each(CHUNK // SUB, piece)

        tile(UA)
        tile(UB)

    def halves(ref, l, rows):
        low, high = slice(0, units // 2), slice(units // 2, units)
        return (lambda: ref[l, rows, low]), (lambda: ref[l, rows, high])

    def contract(i, l, c):
        low, high = halves(act, l, chunk_rows(c))
        send_product(i, l, c, (low, DA), (high, DB))

    def second_norm(i, l, c, r):
        sub = sub_rows(c, r)
        gain, shift = norm_of(l, 0)
        hidden = norm1[l, sub] * gain + shift
        return normalize(hidden + both(i, c, r))

    def norm_back(grad, normed, inverse, gain):
        scaled = grad * gain
        inner = (
            scaled
            - jnp.mean(scaled, -1, keepdims=True)
            - normed * jnp.mean(scaled * normed, -1, keepdims=True)
        )
        return inner * inverse

    def count(l, which, grad, normed):
        ng[l, which : which + 1] += jnp.sum(grad * normed, 0, keepdims=True)
        ng[l, 2 + which : 3 + which] += jnp.sum(grad, 0, keepdims=True)

    def top_back(l, c, r, grad, normed, inverse):
        sub = sub_rows(c, r)
        count(l, 1, grad, normed)
        back = norm_back(grad, normed, inverse, norm_of(l, 1)[0])
        gsum[sub] = back
        gtok[sub] = back.astype(BF)

    def expand_back(i, l, c):
        rows = chunk_rows(c)
        for m in (DA, DB):
            cols = slice((m - DA) * units // 2, (m - DA + 1) * units // 2)
            grad = dot(gtok[rows], flat_rows(full[m][l]))
            slope[l, rows, cols] = (grad * slope[l, rows, cols].astype(F32)).astype(BF)

        low, high = halves(slope, l, rows)
        send_product(i, l, c, (low, UA), (high, UB))

    def flip(source):
        step = length // 4

        def one(j):
            rows = pl.ds(pl.multiple_of(j * step, step), step)
            turned[:, columns(j, step)] = source[rows].astype(F32).T.astype(BF)

        each(4, one)

    def weight_grad(l, m, right, start=0):
        gather_drain(l, m)

        def tile(j):
            cols = pl.ds(pl.multiple_of(start + j * local, LANES), local)
            for part in range(2):
                rows = slice(part * width // 2, (part + 1) * width // 2)
                grad = dot(turned[rows], right[l, :, cols]).astype(BF)
                full[m][
                    l, part * nz // 2 : (part + 1) * nz // 2, :, :, columns(j, local)
                ] = grad.reshape(nz // 2, ny, width // (nz * ny), local)

        each(full[m].shape[-1] // local, tile)
        sum_start(l, m)

    def attend_back(l):
        def one(j):
            q_cols = columns(j, LANES)
            k_cols = pl.ds(pl.multiple_of(local + j * LANES, LANES), LANES)
            v_cols = pl.ds(pl.multiple_of(2 * local + j * LANES, LANES), LANES)
            query, key, value = (packed[l, :, cols] for cols in (q_cols, k_cols, v_cols))
            grad = gmix[:, q_cols]
            key_t = key.astype(F32).T.astype(BF)
            queries, keys, values = [], [], []
            for h in range(2):
                low = prob[l, 2 * j + h]
                wide = low.astype(F32)
                product = wide * dot_nt(value, half(grad, h))
                total = jnp.sum(product, 0, keepdims=True)
                back = (product - wide * total).astype(BF)
                values.append(dot(low, grad))
                keys.append(dot(back, query))
                queries.append(dot(key_t[h * (LANES // 2) : (h + 1) * (LANES // 2)], back))
            packed[l, :, q_cols] = (jnp.concatenate(queries, 0).T * scale).astype(BF)
            packed[l, :, k_cols] = (jnp.where(low_lane, keys[0], keys[1]) * scale).astype(BF)
            packed[l, :, v_cols] = jnp.where(low_lane, values[0], values[1]).astype(BF)

        each(local // LANES, one)

    def middle_back(i, l, c):
        rows = chunk_rows(c)
        arrive(i, c)

        def one(r):
            sub = sub_rows(c, r)
            grad = gsum[sub] + both(i, c, r)
            normed = norm1[l, sub]
            count(l, 0, grad, normed)
            back = norm_back(grad, normed, inv1[l, sub], norm_of(l, 0)[0])
            gsum[sub] = back
            gtok[sub] = back.astype(BF)

        each(CHUNK // SUB, one)
        gmix[rows] = dot(gtok[rows], flat_rows(full[O][l])).astype(BF)

    def project_back(i, l, c):
        rows = chunk_rows(c)
        send_product(
            i,
            l,
            c,
            (lambda: packed[l, rows, 0 : 2 * local], QK),
            (lambda: packed[l, rows, 2 * local : 3 * local], V),
        )


    barrier = pltpu.get_barrier_semaphore()
    peers = [to_x, to_core, to_y] + [to_z(k) for k in range(1, nz)]
    for peer in peers:
        pl.semaphore_signal(barrier, inc=1, device_id=peer, device_id_type=MESH)
    first_rows = pltpu.make_async_copy(x_ref.at[core], zin.at[0], local_sem.at[4])
    top_rows = pltpu.make_async_copy(go_ref.at[core], gtop, local_sem.at[5])
    first_rows.start()
    top_rows.start()
    ng[...] = jnp.zeros_like(ng)
    pl.semaphore_wait(barrier, len(peers))

    gather_own(0, QK, V, N, O, UA, UB, DA, DB)
    gather_far(0, QK, V, N, O)
    gather_pass(0, QK, V, N)
    gather_far(0, UA)
    gather_pass(0, O)
    gather_end(0, QK, V, N)
    gather_own(1, QK, V, N, O, UA, UB, DA, DB)
    first_rows.wait()
    gather_norms(0)
    each(chunks, lambda c: project(0, c))
    gather_far(0, UB)
    attend(0, 0)
    gather_pass(0, UA)
    gather_far(0, DA)
    gather_end(0, O)
    attend_out(0, 0, 0)
    attend(0, 1)
    attend_out(0, 0, 1)
    gather_pass(0, UB)
    gather_far(0, DB)
    gather_end(0, UA, UB)
    gather_pass(0, DA)
    expand(0, 0, 0)
    gather_pass(0, DB)
    gather_near(0, DB)
    gather_far(1, QK, V, N, O)
    expand(0, 0, 1)
    gather_end(0, DA)
    gather_end(0, DB, near=False)
    gather_far(1, UA)
    each(chunks, lambda c: contract(1, 0, c))

    def into_second(c):
        arrive(1, c)
        gain, shift = norm_of(0, 1)

        def one(r):
            sub = sub_rows(c, r)
            normed, inverse = second_norm(1, 0, c, r)
            norm2[sub] = normed
            inv2[sub] = inverse
            zin[1, sub] = (normed * gain + shift).astype(BF)

        each(CHUNK // SUB, one)

    into_second(0)
    gather_pass(1, QK, V, N, O)
    gather_far(1, UB)
    gather_pass(1, UA)
    gather_far(1, DA)
    into_second(1)
    out_start(0, 0, zin.at[1], lo_ref)
    gather_end(1, QK, V, N)
    gather_norms(1)
    each(chunks, lambda c: project(1, c))
    gather_pass(1, UB)
    gather_far(1, DB)
    attend(1, 0)
    gather_end(1, O)
    attend_out(2, 1, 0)
    attend(1, 1)
    attend_out(2, 1, 1)
    gather_pass(1, DA)
    gather_end(1, UA, UB)
    expand(2, 1, 0)
    gather_pass(1, DB)
    gather_end(1, DA, DB)
    contract(3, 1, 0)
    expand(2, 1, 1)
    contract(3, 1, 1)
    top_rows.wait()

    def over_top(c):
        arrive(3, c)
        gain, shift = norm_of(1, 1)

        def one(r):
            sub = sub_rows(c, r)
            normed, inverse = second_norm(3, 1, c, r)
            top_back(1, c, r, gtop[sub].astype(F32), normed, inverse)
            gtop[sub] = (normed * gain + shift).astype(BF)

        each(CHUNK // SUB, one)

    over_top(0)
    expand_back(4, 1, 0)
    over_top(1)
    expand_back(4, 1, 1)
    out_start(1, 1, gtop, lo_ref)
    flip(gtok)
    weight_grad(1, DA, act)
    weight_grad(1, DB, act, units // 2)
    flip(hid.at[1])
    weight_grad(1, UA, slope)
    weight_grad(1, UB, slope, units // 2)
    middle_back(4, 1, 0)
    sum_first(1, DA)
    middle_back(4, 1, 1)
    sum_first(1, DB)
    attend_back(1)
    each(chunks, lambda c: project_back(5, 1, c))
    sum_first(1, UA)
    flip(gtok)
    weight_grad(1, O, mixed)
    flip(zin.at[1])
    weight_grad(1, QK, packed)
    weight_grad(1, V, packed, 2 * local)
    vec_start(1)
    sum_second(1, DA)
    sum_first(1, UB)

    def under(c):
        arrive(5, c)

        def one(r):
            sub = sub_rows(c, r)
            low = (gsum[sub] + both(5, c, r)).astype(BF)
            gin[sub] = low
            top_back(0, c, r, low.astype(F32), norm2[sub], inv2[sub])

        each(CHUNK // SUB, one)
        expand_back(6, 0, c)

    under(0)
    sum_second(1, DB)
    sum_first(1, O)
    sum_first(1, QK)
    sum_second(1, UA)
    under(1)
    out_start(1, 3, gin, ig_ref)
    flip(gtok)
    weight_grad(0, DA, act)
    weight_grad(0, DB, act, units // 2)
    flip(hid.at[0])
    weight_grad(0, UA, slope)
    weight_grad(0, UB, slope, units // 2)
    sum_first(1, V)
    vec_first(1)
    sum_second(1, UB)
    middle_back(6, 0, 0)
    sum_first(0, DA)
    middle_back(6, 0, 1)
    sum_first(0, DB)
    sum_second(1, O)
    sum_second(1, QK)
    attend_back(0)
    each(chunks, lambda c: project_back(7, 0, c))
    sum_first(0, UA)
    sum_second(0, DA)
    flip(gtok)
    weight_grad(0, O, mixed)
    flip(zin.at[0])
    weight_grad(0, QK, packed)
    weight_grad(0, V, packed, 2 * local)
    vec_start(0)
    sum_first(0, UB)
    sum_second(0, DB)
    sum_second(1, V)
    vec_second(1)
    sum_first(0, O)
    sum_first(0, QK)
    sum_first(0, V)
    vec_first(0)
    sum_second(0, UA)

    def bottom(c):
        arrive(7, c)

        def one(r):
            sub = sub_rows(c, r)
            gtop[sub] = (gsum[sub] + both(7, c, r)).astype(BF)

        each(CHUNK // SUB, one)

    out_wait(1, 1, gtop, lo_ref)
    bottom(0)
    sum_second(0, UB)
    bottom(1)
    out_start(0, 2, gtop, ig_ref)
    sum_second(0, O)
    sum_second(0, QK)
    sum_second(0, V)
    vec_second(0)
    for l in (1, 0):
        for m in (DA, DB, UA, UB, O, QK, V):
            sum_last(l, m)
        vec_last(l)
    for l in range(2):
        for m in range(PIECES):
            sum_drain(l, m)
        vec_drain(l)
        gather_drain(l, N)
    out_wait(0, 0, zin.at[1], lo_ref)
    out_wait(0, 2, gtop, ig_ref)
    out_wait(1, 3, gin, ig_ref)


def fused(sizes, x, grad, keys, groups, shards_in):
    nz, ny, length, width, local, units, eps, scale = sizes
    block = width // (nz * ny)
    chunks = length // CHUNK
    spans = (2 * local, local, local) + (units // 2,) * 4
    outs = (3 * local, local, units, units)
    dma = pltpu.SemaphoreType.DMA
    vmem = pltpu.VMEM
    scratch = [vmem((2, nz, ny, block, span), BF) for span in spans]
    scratch += [vmem((2, nz, ny, 8, width), F32)]
    scratch += [vmem((nz, ny, block, span), BF) for span in spans]
    scratch += [vmem((nz, block, span), BF) for span in spans]
    scratch += [vmem((nz - 1, block, span), BF) for span in spans]
    scratch += [
        vmem((8, width), F32),
        vmem((8, width), F32),
        vmem((nz - 1, 8, width), F32),
        vmem((4, 8, width), F32),
        vmem((2, length, width), BF),
        vmem((2, length, 3 * local), BF),
        vmem((2, local // HEAD, length, length), BF),
        vmem((2, length, local), BF),
        vmem((2, length, width), F32),
        vmem((2, length, 1), F32),
        vmem((2, length, width), BF),
        vmem((2, length, units), BF),
        vmem((2, length, units), BF),
        vmem((length, width), F32),
        vmem((length, 1), F32),
        vmem((length, width), F32),
        vmem((length, width), BF),
        vmem((length, local), BF),
        vmem((width, length), BF),
        vmem((length, width), BF),
        vmem((length, width), BF),
        vmem((CHUNK, units // 2), F32),
        vmem((2, 8, width), F32),
        vmem((chunks, CHUNK, width), BF),
        vmem((2, chunks, CHUNK, width), BF),
        dma((6,)),
        dma((4,)),
        dma((4,)),
        dma((chunks,)),
        dma((2, chunks)),
        dma((PIECES + 1, nz - 1)),
        dma((PIECES + 1, nz - 1)),
        dma((PIECES + 1, nz)),
        dma((PIECES + 1, nz)),
        dma((PIECES + 1, 2 * nz)),
        dma((PIECES + 1, 2 * nz)),
        dma((PIECES + 1, 2)),
        dma((PIECES + 1, 2)),
        dma((PIECES + 1, nz)),
        dma((PIECES + 1, nz)),
        dma((PIECES + 1, nz - 1)),
        dma((PIECES + 1, nz - 1)),
    ]
    anywhere = pl.BlockSpec(memory_space=pl.ANY)
    inside = pl.BlockSpec(memory_space=pltpu.VMEM)
    return pl.pallas_call(
        functools.partial(kernel, sizes),
        out_shape=[jax.ShapeDtypeStruct((2, length, width), BF)] * 2
        + [jax.ShapeDtypeStruct((block, span), F32) for span in outs]
        + [jax.ShapeDtypeStruct((8, width), F32)],
        in_specs=[anywhere] * 2 + [inside] * 7,
        out_specs=[anywhere] * 2 + [inside] * 5,
        scratch_shapes=scratch,
        compiler_params=pltpu.CompilerParams(
            collective_id=0, has_side_effects=True, vmem_limit_bytes=63 << 20
        ),
    )(x, grad, keys, groups, *shards_in)


def kernel_shards(
    inputs, segments, partner, grad_output, w_qkv, w_out, w_up, w_down, norm_gain, norm_shift
):
    core = lax.axis_index("section")
    place = lax.axis_index("dp")
    parts = lax.axis_size("dp")
    length, width = inputs.shape[1:]
    local, units = w_out.shape[1], w_up.shape[2]
    block = width // parts
    sizes = (parts // 2, 2, length, width, local, units, norm_eps, score_scale)
    own = lax.dynamic_index_in_dim(segments, core, 0, False)
    mapped = partner_of(own, lax.dynamic_index_in_dim(partner, core, 0, False))
    keys = jnp.broadcast_to(own[:, None], (length, LANES))
    groups = jnp.stack([own, mapped])
    vectors = jnp.concatenate([norm_gain[0], norm_shift[0]]).astype(F32)
    spread = lax.dynamic_update_slice(
        jnp.zeros((8, width), F32), vectors, (0, place * block)
    )
    shards_in = (
        w_qkv[0].reshape(block, 3 * local),
        w_out[0].T,
        w_up[0],
        w_down[0].T,
        spread,
    )
    outs = fused(sizes, inputs, grad_output, keys, groups, shards_in)
    layer_outputs, input_grads, g_qkv, g_out, g_up, g_down, g_norm = outs
    own_norm = lax.dynamic_slice(g_norm, (0, place * block), (8, block))
    return (
        layer_outputs[None],
        input_grads[None],
        g_qkv.reshape(1, block, 3, local),
        g_out.T[None],
        g_up[None],
        g_down.T[None],
        own_norm[None, 0:2],
        own_norm[None, 2:4],
    )


def solution(mesh):
    placed = (
        P("dp", None, None),
        P("dp", None),
        P("dp", None),
        P("dp", None, None),
        P("section", "dp", None, "tensor"),
        P("section", "tensor", "dp"),
        P("section", "dp", "tensor"),
        P("section", "tensor", "dp"),
        P("section", None, "dp"),
        P("section", None, "dp"),
    )
    block = WIDTH // mesh.shape["dp"]
    whole_tiles = block * mesh.shape["dp"] == WIDTH and block % 16 == 0
    return jax.shard_map(
        kernel_shards if whole_tiles else shards,
        mesh=mesh,
        in_specs=placed,
        out_specs=(
            P("section", "dp", None, None),
            P("section", "dp", None, None),
            P("section", "dp", None, "tensor"),
            P("section", "tensor", "dp"),
            P("section", "dp", "tensor"),
            P("section", "tensor", "dp"),
            P("section", None, "dp"),
            P("section", None, "dp"),
        ),
        check_vma=False,
    )
```

```python
import functools

import jax
import jax.numpy as jnp
from jax import lax
from jax.experimental import pallas as pl
from jax.experimental.pallas import tpu as pltpu
from jax.sharding import PartitionSpec as P

HEAD = 64
WIDTH = 768


norm_eps = 1e-06
score_scale = 0.125
masked_value = -1000000000.0


def partner_of(segment_ids, partner):
    table = jnp.arange(partner.shape[-1], dtype=jnp.int32)
    hits = segment_ids[..., None] == table
    return jnp.sum(jnp.where(hits, partner[None, :], 0), -1)


def layer_norm(values, gain, shift):
    center = values - jnp.mean(values, -1, keepdims=True)
    inverse = lax.rsqrt(jnp.mean(center * center, -1, keepdims=True) + norm_eps)
    normed = center * inverse
    return (normed * gain + shift, normed, inverse)


def norm_back(grad, normed, inverse, gain):
    scaled = grad * gain
    inner = (
        scaled
        - jnp.mean(scaled, -1, keepdims=True)
        - normed * jnp.mean(scaled * normed, -1, keepdims=True)
    )
    return inner * inverse


def gelu_slope(values):
    lower = 0.5 * (1.0 + lax.erf(values * 0.7071067811865476))
    density = jnp.exp(-0.5 * values * values) * 0.3989422804014327
    return lower + values * density


def swapped(value, axis):
    size = lax.axis_size(axis)
    return lax.ppermute(value, axis, [(i, size - 1 - i) for i in range(size)])


def tensor_sum(partial_value):
    low = partial_value.astype(jnp.bfloat16)
    return low.astype(jnp.float32) + swapped(low, "tensor").astype(jnp.float32)


def masked_scores(query, key, query_groups, key_groups):
    scores = (
        jnp.einsum("qhd,khd->hqk", query, key, preferred_element_type=jnp.float32) * score_scale
    )
    allowed = query_groups[:, None] == key_groups[None, :]
    return jnp.where(allowed[None], scores, masked_value)


def attend(query, key, value, query_groups, key_groups):
    scores = masked_scores(query, key, query_groups, key_groups)
    top = jnp.max(scores, -1, keepdims=True)
    expo = jnp.exp(scores - top)
    total = jnp.sum(expo, -1, keepdims=True)
    probs = (expo / total).astype(jnp.bfloat16)
    mixed = jnp.einsum("hqk,khd->qhd", probs, value, preferred_element_type=jnp.float32)
    return (mixed.astype(jnp.bfloat16), (top + jnp.log(total))[..., 0])


def attend_back(query, key, value, query_groups, key_groups, spread, grad_mixed):
    scores = masked_scores(query, key, query_groups, key_groups)
    probs = jnp.exp(scores - spread[..., None])
    probs_low = probs.astype(jnp.bfloat16)
    grad_probs = jnp.einsum("qhd,khd->hqk", grad_mixed, value, preferred_element_type=jnp.float32)
    grad_value = jnp.einsum(
        "hqk,qhd->khd", probs_low, grad_mixed, preferred_element_type=jnp.float32
    )
    row_dot = jnp.sum(probs * grad_probs, -1, keepdims=True)
    grad_scores = (probs * (grad_probs - row_dot)).astype(jnp.bfloat16)
    grad_query = (
        jnp.einsum("hqk,khd->qhd", grad_scores, key, preferred_element_type=jnp.float32)
        * score_scale
    )
    grad_key = (
        jnp.einsum("hqk,qhd->khd", grad_scores, query, preferred_element_type=jnp.float32)
        * score_scale
    )
    return jnp.stack(
        [
            grad_query.astype(jnp.bfloat16),
            grad_key.astype(jnp.bfloat16),
            grad_value.astype(jnp.bfloat16),
        ],
        1,
    )


def layer_forward(flat, weights, query_groups, key_groups):
    w_qkv, w_out, w_up, w_down, gains, shifts = weights
    length = flat.shape[0]
    local = w_qkv.shape[2]
    packed = jnp.einsum("nd,dcm->ncm", flat, w_qkv, preferred_element_type=jnp.float32).astype(
        jnp.bfloat16
    )
    heads = packed.reshape(length, 3, local // HEAD, HEAD)
    mixed, spread = attend(heads[:, 0], heads[:, 1], heads[:, 2], query_groups, key_groups)
    mixed_flat = mixed.reshape(length, local)
    attn_out = tensor_sum(jnp.dot(mixed_flat, w_out, preferred_element_type=jnp.float32))
    hidden, normed_first, inverse_first = layer_norm(
        flat.astype(jnp.float32) + attn_out, gains[0], shifts[0]
    )
    hidden_low = hidden.astype(jnp.bfloat16)
    pre = jnp.dot(hidden_low, w_up, preferred_element_type=jnp.float32)
    act = jax.nn.gelu(pre, approximate=False).astype(jnp.bfloat16)
    ffn_out = tensor_sum(jnp.dot(act, w_down, preferred_element_type=jnp.float32))
    result, normed_second, inverse_second = layer_norm(hidden + ffn_out, gains[1], shifts[1])
    kept = (
        flat,
        heads,
        spread,
        mixed_flat,
        normed_first,
        inverse_first,
        hidden_low,
        pre,
        act,
        normed_second,
        inverse_second,
    )
    return (result.astype(jnp.bfloat16), kept)


def layer_backward(grad_result, kept, weights, query_groups, key_groups):
    w_qkv, w_out, w_up, w_down, gains, shifts = weights
    (
        flat,
        heads,
        spread,
        mixed_flat,
        normed_first,
        inverse_first,
        hidden_low,
        pre,
        act,
        normed_second,
        inverse_second,
    ) = kept
    length = flat.shape[0]
    local = w_qkv.shape[2]
    gain_second = jnp.sum(grad_result * normed_second, 0)
    shift_second = jnp.sum(grad_result, 0)
    grad_sum2 = norm_back(grad_result, normed_second, inverse_second, gains[1])
    grad_ffn = grad_sum2.astype(jnp.bfloat16)
    grad_down = jnp.einsum("nf,nd->fd", act, grad_ffn, preferred_element_type=jnp.float32)
    grad_act = jnp.einsum("nd,fd->nf", grad_ffn, w_down, preferred_element_type=jnp.float32)
    grad_pre = (grad_act * gelu_slope(pre)).astype(jnp.bfloat16)
    grad_up = jnp.einsum("nd,nf->df", hidden_low, grad_pre, preferred_element_type=jnp.float32)
    grad_hidden = grad_sum2 + tensor_sum(
        jnp.einsum("nf,df->nd", grad_pre, w_up, preferred_element_type=jnp.float32)
    )
    gain_first = jnp.sum(grad_hidden * normed_first, 0)
    shift_first = jnp.sum(grad_hidden, 0)
    grad_resid = norm_back(grad_hidden, normed_first, inverse_first, gains[0])
    grad_attn = grad_resid.astype(jnp.bfloat16)
    grad_out = jnp.einsum("nm,nd->md", mixed_flat, grad_attn, preferred_element_type=jnp.float32)
    grad_mixed = jnp.einsum(
        "nd,md->nm", grad_attn, w_out, preferred_element_type=jnp.float32
    ).astype(jnp.bfloat16)
    grad_mixed = grad_mixed.reshape(length, local // HEAD, HEAD)
    grad_heads = attend_back(
        heads[:, 0], heads[:, 1], heads[:, 2], query_groups, key_groups, spread, grad_mixed
    )
    grad_packed = grad_heads.reshape(length, 3, local)
    grad_qkv = jnp.einsum("nd,ncm->dcm", flat, grad_packed, preferred_element_type=jnp.float32)
    grad_input = grad_resid + tensor_sum(
        jnp.einsum("ncm,dcm->nd", grad_packed, w_qkv, preferred_element_type=jnp.float32)
    )
    grads = (
        grad_qkv.astype(jnp.bfloat16),
        grad_out.astype(jnp.bfloat16),
        grad_up.astype(jnp.bfloat16),
        grad_down.astype(jnp.bfloat16),
        jnp.stack([gain_first, gain_second]),
        jnp.stack([shift_first, shift_second]),
    )
    return (grads, grad_input.astype(jnp.bfloat16))


def shards(
    inputs, segments, partner, grad_output, w_qkv, w_out, w_up, w_down, norm_gain, norm_shift
):
    core = lax.axis_index("section")
    rows = inputs.shape[0] // lax.axis_size("section")

    def per_row(row):
        key_groups = lax.dynamic_index_in_dim(segments, row, 0, False)
        mapped = partner_of(key_groups, lax.dynamic_index_in_dim(partner, row, 0, False))
        flat = lax.dynamic_index_in_dim(inputs, row, 0, False)
        first, kept_first = layer_forward(flat, layers[0], key_groups, key_groups)
        second, kept_second = layer_forward(first, layers[1], mapped, key_groups)
        grad_top = lax.dynamic_index_in_dim(grad_output, row, 0, False).astype(jnp.float32)
        grads_second, grad_mid = layer_backward(
            grad_top, kept_second, layers[1], mapped, key_groups
        )
        grads_first, grad_low = layer_backward(
            grad_mid.astype(jnp.float32), kept_first, layers[0], key_groups, key_groups
        )
        return (first, second, grad_low, grad_mid, grads_first, grads_second)

    def gathered(shard, axis):
        own = lax.all_gather(shard[0], "dp", axis=axis, tiled=True)
        other = swapped(own, "section")
        return (jnp.where(core == 0, own, other), jnp.where(core == 0, other, own))

    pairs = [
        gathered(w_qkv, 0),
        gathered(w_out, 1),
        gathered(w_up, 0),
        gathered(w_down, 1),
        gathered(norm_gain, 1),
        gathered(norm_shift, 1),
    ]
    layers = [
        [pair[layer].astype(jnp.float32) if place > 3 else pair[layer] for place, pair in enumerate(pairs)]
        for layer in range(2)
    ]
    done = [per_row(core * rows + step) for step in range(rows)]

    def summed(first, second, axis):
        mine = jnp.where(core == 0, first, second)
        away = jnp.where(core == 0, second, first)
        both = mine.astype(jnp.float32) + swapped(away, "section").astype(jnp.float32)
        return lax.psum_scatter(both.astype(first.dtype), "dp", scatter_dimension=axis, tiled=True).astype(jnp.float32)

    def total(layer, place):
        value = done[0][4 + layer][place]
        for item in done[1:]:
            value = (value.astype(jnp.float32) + item[4 + layer][place].astype(jnp.float32)).astype(value.dtype)
        return value

    axes = (0, 1, 0, 1, 1, 1)
    sums = [summed(total(0, place), total(1, place), axis) for place, axis in enumerate(axes)]

    def regrouped(first, second):
        mine = jnp.where(core == 0, first, second)
        other = swapped(jnp.where(core == 0, second, first), "section")
        return jnp.where(
            core == 0, jnp.concatenate([mine, other]), jnp.concatenate([other, mine])
        )

    layer_outputs = regrouped(
        jnp.stack([item[0] for item in done]), jnp.stack([item[1] for item in done])
    )
    input_grads = regrouped(
        jnp.stack([item[2] for item in done]), jnp.stack([item[3] for item in done])
    )
    return (layer_outputs[None], input_grads[None]) + tuple(value[None] for value in sums)


MESH = pl.DeviceIdType.MESH
BF = jnp.bfloat16
F32 = jnp.float32
CHUNK = 256
SUB = 128
TILE = 256
LANES = 128
QK, V, O, UA, UB, DA, DB, N = range(8)
PIECES = N
Y_FIRST = (V, O, N)
NT = (((1,), (1,)), ((), ()))
TN = (((0,), (0,)), ((), ()))


def dot(left, right):
    return jnp.dot(left, right, preferred_element_type=F32)


def dot_nt(left, right):
    return lax.dot_general(left, right, NT, preferred_element_type=F32)


def dot_tn(left, right):
    return lax.dot_general(left, right, TN, preferred_element_type=F32)


def flat_rows(value):
    return value.reshape(-1, value.shape[-1])


def kernel(
    sizes,
    x_ref,
    go_ref,
    keys_ref,
    groups_ref,
    sq,
    so,
    su,
    sd,
    sn,
    lo_ref,
    ig_ref,
    oq,
    oo,
    ou,
    od,
    on,
    *refs,
):
    nz, ny, length, width, local, units, eps, scale = sizes
    full, refs = refs[: PIECES + 1], refs[PIECES + 1 :]
    summed, refs = refs[:PIECES], refs[PIECES:]
    from_y, refs = refs[:PIECES], refs[PIECES:]
    from_z, refs = refs[:PIECES], refs[PIECES:]
    (
        rn,
        yn,
        vn,
        ng,
        zin,
        packed,
        prob,
        mixed,
        norm1,
        hid,
        act,
        slope,
        norm2,
        roots,
        gsum,
        gtok,
        gmix,
        gtop,
        gin,
        norms,
        xs,
        xr,
        local_sem,
        out_send,
        out_recv,
        xs_sem,
        xr_sem,
        az_s,
        az_r,
        ay_s,
        ay_r,
        ac_s,
        ac_r,
        gc_s,
        gc_r,
        gy_s,
        gy_r,
        gz_s,
        gz_r,
    ) = refs
    chunks = length // CHUNK
    core = lax.axis_index("section")
    place = lax.axis_index("dp")
    side = lax.axis_index("tensor")
    z, y = place // ny, lax.rem(place, ny)
    other_y = 1 - y
    to_x = {"tensor": 1 - side}
    to_core = {"section": 1 - core}
    to_y = {"dp": z * ny + other_y}

    def turn(k):
        return lax.rem(z + k + nz, nz)

    def to_z(k):
        return {"dp": turn(k) * ny + y}

    def pieces(q, o, u, d):
        low, high = slice(0, units // 2), slice(units // 2, units)
        ends = slice(0, 2 * local), slice(2 * local, 3 * local)
        cuts = ((q, ends[0]), (q, ends[1]), (o, slice(0, local)))
        cuts += ((u, low), (u, high), (d, low), (d, high))
        return tuple(ref.at[:, cut] for ref, cut in cuts)

    shard = pieces(sq, so, su, sd) + (sn,)
    result = pieces(oq, oo, ou, od)

    def remote(src, dst, send, recv, target):
        return pltpu.make_async_remote_copy(
            src_ref=src,
            dst_ref=dst,
            send_sem=send,
            recv_sem=recv,
            device_id=target,
            device_id_type=MESH,
        )

    def each(count, body):
        lax.fori_loop(0, count, lambda i, none: (body(i), none)[1], 0)

    at_end = jnp.logical_or(z == 0, z == nz - 1)
    middle = jnp.logical_not(at_end)
    far_end = jnp.where(z < nz // 2, 0, nz - 1)
    far_origin = nz - 1 - far_end
    near_z = {"dp": jnp.where(z == 0, 1, nz - 2) * ny + y}
    end_z = {"dp": far_end * ny + y}

    def is_far(k):
        return jnp.logical_or(
            jnp.logical_and(z == 0, k == nz - 1), jnp.logical_and(z == nz - 1, k == 1)
        )

    def is_late(k):
        return jnp.logical_or(
            jnp.logical_and(z == 0, k == 1), jnp.logical_and(z == nz - 1, k == nz - 1)
        )

    def offsets(body):
        lax.fori_loop(1, nz, lambda k, none: (body(k), none)[1], 0)


    def column(c):
        return (y, other_y)[c]

    def lines(m):
        return (0, 1) if m in Y_FIRST else (0,)

    def gather_z(l, m, k, c, src=None):
        ref = full[m].at[l, z, column(c)]
        return remote(
            ref if src is None else src,
            ref,
            az_s.at[m, c, k - 1],
            az_r.at[m, c, k - 1],
            to_z(k),
        )

    def gather_relay(l, m, c):
        ref = full[m].at[l, far_origin, column(c)]
        slot = jnp.where(z == 1, 0, nz - 2)
        return remote(ref, ref, az_s.at[m, c, nz - 1], az_r.at[m, c, slot], end_z)

    def gather_y(l, m, k, src=None):
        ref = full[m].at[l, turn(-k), y]
        return remote(ref if src is None else src, ref, ay_s.at[m, k], ay_r.at[m, k], to_y)

    def gather_core(l, m, k, c, src=None):
        ref = full[m].at[l, turn(-k), column(c)]
        slot = k + c * nz
        return remote(
            ref if src is None else src, ref, ac_s.at[m, slot], ac_r.at[m, slot], to_core
        )

    def gather_own(l, *mats):
        @pl.when(core == l)
        def _():
            for m in mats:
                gather_y(l, m, 0, shard[m]).start()
                gather_core(l, m, 0, 0, shard[m]).start()
                full[m][l, z, y] = shard[m][...]

    def gather_far(l, *mats):
        @pl.when(core == l)
        def _():
            for m in mats:

                def one(k):
                    @pl.when(jnp.logical_not(is_far(k)))
                    def _():
                        gather_z(l, m, k, 0, shard[m]).start()

                offsets(one)

    def gather_cross(l, *mats):
        @pl.when(core == l)
        def _():
            for m in mats:
                gather_y(l, m, 0).wait_recv()
                gather_core(l, m, 0, 1).start()

                def one(k):
                    @pl.when(jnp.logical_not(is_far(k)))
                    def _():
                        gather_z(l, m, k, 1).start()

                offsets(one)

    def gather_hand(l, m, k, c):
        gather_z(l, m, k, c).wait_recv()
        gather_core(l, m, k, c).start()
        if m not in Y_FIRST:
            gather_y(l, m, k).start()

    def gather_pass(l, *mats):
        @pl.when(core == l)
        def _():
            for m in mats:
                for c in lines(m):

                    def one(k):
                        @pl.when(jnp.logical_not(is_late(k)))
                        def _():
                            gather_hand(l, m, k, c)

                        @pl.when(jnp.logical_and(middle, k == nz // 2))
                        def _():
                            gather_relay(l, m, c).start()

                    offsets(one)

    def gather_late(l, *mats):
        @pl.when(jnp.logical_and(core == l, at_end))
        def _():
            for m in mats:
                for c in lines(m):
                    gather_hand(l, m, jnp.where(z == 0, 1, nz - 1), c)

    def gather_near(l, m):
        @pl.when(core != l)
        def _():
            each(nz, lambda k: gather_core(l, m, k, 0).wait_recv())

    def gather_end(l, *mats, near=True):
        @pl.when(core == l)
        def _():
            for m in mats:
                if m not in Y_FIRST:

                    def one(k):
                        gather_y(l, m, k).wait_recv()
                        gather_core(l, m, k, 1).start()

                    each(nz, one)

        for m in mats:
            if near:
                gather_near(l, m)

        @pl.when(core != l)
        def _():
            for m in mats:
                each(nz, lambda k: gather_core(l, m, k, 1).wait_recv())

    def gather_drain(l, m):
        @pl.when(core == l)
        def _():
            for c in lines(m):

                def one(k):
                    @pl.when(jnp.logical_not(is_far(k)))
                    def _():
                        gather_z(l, m, k, c).wait_send()

                offsets(one)

                @pl.when(middle)
                def _():
                    gather_relay(l, m, c).wait_send()

            gather_y(l, m, 0).wait_send()
            if m not in Y_FIRST:
                offsets(lambda k: gather_y(l, m, k).wait_send())

            def core_sent(k):
                gather_core(l, m, k, 0).wait_send()
                gather_core(l, m, k, 1).wait_send()

            each(nz, core_sent)


    def sum_core(l, m, part):
        column = (other_y, y)[part]
        return remote(
            full[m].at[l, :, column],
            summed[m].at[:, column],
            gc_s.at[m, part],
            gc_r.at[m, part],
            to_core,
        )

    def sum_y(l, m, k):
        return remote(
            full[m].at[l, k, other_y], from_y[m].at[k], gy_s.at[m, k], gy_r.at[m, k], to_y
        )

    def sum_z(l, m, k):
        return remote(
            full[m].at[l, turn(k), y],
            from_z[m].at[k - 1],
            gz_s.at[m, k - 1],
            gz_r.at[m, k - 1],
            to_z(k),
        )

    def sum_near(l, m, k):
        return remote(
            full[m].at[l, turn(k), y],
            from_z[m].at[nz - 1],
            gz_s.at[m, k - 1],
            gz_r.at[m, nz - 1],
            near_z,
        )

    def sum_start(l, m):
        @pl.when(core != l)
        def _():
            sum_core(l, m, 0).start()
            sum_core(l, m, 1).start()

    def sum_first(l, m):
        @pl.when(core == l)
        def _():
            sum_core(l, m, 0).wait_recv()

            def one(k):
                both = full[m][l, k, other_y].astype(F32) + summed[m][k, other_y].astype(F32)
                full[m][l, k, other_y] = both.astype(BF)
                sum_y(l, m, k).start()

            each(nz, one)

    def sum_second(l, m):
        @pl.when(core == l)
        def _():
            sum_core(l, m, 1).wait_recv()

            def total(k):
                at = turn(k)
                sum_y(l, m, at).wait_recv()
                both = full[m][l, at, y].astype(F32) + summed[m][at, y].astype(F32)
                return both + from_y[m][at].astype(F32)

            def one(k):
                full[m][l, turn(k), y] = total(k).astype(BF)
                far = is_far(k)
                held = jnp.logical_and(middle, k == nz // 2)

                @pl.when(far)
                def _():
                    sum_near(l, m, k).start()

                @pl.when(jnp.logical_not(jnp.logical_or(far, held)))
                def _():
                    sum_z(l, m, k).start()

            offsets(one)
            result[m][...] = total(0)

    def sum_relay(l, m):
        @pl.when(jnp.logical_and(core == l, middle))
        def _():
            k = nz // 2
            sum_near(l, m, k).wait_recv()
            both = full[m][l, turn(k), y].astype(F32) + from_z[m][nz - 1].astype(F32)
            full[m][l, turn(k), y] = both.astype(BF)
            sum_z(l, m, k).start()

    def sum_last(l, m):
        @pl.when(core == l)
        def _():
            def one(k):
                @pl.when(jnp.logical_not(is_late(k)))
                def _():
                    sum_z(l, m, k).wait_recv()
                    result[m][...] += from_z[m][k - 1].astype(F32)

            offsets(one)

    def sum_drain(l, m):
        @pl.when(core != l)
        def _():
            sum_core(l, m, 0).wait_send()
            sum_core(l, m, 1).wait_send()

        @pl.when(core == l)
        def _():
            each(nz, lambda k: sum_y(l, m, k).wait_send())
            offsets(lambda k: sum_z(l, m, k).wait_send())


    def vec_core(l):
        return remote(ng.at[l], rn, gc_s.at[PIECES, 0], gc_r.at[PIECES, 0], to_core)

    def vec_y(l):
        return remote(ng.at[2], yn, gy_s.at[PIECES, 0], gy_r.at[PIECES, 0], to_y)

    def vec_z(l, k):
        return remote(
            ng.at[3], vn.at[k - 1], gz_s.at[PIECES, k - 1], gz_r.at[PIECES, k - 1], to_z(k)
        )

    def vec_start(l):
        @pl.when(core != l)
        def _():
            vec_core(l).start()

    def vec_first(l):
        @pl.when(core == l)
        def _():
            vec_core(l).wait_recv()
            ng[2] = ng[l] + rn[...]
            vec_y(l).start()

    def vec_second(l):
        @pl.when(core == l)
        def _():
            vec_y(l).wait_recv()
            ng[3] = ng[2] + yn[...]
            for k in range(1, nz):
                vec_z(l, k).start()

    def vec_last(l):
        @pl.when(core == l)
        def _():
            total = ng[3]
            for k in range(1, nz):
                vec_z(l, k).wait_recv()
                total = total + vn[k - 1]
            on[...] = total

    def vec_drain(l):
        @pl.when(core != l)
        def _():
            vec_core(l).wait_send()

        @pl.when(core == l)
        def _():
            vec_y(l).wait_send()
            for k in range(1, nz):
                vec_z(l, k).wait_send()


    def exchange(i, c):
        return remote(xs.at[c], xr.at[i % 2, c], xs_sem.at[c], xr_sem.at[i % 2, c], to_x)

    def send(i, c):
        exchange(i, c).start()

    def arrive(i, c):
        exchange(i, c).wait()

    def both(i, c, r):
        rows = pl.ds(r * SUB, SUB)
        return xs[c, rows].astype(F32) + xr[i % 2, c, rows].astype(F32)

    def chunk_rows(c):
        return pl.ds(pl.multiple_of(c * CHUNK, CHUNK), CHUNK)

    def sub_rows(c, r):
        return pl.ds(pl.multiple_of(c * CHUNK + r * SUB, SUB), SUB)

    def columns(j, span):
        return pl.ds(pl.multiple_of(j * span, LANES), span)


    def out_copy(l, which, src, dst):
        def away():
            return remote(src, dst.at[core], out_send.at[which], out_recv.at[which], to_core)

        def here():
            return pltpu.make_async_copy(src, dst.at[core], local_sem.at[which])

        return here, away

    def out_start(l, which, src, dst):
        here, away = out_copy(l, which, src, dst)

        @pl.when(core == l)
        def _():
            here().start()

        @pl.when(core != l)
        def _():
            away().start()

    def out_wait(l, which, src, dst):
        here, away = out_copy(l, which, src, dst)

        @pl.when(core == l)
        def _():
            here().wait()
            remote(
                src, dst.at[1 - core], out_send.at[which], out_recv.at[which], to_core
            ).wait_recv()

        @pl.when(core != l)
        def _():
            away().wait_send()


    def project(l, c):
        rows = chunk_rows(c)
        for m, span in ((QK, slice(0, 2 * local)), (V, slice(2 * local, 3 * local))):
            packed[l, rows, span] = dot(zin[l, rows], flat_rows(full[m][l])).astype(BF)

    low_lane = lax.broadcasted_iota(jnp.int32, (1, LANES), 1) < LANES // 2

    def both_heads(value):
        none = jnp.zeros_like(value)
        return jnp.concatenate(
            [jnp.where(low_lane, value, none), jnp.where(low_lane, none, value)], 0
        )

    def one_head(value):
        half = value.shape[0] // 2
        return jnp.where(low_lane, value[:half], value[half:])

    def head_columns(j):
        return tuple(
            slice(part * local + j * LANES, part * local + (j + 1) * LANES)
            for part in range(3)
        )

    def attend(l, c):
        rows = slice(c * CHUNK, (c + 1) * CHUNK)
        keys = jnp.concatenate([keys_ref[...]] * (2 * CHUNK // LANES), 1)
        groups = jnp.concatenate([groups_ref[l : l + 1, rows]] * 2, 1)
        allowed = keys == groups
        for j in range(local // LANES):
            q_cols, k_cols, v_cols = head_columns(j)
            query = both_heads(packed[l, rows, q_cols] * scale)
            scores = jnp.where(allowed, dot_nt(packed[l, :, k_cols], query), -1e9)
            expo = jnp.exp(scores - jnp.max(scores, 0, keepdims=True))
            low = (expo * (1.0 / jnp.sum(expo, 0, keepdims=True))).astype(BF)
            prob[l, 2 * j, :, rows] = low[:, :CHUNK]
            prob[l, 2 * j + 1, :, rows] = low[:, CHUNK:]
            mixed[l, rows, q_cols] = one_head(dot_tn(low, packed[l, :, v_cols])).astype(BF)

    def send_product(i, l, c, *pairs):
        total = 0.0
        for left, m in pairs:
            total = total + dot_nt(left(), flat_rows(full[m][l]))
        xs[c] = total.astype(BF)
        send(i, c)

    def attend_out(i, l, c):
        send_product(i, l, c, (lambda: mixed[l, chunk_rows(c)], O))

    def gather_norms(l):
        norms[l] = jnp.sum(flat_rows(full[PIECES][l]).reshape(nz * ny, 8, width), 0)

    def norm_of(l, which):
        return norms[l, which : which + 1], norms[l, 2 + which : 3 + which]

    def normalize(value):
        center = value - jnp.mean(value, -1, keepdims=True)
        inverse = lax.rsqrt(jnp.mean(center * center, -1, keepdims=True) + eps)
        return center * inverse, inverse

    def expand(i, l, c):
        rows = chunk_rows(c)
        arrive(i, c)
        gain, shift = norm_of(l, 0)

        def one(r):
            sub = sub_rows(c, r)
            normed, inverse = normalize(zin[l, sub].astype(F32) + both(i, c, r))
            norm1[l, sub] = normed
            roots[sub, l : l + 1] = inverse
            hid[l, sub] = (normed * gain + shift).astype(BF)

        each(CHUNK // SUB, one)

        for m in (UA, UB):
            for part in range(units // 2 // TILE):
                cols = slice(part * TILE, (part + 1) * TILE)
                pre = dot(hid[l, rows], flat_rows(full[m][l, :, :, :, cols]))
                lower = 0.5 + 0.5 * lax.erf(pre * 0.7071067811865476)
                density = jnp.exp(-0.5 * pre * pre) * 0.3989422804014327
                start = (m - UA) * units // 2 + part * TILE
                act[l, rows, start : start + TILE] = (pre * lower).astype(BF)
                slope[l, rows, start : start + TILE] = (lower + pre * density).astype(BF)

    def halves(ref, l, rows):
        low, high = slice(0, units // 2), slice(units // 2, units)
        return (lambda: ref[l, rows, low]), (lambda: ref[l, rows, high])

    def contract(i, l, c):
        low, high = halves(act, l, chunk_rows(c))
        send_product(i, l, c, (low, DA), (high, DB))

    def second_norm(i, l, c, r):
        sub = sub_rows(c, r)
        gain, shift = norm_of(l, 0)
        hidden = norm1[l, sub] * gain + shift
        return normalize(hidden + both(i, c, r))

    def norm_back(grad, normed, inverse, gain):
        scaled = grad * gain
        inner = (
            scaled
            - jnp.mean(scaled, -1, keepdims=True)
            - normed * jnp.mean(scaled * normed, -1, keepdims=True)
        )
        return inner * inverse

    def count(l, which, grad, normed):
        ng[l, which : which + 1] += jnp.sum(grad * normed, 0, keepdims=True)
        ng[l, 2 + which : 3 + which] += jnp.sum(grad, 0, keepdims=True)

    def top_back(l, c, r, grad, normed, inverse):
        sub = sub_rows(c, r)
        count(l, 1, grad, normed)
        back = norm_back(grad, normed, inverse, norm_of(l, 1)[0])
        gsum[sub] = back
        gtok[sub] = back.astype(BF)

    def expand_back(i, l, c):
        rows = chunk_rows(c)
        for m in (DA, DB):
            cols = slice((m - DA) * units // 2, (m - DA + 1) * units // 2)
            grad = dot(gtok[rows], flat_rows(full[m][l]))
            slope[l, rows, cols] = (grad * slope[l, rows, cols].astype(F32)).astype(BF)

        low, high = halves(slope, l, rows)
        send_product(i, l, c, (low, UA), (high, UB))

    def weight_grad(l, m, source, right, start=0):
        gather_drain(l, m)
        grad = dot_tn(source[...], right[l, :, start : start + full[m].shape[-1]])
        full[m][l] = grad.astype(BF).reshape(full[m].shape[1:])
        sum_start(l, m)

    def attend_back(l):
        for j in range(local // LANES):
            q_cols, k_cols, v_cols = head_columns(j)
            grad = both_heads(gmix[:, q_cols])
            low = jnp.concatenate([prob[l, 2 * j], prob[l, 2 * j + 1]], 1)
            wide = low.astype(F32)
            product = wide * dot_nt(packed[l, :, v_cols], grad)
            total = jnp.sum(product, 0, keepdims=True)
            back = (product - wide * total).astype(BF)
            packed[l, :, v_cols] = dot(low, grad).astype(BF)
            g_key = dot(back, both_heads(packed[l, :, q_cols]))
            g_query = one_head(dot_tn(back, packed[l, :, k_cols]))
            packed[l, :, q_cols] = (g_query * scale).astype(BF)
            packed[l, :, k_cols] = (g_key * scale).astype(BF)

    def middle_back(i, l, c):
        rows = chunk_rows(c)
        arrive(i, c)

        def one(r):
            sub = sub_rows(c, r)
            grad = gsum[sub] + both(i, c, r)
            normed = norm1[l, sub]
            count(l, 0, grad, normed)
            back = norm_back(grad, normed, roots[sub, l : l + 1], norm_of(l, 0)[0])
            gsum[sub] = back
            gtok[sub] = back.astype(BF)

        each(CHUNK // SUB, one)
        gmix[rows] = dot(gtok[rows], flat_rows(full[O][l])).astype(BF)

    def project_back(i, l, c):
        rows = chunk_rows(c)
        send_product(
            i,
            l,
            c,
            (lambda: packed[l, rows, 0 : 2 * local], QK),
            (lambda: packed[l, rows, 2 * local : 3 * local], V),
        )


    barrier = pltpu.get_barrier_semaphore()
    peers = [to_x, to_core, to_y] + [to_z(k) for k in range(1, nz)]
    for peer in peers:
        pl.semaphore_signal(barrier, inc=1, device_id=peer, device_id_type=MESH)
    first_rows = pltpu.make_async_copy(x_ref.at[core], zin.at[0], local_sem.at[4])
    top_rows = pltpu.make_async_copy(go_ref.at[core], gtop, local_sem.at[5])
    first_rows.start()
    top_rows.start()
    ng[...] = jnp.zeros_like(ng)
    pl.semaphore_wait(barrier, len(peers))

    gather_own(0, QK, V, N, O, UA, UB, DA, DB)
    gather_far(0, QK, V, N, O)
    gather_cross(0, V, N, O)
    gather_far(0, UA)
    gather_pass(0, QK, V, N, O)
    gather_far(0, UB)
    gather_late(0, QK, V, N, O)
    gather_end(0, QK, V, N)
    gather_own(1, QK, V, N, O, UA, UB, DA, DB)
    first_rows.wait()
    gather_norms(0)
    each(chunks, lambda c: project(0, c))
    attend(0, 0)
    gather_pass(0, UA)
    gather_far(0, DA)
    gather_end(0, O)
    attend_out(0, 0, 0)
    attend(0, 1)
    attend_out(0, 0, 1)
    gather_late(0, UA)
    gather_pass(0, UB)
    gather_far(0, DB)
    gather_end(0, UA)
    gather_late(0, UB)
    gather_pass(0, DA)
    gather_end(0, UB)
    expand(0, 0, 0)
    gather_late(0, DA)
    gather_pass(0, DB)
    gather_far(1, QK, V, N, O)
    gather_cross(1, V, N, O)
    expand(0, 0, 1)
    gather_late(0, DB)
    gather_end(0, DA, DB)
    gather_far(1, UA)
    each(chunks, lambda c: contract(1, 0, c))

    def into_second(c):
        arrive(1, c)
        gain, shift = norm_of(0, 1)

        def one(r):
            sub = sub_rows(c, r)
            normed, inverse = second_norm(1, 0, c, r)
            norm2[sub] = normed.astype(BF)
            roots[sub, 2:3] = inverse
            zin[1, sub] = (normed * gain + shift).astype(BF)

        each(CHUNK // SUB, one)

    gather_pass(1, QK, V, N, O)
    gather_far(1, UB)
    into_second(0)
    gather_late(1, QK, V, N, O)
    gather_pass(1, UA)
    gather_far(1, DA)
    into_second(1)
    gather_late(1, UA)
    out_start(0, 0, zin.at[1], lo_ref)
    gather_end(1, QK, V, N)
    gather_norms(1)
    each(chunks, lambda c: project(1, c))
    gather_pass(1, UB)
    gather_far(1, DB)
    attend(1, 0)
    gather_end(1, O)
    attend_out(2, 1, 0)
    gather_late(1, UB)
    gather_pass(1, DA)
    attend(1, 1)
    attend_out(2, 1, 1)
    gather_late(1, DA)
    gather_pass(1, DB)
    gather_end(1, UA, UB)
    expand(2, 1, 0)
    gather_late(1, DB)
    gather_end(1, DA, DB)
    contract(3, 1, 0)
    expand(2, 1, 1)
    contract(3, 1, 1)
    top_rows.wait()

    def over_top(c):
        arrive(3, c)
        gain, shift = norm_of(1, 1)

        def one(r):
            sub = sub_rows(c, r)
            normed, inverse = second_norm(3, 1, c, r)
            top_back(1, c, r, gtop[sub].astype(F32), normed, inverse)
            gtop[sub] = (normed * gain + shift).astype(BF)

        each(CHUNK // SUB, one)

    over_top(0)
    expand_back(4, 1, 0)
    over_top(1)
    expand_back(4, 1, 1)
    out_start(1, 1, gtop, lo_ref)
    weight_grad(1, DA, gtok, act)
    weight_grad(1, DB, gtok, act, units // 2)
    weight_grad(1, UA, hid.at[1], slope)
    weight_grad(1, UB, hid.at[1], slope, units // 2)
    middle_back(4, 1, 0)
    sum_first(1, DA)
    middle_back(4, 1, 1)
    sum_first(1, DB)
    attend_back(1)
    sum_second(1, DA)
    each(chunks, lambda c: project_back(5, 1, c))
    sum_first(1, UA)
    weight_grad(1, O, gtok, mixed)
    weight_grad(1, QK, zin.at[1], packed)
    weight_grad(1, V, zin.at[1], packed, 2 * local)
    vec_start(1)
    sum_relay(1, DA)
    sum_second(1, DB)
    sum_first(1, UB)
    sum_first(1, O)

    def under(c):
        arrive(5, c)

        def one(r):
            sub = sub_rows(c, r)
            low = (gsum[sub] + both(5, c, r)).astype(BF)
            gin[sub] = low
            top_back(0, c, r, low.astype(F32), norm2[sub].astype(F32), roots[sub, 2:3])

        each(CHUNK // SUB, one)
        expand_back(6, 0, c)

    sum_relay(1, DB)
    under(0)
    sum_second(1, UA)
    sum_first(1, QK)
    sum_first(1, V)
    under(1)
    out_start(1, 3, gin, ig_ref)
    weight_grad(0, DA, gtok, act)
    weight_grad(0, DB, gtok, act, units // 2)
    sum_relay(1, UA)
    sum_second(1, UB)
    weight_grad(0, UA, hid.at[0], slope)
    weight_grad(0, UB, hid.at[0], slope, units // 2)
    vec_first(1)
    sum_first(0, DA)
    middle_back(6, 0, 0)
    sum_first(0, DB)
    sum_relay(1, UB)
    sum_second(1, O)
    middle_back(6, 0, 1)
    attend_back(0)
    sum_second(0, DA)
    sum_second(1, QK)
    sum_relay(1, O)
    each(chunks, lambda c: project_back(7, 0, c))
    sum_first(0, UA)
    weight_grad(0, O, gtok, mixed)
    weight_grad(0, QK, zin.at[0], packed)
    weight_grad(0, V, zin.at[0], packed, 2 * local)
    vec_start(0)
    sum_relay(0, DA)
    sum_second(0, DB)
    sum_first(0, UB)
    sum_relay(1, QK)
    sum_second(1, V)
    vec_second(1)
    sum_first(0, O)
    sum_relay(0, DB)
    sum_second(0, UA)
    sum_first(0, QK)
    sum_first(0, V)
    vec_first(0)
    sum_relay(1, V)

    def bottom(c):
        arrive(7, c)

        def one(r):
            sub = sub_rows(c, r)
            gtop[sub] = (gsum[sub] + both(7, c, r)).astype(BF)

        each(CHUNK // SUB, one)

    out_wait(1, 1, gtop, lo_ref)
    bottom(0)
    sum_relay(0, UA)
    sum_second(0, UB)
    sum_second(0, O)
    bottom(1)
    out_start(0, 2, gtop, ig_ref)
    sum_relay(0, UB)
    sum_relay(0, O)
    sum_second(0, QK)
    sum_second(0, V)
    vec_second(0)
    sum_relay(0, QK)
    sum_relay(0, V)
    for l in (1, 0):
        for m in (DA, DB, UA, UB, O, QK, V):
            sum_last(l, m)
        vec_last(l)
    for l in range(2):
        for m in range(PIECES):
            sum_drain(l, m)
        vec_drain(l)
        gather_drain(l, N)
    out_wait(0, 0, zin.at[1], lo_ref)
    out_wait(0, 2, gtop, ig_ref)
    out_wait(1, 3, gin, ig_ref)


def fused(sizes, x, grad, keys, groups, shards_in):
    nz, ny, length, width, local, units, eps, scale = sizes
    block = width // (nz * ny)
    chunks = length // CHUNK
    spans = (2 * local, local, local) + (units // 2,) * 4
    outs = (3 * local, local, units, units)
    dma = pltpu.SemaphoreType.DMA
    vmem = pltpu.VMEM
    scratch = [vmem((2, nz, ny, block, span), BF) for span in spans]
    scratch += [vmem((2, nz, ny, 8, width), F32)]
    scratch += [vmem((nz, ny, block, span), BF) for span in spans]
    scratch += [vmem((nz, block, span), BF) for span in spans]
    scratch += [vmem((nz, block, span), BF) for span in spans]
    scratch += [
        vmem((8, width), F32),
        vmem((8, width), F32),
        vmem((nz - 1, 8, width), F32),
        vmem((4, 8, width), F32),
        vmem((2, length, width), BF),
        vmem((2, length, 3 * local), BF),
        vmem((2, local // HEAD, length, length), BF),
        vmem((2, length, local), BF),
        vmem((2, length, width), F32),
        vmem((2, length, width), BF),
        vmem((2, length, units), BF),
        vmem((2, length, units), BF),
        vmem((length, width), BF),
        vmem((length, 4), F32),
        vmem((length, width), F32),
        vmem((length, width), BF),
        vmem((length, local), BF),
        vmem((length, width), BF),
        vmem((length, width), BF),
        vmem((2, 8, width), F32),
        vmem((chunks, CHUNK, width), BF),
        vmem((2, chunks, CHUNK, width), BF),
        dma((6,)),
        dma((4,)),
        dma((4,)),
        dma((chunks,)),
        dma((2, chunks)),
        dma((PIECES + 1, 2, nz)),
        dma((PIECES + 1, 2, nz)),
        dma((PIECES + 1, nz)),
        dma((PIECES + 1, nz)),
        dma((PIECES + 1, 2 * nz)),
        dma((PIECES + 1, 2 * nz)),
        dma((PIECES + 1, 2)),
        dma((PIECES + 1, 2)),
        dma((PIECES + 1, nz)),
        dma((PIECES + 1, nz)),
        dma((PIECES + 1, nz - 1)),
        dma((PIECES + 1, nz)),
    ]
    anywhere = pl.BlockSpec(memory_space=pl.ANY)
    inside = pl.BlockSpec(memory_space=pltpu.VMEM)
    return pl.pallas_call(
        functools.partial(kernel, sizes),
        out_shape=[jax.ShapeDtypeStruct((2, length, width), BF)] * 2
        + [jax.ShapeDtypeStruct((block, span), F32) for span in outs]
        + [jax.ShapeDtypeStruct((8, width), F32)],
        in_specs=[anywhere] * 2 + [inside] * 7,
        out_specs=[anywhere] * 2 + [inside] * 5,
        scratch_shapes=scratch,
        compiler_params=pltpu.CompilerParams(
            collective_id=0, has_side_effects=True, vmem_limit_bytes=63 << 20
        ),
    )(x, grad, keys, groups, *shards_in)


def kernel_shards(
    inputs, segments, partner, grad_output, w_qkv, w_out, w_up, w_down, norm_gain, norm_shift
):
    core = lax.axis_index("section")
    place = lax.axis_index("dp")
    parts = lax.axis_size("dp")
    length, width = inputs.shape[1:]
    local, units = w_out.shape[1], w_up.shape[2]
    block = width // parts
    sizes = (parts // 2, 2, length, width, local, units, norm_eps, score_scale)
    own = lax.dynamic_index_in_dim(segments, core, 0, False)
    mapped = partner_of(own, lax.dynamic_index_in_dim(partner, core, 0, False))
    keys = jnp.broadcast_to(own[:, None], (length, LANES))
    groups = jnp.stack([own, mapped])
    vectors = jnp.concatenate([norm_gain[0], norm_shift[0]]).astype(F32)
    spread = lax.dynamic_update_slice(
        jnp.zeros((8, width), F32), vectors, (0, place * block)
    )
    shards_in = (
        w_qkv[0].reshape(block, 3 * local),
        w_out[0].T,
        w_up[0],
        w_down[0].T,
        spread,
    )
    outs = fused(sizes, inputs, grad_output, keys, groups, shards_in)
    layer_outputs, input_grads, g_qkv, g_out, g_up, g_down, g_norm = outs
    own_norm = lax.dynamic_slice(g_norm, (0, place * block), (8, block))
    return (
        layer_outputs[None],
        input_grads[None],
        g_qkv.reshape(1, block, 3, local),
        g_out.T[None],
        g_up[None],
        g_down.T[None],
        own_norm[None, 0:2],
        own_norm[None, 2:4],
    )


def solution(mesh):
    placed = (
        P("dp", None, None),
        P("dp", None),
        P("dp", None),
        P("dp", None, None),
        P("section", "dp", None, "tensor"),
        P("section", "tensor", "dp"),
        P("section", "dp", "tensor"),
        P("section", "tensor", "dp"),
        P("section", None, "dp"),
        P("section", None, "dp"),
    )
    block = WIDTH // mesh.shape["dp"]
    whole_tiles = block * mesh.shape["dp"] == WIDTH and block % 16 == 0
    return jax.shard_map(
        kernel_shards if whole_tiles else shards,
        mesh=mesh,
        in_specs=placed,
        out_specs=(
            P("section", "dp", None, None),
            P("section", "dp", None, None),
            P("section", "dp", None, "tensor"),
            P("section", "tensor", "dp"),
            P("section", "dp", "tensor"),
            P("section", "tensor", "dp"),
            P("section", None, "dp"),
            P("section", None, "dp"),
        ),
        check_vma=False,
    )
```

```python
import functools

import jax
import jax.numpy as jnp
from jax import lax
from jax.experimental import pallas as pl
from jax.experimental.pallas import tpu as pltpu
from jax.sharding import PartitionSpec as P

HEAD = 64
WIDTH = 768


norm_eps = 1e-06
score_scale = 0.125
masked_value = -1000000000.0


def partner_of(segment_ids, partner):
    table = jnp.arange(partner.shape[-1], dtype=jnp.int32)
    hits = segment_ids[..., None] == table
    return jnp.sum(jnp.where(hits, partner[None, :], 0), -1)


def layer_norm(values, gain, shift):
    center = values - jnp.mean(values, -1, keepdims=True)
    inverse = lax.rsqrt(jnp.mean(center * center, -1, keepdims=True) + norm_eps)
    normed = center * inverse
    return (normed * gain + shift, normed, inverse)


def norm_back(grad, normed, inverse, gain):
    scaled = grad * gain
    inner = (
        scaled
        - jnp.mean(scaled, -1, keepdims=True)
        - normed * jnp.mean(scaled * normed, -1, keepdims=True)
    )
    return inner * inverse


def gelu_slope(values):
    lower = 0.5 * (1.0 + lax.erf(values * 0.7071067811865476))
    density = jnp.exp(-0.5 * values * values) * 0.3989422804014327
    return lower + values * density


def swapped(value, axis):
    size = lax.axis_size(axis)
    return lax.ppermute(value, axis, [(i, size - 1 - i) for i in range(size)])


def tensor_sum(partial_value):
    low = partial_value.astype(jnp.bfloat16)
    return low.astype(jnp.float32) + swapped(low, "tensor").astype(jnp.float32)


def masked_scores(query, key, query_groups, key_groups):
    scores = (
        jnp.einsum("qhd,khd->hqk", query, key, preferred_element_type=jnp.float32) * score_scale
    )
    allowed = query_groups[:, None] == key_groups[None, :]
    return jnp.where(allowed[None], scores, masked_value)


def attend(query, key, value, query_groups, key_groups):
    scores = masked_scores(query, key, query_groups, key_groups)
    top = jnp.max(scores, -1, keepdims=True)
    expo = jnp.exp(scores - top)
    total = jnp.sum(expo, -1, keepdims=True)
    probs = (expo / total).astype(jnp.bfloat16)
    mixed = jnp.einsum("hqk,khd->qhd", probs, value, preferred_element_type=jnp.float32)
    return (mixed.astype(jnp.bfloat16), (top + jnp.log(total))[..., 0])


def attend_back(query, key, value, query_groups, key_groups, spread, grad_mixed):
    scores = masked_scores(query, key, query_groups, key_groups)
    probs = jnp.exp(scores - spread[..., None])
    probs_low = probs.astype(jnp.bfloat16)
    grad_probs = jnp.einsum("qhd,khd->hqk", grad_mixed, value, preferred_element_type=jnp.float32)
    grad_value = jnp.einsum(
        "hqk,qhd->khd", probs_low, grad_mixed, preferred_element_type=jnp.float32
    )
    row_dot = jnp.sum(probs * grad_probs, -1, keepdims=True)
    grad_scores = (probs * (grad_probs - row_dot)).astype(jnp.bfloat16)
    grad_query = (
        jnp.einsum("hqk,khd->qhd", grad_scores, key, preferred_element_type=jnp.float32)
        * score_scale
    )
    grad_key = (
        jnp.einsum("hqk,qhd->khd", grad_scores, query, preferred_element_type=jnp.float32)
        * score_scale
    )
    return jnp.stack(
        [
            grad_query.astype(jnp.bfloat16),
            grad_key.astype(jnp.bfloat16),
            grad_value.astype(jnp.bfloat16),
        ],
        1,
    )


def layer_forward(flat, weights, query_groups, key_groups):
    w_qkv, w_out, w_up, w_down, gains, shifts = weights
    length = flat.shape[0]
    local = w_qkv.shape[2]
    packed = jnp.einsum("nd,dcm->ncm", flat, w_qkv, preferred_element_type=jnp.float32).astype(
        jnp.bfloat16
    )
    heads = packed.reshape(length, 3, local // HEAD, HEAD)
    mixed, spread = attend(heads[:, 0], heads[:, 1], heads[:, 2], query_groups, key_groups)
    mixed_flat = mixed.reshape(length, local)
    attn_out = tensor_sum(jnp.dot(mixed_flat, w_out, preferred_element_type=jnp.float32))
    hidden, normed_first, inverse_first = layer_norm(
        flat.astype(jnp.float32) + attn_out, gains[0], shifts[0]
    )
    hidden_low = hidden.astype(jnp.bfloat16)
    pre = jnp.dot(hidden_low, w_up, preferred_element_type=jnp.float32)
    act = jax.nn.gelu(pre, approximate=False).astype(jnp.bfloat16)
    ffn_out = tensor_sum(jnp.dot(act, w_down, preferred_element_type=jnp.float32))
    result, normed_second, inverse_second = layer_norm(hidden + ffn_out, gains[1], shifts[1])
    kept = (
        flat,
        heads,
        spread,
        mixed_flat,
        normed_first,
        inverse_first,
        hidden_low,
        pre,
        act,
        normed_second,
        inverse_second,
    )
    return (result.astype(jnp.bfloat16), kept)


def layer_backward(grad_result, kept, weights, query_groups, key_groups):
    w_qkv, w_out, w_up, w_down, gains, shifts = weights
    (
        flat,
        heads,
        spread,
        mixed_flat,
        normed_first,
        inverse_first,
        hidden_low,
        pre,
        act,
        normed_second,
        inverse_second,
    ) = kept
    length = flat.shape[0]
    local = w_qkv.shape[2]
    gain_second = jnp.sum(grad_result * normed_second, 0)
    shift_second = jnp.sum(grad_result, 0)
    grad_sum2 = norm_back(grad_result, normed_second, inverse_second, gains[1])
    grad_ffn = grad_sum2.astype(jnp.bfloat16)
    grad_down = jnp.einsum("nf,nd->fd", act, grad_ffn, preferred_element_type=jnp.float32)
    grad_act = jnp.einsum("nd,fd->nf", grad_ffn, w_down, preferred_element_type=jnp.float32)
    grad_pre = (grad_act * gelu_slope(pre)).astype(jnp.bfloat16)
    grad_up = jnp.einsum("nd,nf->df", hidden_low, grad_pre, preferred_element_type=jnp.float32)
    grad_hidden = grad_sum2 + tensor_sum(
        jnp.einsum("nf,df->nd", grad_pre, w_up, preferred_element_type=jnp.float32)
    )
    gain_first = jnp.sum(grad_hidden * normed_first, 0)
    shift_first = jnp.sum(grad_hidden, 0)
    grad_resid = norm_back(grad_hidden, normed_first, inverse_first, gains[0])
    grad_attn = grad_resid.astype(jnp.bfloat16)
    grad_out = jnp.einsum("nm,nd->md", mixed_flat, grad_attn, preferred_element_type=jnp.float32)
    grad_mixed = jnp.einsum(
        "nd,md->nm", grad_attn, w_out, preferred_element_type=jnp.float32
    ).astype(jnp.bfloat16)
    grad_mixed = grad_mixed.reshape(length, local // HEAD, HEAD)
    grad_heads = attend_back(
        heads[:, 0], heads[:, 1], heads[:, 2], query_groups, key_groups, spread, grad_mixed
    )
    grad_packed = grad_heads.reshape(length, 3, local)
    grad_qkv = jnp.einsum("nd,ncm->dcm", flat, grad_packed, preferred_element_type=jnp.float32)
    grad_input = grad_resid + tensor_sum(
        jnp.einsum("ncm,dcm->nd", grad_packed, w_qkv, preferred_element_type=jnp.float32)
    )
    grads = (
        grad_qkv.astype(jnp.bfloat16),
        grad_out.astype(jnp.bfloat16),
        grad_up.astype(jnp.bfloat16),
        grad_down.astype(jnp.bfloat16),
        jnp.stack([gain_first, gain_second]),
        jnp.stack([shift_first, shift_second]),
    )
    return (grads, grad_input.astype(jnp.bfloat16))


def shards(
    inputs, segments, partner, grad_output, w_qkv, w_out, w_up, w_down, norm_gain, norm_shift
):
    core = lax.axis_index("section")
    rows = inputs.shape[0] // lax.axis_size("section")

    def per_row(row):
        key_groups = lax.dynamic_index_in_dim(segments, row, 0, False)
        mapped = partner_of(key_groups, lax.dynamic_index_in_dim(partner, row, 0, False))
        flat = lax.dynamic_index_in_dim(inputs, row, 0, False)
        first, kept_first = layer_forward(flat, layers[0], key_groups, key_groups)
        second, kept_second = layer_forward(first, layers[1], mapped, key_groups)
        grad_top = lax.dynamic_index_in_dim(grad_output, row, 0, False).astype(jnp.float32)
        grads_second, grad_mid = layer_backward(
            grad_top, kept_second, layers[1], mapped, key_groups
        )
        grads_first, grad_low = layer_backward(
            grad_mid.astype(jnp.float32), kept_first, layers[0], key_groups, key_groups
        )
        return (first, second, grad_low, grad_mid, grads_first, grads_second)

    def gathered(shard, axis):
        own = lax.all_gather(shard[0], "dp", axis=axis, tiled=True)
        other = swapped(own, "section")
        return (jnp.where(core == 0, own, other), jnp.where(core == 0, other, own))

    pairs = [
        gathered(w_qkv, 0),
        gathered(w_out, 1),
        gathered(w_up, 0),
        gathered(w_down, 1),
        gathered(norm_gain, 1),
        gathered(norm_shift, 1),
    ]
    layers = [
        [pair[layer].astype(jnp.float32) if place > 3 else pair[layer] for place, pair in enumerate(pairs)]
        for layer in range(2)
    ]
    done = [per_row(core * rows + step) for step in range(rows)]

    def summed(first, second, axis):
        mine = jnp.where(core == 0, first, second)
        away = jnp.where(core == 0, second, first)
        both = mine.astype(jnp.float32) + swapped(away, "section").astype(jnp.float32)
        return lax.psum_scatter(both.astype(first.dtype), "dp", scatter_dimension=axis, tiled=True).astype(jnp.float32)

    def total(layer, place):
        value = done[0][4 + layer][place]
        for item in done[1:]:
            value = (value.astype(jnp.float32) + item[4 + layer][place].astype(jnp.float32)).astype(value.dtype)
        return value

    axes = (0, 1, 0, 1, 1, 1)
    sums = [summed(total(0, place), total(1, place), axis) for place, axis in enumerate(axes)]

    def regrouped(first, second):
        mine = jnp.where(core == 0, first, second)
        other = swapped(jnp.where(core == 0, second, first), "section")
        return jnp.where(
            core == 0, jnp.concatenate([mine, other]), jnp.concatenate([other, mine])
        )

    layer_outputs = regrouped(
        jnp.stack([item[0] for item in done]), jnp.stack([item[1] for item in done])
    )
    input_grads = regrouped(
        jnp.stack([item[2] for item in done]), jnp.stack([item[3] for item in done])
    )
    return (layer_outputs[None], input_grads[None]) + tuple(value[None] for value in sums)


MESH = pl.DeviceIdType.MESH
BF = jnp.bfloat16
F32 = jnp.float32
CHUNK = 256
SUB = 128
TILE = 256
LANES = 128
QK, V, O, UA, UB, DA, DB, N = range(8)
PIECES = N
Y_FIRST = (V, O, N)
NT = (((1,), (1,)), ((), ()))
TN = (((0,), (0,)), ((), ()))


def dot(left, right):
    return jnp.dot(left, right, preferred_element_type=F32)


def dot_nt(left, right):
    return lax.dot_general(left, right, NT, preferred_element_type=F32)


def dot_tn(left, right):
    return lax.dot_general(left, right, TN, preferred_element_type=F32)


def flat_rows(value):
    return value.reshape(-1, value.shape[-1])


def kernel(
    sizes,
    partner_ref,
    gain_ref,
    shift_ref,
    x_ref,
    go_ref,
    segs_ref,
    sq,
    so,
    su,
    sd,
    lo_ref,
    ig_ref,
    oq,
    oo,
    ou,
    od,
    on,
    *refs,
):
    nz, ny, length, width, local, units, eps, scale = sizes
    block = width // (nz * ny)
    full, refs = refs[: PIECES + 1], refs[PIECES + 1 :]
    summed, refs = refs[:PIECES], refs[PIECES:]
    from_y, refs = refs[:PIECES], refs[PIECES:]
    from_z, refs = refs[:PIECES], refs[PIECES:]
    result, refs = refs[:PIECES], refs[PIECES:]
    (
        keys_ref,
        groups_ref,
        segs,
        out_norm,
        rn,
        yn,
        vn,
        ng,
        zin,
        packed,
        prob,
        mixed,
        norm1,
        hid,
        act,
        slope,
        norm2,
        roots,
        gsum,
        gtok,
        gmix,
        gtop,
        gin,
        norms,
        xs,
        xr,
        local_sem,
        own_sem,
        done_sem,
        out_send,
        out_recv,
        xs_sem,
        xr_sem,
        az_s,
        az_r,
        ay_s,
        ay_r,
        ac_s,
        ac_r,
        gc_s,
        gc_r,
        gy_s,
        gy_r,
        gz_s,
        gz_r,
    ) = refs
    chunks = length // CHUNK
    core = lax.axis_index("section")
    place = lax.axis_index("dp")
    side = lax.axis_index("tensor")
    z, y = place // ny, lax.rem(place, ny)
    other_y = 1 - y
    to_x = {"tensor": 1 - side}
    to_core = {"section": 1 - core}
    to_y = {"dp": z * ny + other_y}

    def turn(k):
        return lax.rem(z + k + nz, nz)

    def to_z(k):
        return {"dp": turn(k) * ny + y}

    half = units // 2
    shard = {
        QK: sq.at[0:2],
        V: sq.at[2],
        O: so,
        UA: su.at[:, 0:half],
        UB: su.at[:, half:units],
        DA: sd.at[:, 0:half],
        DB: sd.at[:, half:units],
    }
    target = {
        QK: oq.at[0:2],
        V: oq.at[2],
        UA: ou.at[:, 0:half],
        UB: ou.at[:, half:units],
        O: oo,
        DA: od.at[:, 0:half],
        DB: od.at[:, half:units],
    }

    def remote(src, dst, send, recv, target):
        return pltpu.make_async_remote_copy(
            src_ref=src,
            dst_ref=dst,
            send_sem=send,
            recv_sem=recv,
            device_id=target,
            device_id_type=MESH,
        )

    def each(count, body):
        lax.fori_loop(0, count, lambda i, none: (body(i), none)[1], 0)

    at_end = jnp.logical_or(z == 0, z == nz - 1)
    middle = jnp.logical_not(at_end)
    far_end = jnp.where(z < nz // 2, 0, nz - 1)
    far_origin = nz - 1 - far_end
    near_z = {"dp": jnp.where(z == 0, 1, nz - 2) * ny + y}
    end_z = {"dp": far_end * ny + y}

    def is_far(k):
        return jnp.logical_or(
            jnp.logical_and(z == 0, k == nz - 1), jnp.logical_and(z == nz - 1, k == 1)
        )

    def is_late(k):
        return jnp.logical_or(
            jnp.logical_and(z == 0, k == 1), jnp.logical_and(z == nz - 1, k == nz - 1)
        )

    def offsets(body):
        lax.fori_loop(1, nz, lambda k, none: (body(k), none)[1], 0)


    def column(c):
        return (y, other_y)[c]

    def lines(m):
        return (0, 1) if m in Y_FIRST else (0,)

    def gather_z(l, m, k, c, src=None):
        ref = full[m].at[l, z, column(c)]
        return remote(
            ref if src is None else src,
            ref,
            az_s.at[m, c, k - 1],
            az_r.at[m, c, k - 1],
            to_z(k),
        )

    def gather_relay(l, m, c):
        ref = full[m].at[l, far_origin, column(c)]
        slot = jnp.where(z == 1, 0, nz - 2)
        return remote(ref, ref, az_s.at[m, c, nz - 1], az_r.at[m, c, slot], end_z)

    def gather_y(l, m, k, src=None):
        ref = full[m].at[l, turn(-k), y]
        return remote(ref if src is None else src, ref, ay_s.at[m, k], ay_r.at[m, k], to_y)

    def gather_core(l, m, k, c, src=None):
        ref = full[m].at[l, turn(-k), column(c)]
        slot = k + c * nz
        return remote(
            ref if src is None else src, ref, ac_s.at[m, slot], ac_r.at[m, slot], to_core
        )

    def own_copy(l, m):
        return pltpu.make_async_copy(shard[m], full[m].at[l, z, y], own_sem.at[m])

    def gather_own(l, *mats):
        @pl.when(core == l)
        def _():
            for m in mats:
                if m in shard:
                    own_copy(l, m).start()
                gather_y(l, m, 0, shard.get(m)).start()
                gather_core(l, m, 0, 0, shard.get(m)).start()

    def gather_far(l, *mats):
        @pl.when(core == l)
        def _():
            for m in mats:

                def one(k):
                    @pl.when(jnp.logical_not(is_far(k)))
                    def _():
                        gather_z(l, m, k, 0, shard.get(m)).start()

                offsets(one)

    def gather_cross(l, *mats):
        @pl.when(core == l)
        def _():
            for m in mats:
                gather_y(l, m, 0).wait_recv()
                gather_core(l, m, 0, 1).start()

                def one(k):
                    @pl.when(jnp.logical_not(is_far(k)))
                    def _():
                        gather_z(l, m, k, 1).start()

                offsets(one)

    def gather_hand(l, m, k, c):
        gather_z(l, m, k, c).wait_recv()
        gather_core(l, m, k, c).start()
        if m not in Y_FIRST:
            gather_y(l, m, k).start()

    def gather_pass(l, *mats):
        @pl.when(core == l)
        def _():
            for m in mats:
                for c in lines(m):

                    def one(k):
                        @pl.when(jnp.logical_not(is_late(k)))
                        def _():
                            gather_hand(l, m, k, c)

                        @pl.when(jnp.logical_and(middle, k == nz // 2))
                        def _():
                            gather_relay(l, m, c).start()

                    offsets(one)

    def gather_late(l, *mats):
        @pl.when(jnp.logical_and(core == l, at_end))
        def _():
            for m in mats:
                for c in lines(m):
                    gather_hand(l, m, jnp.where(z == 0, 1, nz - 1), c)

    def gather_near(l, m):
        @pl.when(core != l)
        def _():
            each(nz, lambda k: gather_core(l, m, k, 0).wait_recv())

    def gather_end(l, *mats, near=True):
        @pl.when(core == l)
        def _():
            for m in mats:
                if m in shard:
                    own_copy(l, m).wait()
                if m not in Y_FIRST:

                    def one(k):
                        gather_y(l, m, k).wait_recv()
                        gather_core(l, m, k, 1).start()

                    each(nz, one)

        for m in mats:
            if near:
                gather_near(l, m)

        @pl.when(core != l)
        def _():
            for m in mats:
                each(nz, lambda k: gather_core(l, m, k, 1).wait_recv())

    def gather_drain(l, m):
        @pl.when(core == l)
        def _():
            for c in lines(m):

                def one(k):
                    @pl.when(jnp.logical_not(is_far(k)))
                    def _():
                        gather_z(l, m, k, c).wait_send()

                offsets(one)

                @pl.when(middle)
                def _():
                    gather_relay(l, m, c).wait_send()

            gather_y(l, m, 0).wait_send()
            if m not in Y_FIRST:
                offsets(lambda k: gather_y(l, m, k).wait_send())

            def core_sent(k):
                gather_core(l, m, k, 0).wait_send()
                gather_core(l, m, k, 1).wait_send()

            each(nz, core_sent)


    def sum_core(l, m, part):
        column = (other_y, y)[part]
        return remote(
            full[m].at[l, :, column],
            summed[m].at[:, column],
            gc_s.at[m, part],
            gc_r.at[m, part],
            to_core,
        )

    def sum_y(l, m, k):
        return remote(
            full[m].at[l, k, other_y], from_y[m].at[k], gy_s.at[m, k], gy_r.at[m, k], to_y
        )

    def sum_z(l, m, k):
        return remote(
            full[m].at[l, turn(k), y],
            from_z[m].at[k - 1],
            gz_s.at[m, k - 1],
            gz_r.at[m, k - 1],
            to_z(k),
        )

    def sum_near(l, m, k):
        return remote(
            full[m].at[l, turn(k), y],
            from_z[m].at[nz - 1],
            gz_s.at[m, k - 1],
            gz_r.at[m, nz - 1],
            near_z,
        )

    def sum_start(l, m):
        @pl.when(core != l)
        def _():
            sum_core(l, m, 0).start()
            sum_core(l, m, 1).start()

    def sum_first(l, m):
        @pl.when(core == l)
        def _():
            sum_core(l, m, 0).wait_recv()

            def one(k):
                both = full[m][l, k, other_y].astype(F32) + summed[m][k, other_y].astype(F32)
                full[m][l, k, other_y] = both.astype(BF)
                sum_y(l, m, k).start()

            each(nz, one)

    def sum_second(l, m):
        @pl.when(core == l)
        def _():
            sum_core(l, m, 1).wait_recv()

            def total(k):
                at = turn(k)
                sum_y(l, m, at).wait_recv()
                both = full[m][l, at, y].astype(F32) + summed[m][at, y].astype(F32)
                return both + from_y[m][at].astype(F32)

            def one(k):
                full[m][l, turn(k), y] = total(k).astype(BF)
                far = is_far(k)
                held = jnp.logical_and(middle, k == nz // 2)

                @pl.when(far)
                def _():
                    sum_near(l, m, k).start()

                @pl.when(jnp.logical_not(jnp.logical_or(far, held)))
                def _():
                    sum_z(l, m, k).start()

            offsets(one)
            result[m][...] = total(0)

    def sum_relay(l, m):
        @pl.when(jnp.logical_and(core == l, middle))
        def _():
            k = nz // 2
            sum_near(l, m, k).wait_recv()
            both = full[m][l, turn(k), y].astype(F32) + from_z[m][nz - 1].astype(F32)
            full[m][l, turn(k), y] = both.astype(BF)
            sum_z(l, m, k).start()

    def sum_last(l, m):
        @pl.when(core == l)
        def _():
            def one(k):
                @pl.when(jnp.logical_not(is_late(k)))
                def _():
                    sum_z(l, m, k).wait_recv()
                    result[m][...] += from_z[m][k - 1].astype(F32)

            offsets(one)
            result_out(m).start()

    def result_out(m):
        return pltpu.make_async_copy(result[m], target[m], done_sem.at[m])

    def sum_drain(l, m):
        @pl.when(core != l)
        def _():
            sum_core(l, m, 0).wait_send()
            sum_core(l, m, 1).wait_send()

        @pl.when(core == l)
        def _():
            each(nz, lambda k: sum_y(l, m, k).wait_send())
            offsets(lambda k: sum_z(l, m, k).wait_send())


    def vec_core(l):
        return remote(ng.at[l], rn, gc_s.at[PIECES, 0], gc_r.at[PIECES, 0], to_core)

    def vec_y(l):
        return remote(ng.at[2], yn, gy_s.at[PIECES, 0], gy_r.at[PIECES, 0], to_y)

    def vec_z(l, k):
        return remote(
            ng.at[3], vn.at[k - 1], gz_s.at[PIECES, k - 1], gz_r.at[PIECES, k - 1], to_z(k)
        )

    def vec_start(l):
        @pl.when(core != l)
        def _():
            vec_core(l).start()

    def vec_first(l):
        @pl.when(core == l)
        def _():
            vec_core(l).wait_recv()
            ng[2] = ng[l] + rn[...]
            vec_y(l).start()

    def vec_second(l):
        @pl.when(core == l)
        def _():
            vec_y(l).wait_recv()
            ng[3] = ng[2] + yn[...]
            for k in range(1, nz):
                vec_z(l, k).start()

    def vec_last(l):
        @pl.when(core == l)
        def _():
            total = ng[3]
            for k in range(1, nz):
                vec_z(l, k).wait_recv()
                total = total + vn[k - 1]
            turned = pltpu.roll(total, lax.rem(place * -block + width, width), 1)
            out_norm[...] = turned[:, 0:LANES]
            norm_out().start()

    def norm_out():
        return pltpu.make_async_copy(out_norm, on, local_sem.at[9])

    def vec_drain(l):
        @pl.when(core != l)
        def _():
            vec_core(l).wait_send()

        @pl.when(core == l)
        def _():
            vec_y(l).wait_send()
            for k in range(1, nz):
                vec_z(l, k).wait_send()


    def exchange(i, c):
        return remote(xs.at[c], xr.at[i % 2, c], xs_sem.at[c], xr_sem.at[i % 2, c], to_x)

    def send(i, c):
        exchange(i, c).start()

    def arrive(i, c):
        exchange(i, c).wait()

    def both(i, c, r):
        rows = pl.ds(r * SUB, SUB)
        return xs[c, rows].astype(F32) + xr[i % 2, c, rows].astype(F32)

    def chunk_rows(c):
        return pl.ds(pl.multiple_of(c * CHUNK, CHUNK), CHUNK)

    def sub_rows(c, r):
        return pl.ds(pl.multiple_of(c * CHUNK + r * SUB, SUB), SUB)

    def columns(j, span):
        return pl.ds(pl.multiple_of(j * span, LANES), span)


    def out_copy(l, which, src, dst):
        def away():
            return remote(src, dst.at[core], out_send.at[which], out_recv.at[which], to_core)

        def here():
            return pltpu.make_async_copy(src, dst.at[core], local_sem.at[which])

        return here, away

    def out_start(l, which, src, dst):
        here, away = out_copy(l, which, src, dst)

        @pl.when(core == l)
        def _():
            here().start()

        @pl.when(core != l)
        def _():
            away().start()

    def out_wait(l, which, src, dst):
        here, away = out_copy(l, which, src, dst)

        @pl.when(core == l)
        def _():
            here().wait()
            remote(
                src, dst.at[1 - core], out_send.at[which], out_recv.at[which], to_core
            ).wait_recv()

        @pl.when(core != l)
        def _():
            away().wait_send()


    def weight(l, m):
        if m == QK:
            pair = full[m][l, :, :, 0], full[m][l, :, :, 1]
            return jnp.concatenate([flat_rows(one) for one in pair], 1)
        return flat_rows(full[m][l])

    def project(l, c):
        rows = chunk_rows(c)
        for m, span in ((QK, slice(0, 2 * local)), (V, slice(2 * local, 3 * local))):
            packed[l, rows, span] = dot(zin[l, rows], weight(l, m)).astype(BF)

    low_lane = lax.broadcasted_iota(jnp.int32, (1, LANES), 1) < LANES // 2

    def both_heads(value):
        none = jnp.zeros_like(value)
        return jnp.concatenate(
            [jnp.where(low_lane, value, none), jnp.where(low_lane, none, value)], 0
        )

    def one_head(value):
        half = value.shape[0] // 2
        return jnp.where(low_lane, value[:half], value[half:])

    def head_columns(j):
        return tuple(
            slice(part * local + j * LANES, part * local + (j + 1) * LANES)
            for part in range(3)
        )

    def attend(l, c):
        rows = slice(c * CHUNK, (c + 1) * CHUNK)
        keys = jnp.concatenate([keys_ref[...]] * (2 * CHUNK // LANES), 1)
        groups = jnp.concatenate([groups_ref[l : l + 1, rows]] * 2, 1)
        allowed = keys == groups
        for j in range(local // LANES):
            q_cols, k_cols, v_cols = head_columns(j)
            query = both_heads(packed[l, rows, q_cols] * scale)
            scores = jnp.where(allowed, dot_nt(packed[l, :, k_cols], query), -1e9)
            expo = jnp.exp(scores - jnp.max(scores, 0, keepdims=True))
            low = (expo * (1.0 / jnp.sum(expo, 0, keepdims=True))).astype(BF)
            prob[l, 2 * j, :, rows] = low[:, :CHUNK]
            prob[l, 2 * j + 1, :, rows] = low[:, CHUNK:]
            mixed[l, rows, q_cols] = one_head(dot_tn(low, packed[l, :, v_cols])).astype(BF)

    def send_product(i, l, c, *pairs):
        total = 0.0
        for left, m in pairs:
            total = total + dot_nt(left(), weight(l, m))
        xs[c] = total.astype(BF)
        send(i, c)

    def attend_out(i, l, c):
        send_product(i, l, c, (lambda: mixed[l, chunk_rows(c)], O))

    def gather_norms(l):
        norms[l] = jnp.sum(flat_rows(full[PIECES][l]).reshape(nz * ny, 8, width), 0)

    def norm_of(l, which):
        return norms[l, which : which + 1], norms[l, 2 + which : 3 + which]

    def normalize(value):
        center = value - jnp.mean(value, -1, keepdims=True)
        inverse = lax.rsqrt(jnp.mean(center * center, -1, keepdims=True) + eps)
        return center * inverse, inverse

    def expand(i, l, c):
        rows = chunk_rows(c)
        arrive(i, c)
        gain, shift = norm_of(l, 0)

        def one(r):
            sub = sub_rows(c, r)
            normed, inverse = normalize(zin[l, sub].astype(F32) + both(i, c, r))
            norm1[l, sub] = normed
            roots[sub, l : l + 1] = inverse
            hid[l, sub] = (normed * gain + shift).astype(BF)

        each(CHUNK // SUB, one)

        for m in (UA, UB):
            for part in range(units // 2 // TILE):
                cols = slice(part * TILE, (part + 1) * TILE)
                pre = dot(hid[l, rows], flat_rows(full[m][l, :, :, :, cols]))
                lower = 0.5 + 0.5 * lax.erf(pre * 0.7071067811865476)
                density = jnp.exp(-0.5 * pre * pre) * 0.3989422804014327
                start = (m - UA) * units // 2 + part * TILE
                act[l, rows, start : start + TILE] = (pre * lower).astype(BF)
                slope[l, rows, start : start + TILE] = (lower + pre * density).astype(BF)

    def halves(ref, l, rows):
        low, high = slice(0, units // 2), slice(units // 2, units)
        return (lambda: ref[l, rows, low]), (lambda: ref[l, rows, high])

    def contract(i, l, c):
        low, high = halves(act, l, chunk_rows(c))
        send_product(i, l, c, (low, DA), (high, DB))

    def second_norm(i, l, c, r):
        sub = sub_rows(c, r)
        gain, shift = norm_of(l, 0)
        hidden = norm1[l, sub] * gain + shift
        return normalize(hidden + both(i, c, r))

    def norm_back(grad, normed, inverse, gain):
        scaled = grad * gain
        inner = (
            scaled
            - jnp.mean(scaled, -1, keepdims=True)
            - normed * jnp.mean(scaled * normed, -1, keepdims=True)
        )
        return inner * inverse

    def count(l, which, grad, normed):
        ng[l, which : which + 1] += jnp.sum(grad * normed, 0, keepdims=True)
        ng[l, 2 + which : 3 + which] += jnp.sum(grad, 0, keepdims=True)

    def top_back(l, c, r, grad, normed, inverse):
        sub = sub_rows(c, r)
        count(l, 1, grad, normed)
        back = norm_back(grad, normed, inverse, norm_of(l, 1)[0])
        gsum[sub] = back
        gtok[sub] = back.astype(BF)

    def expand_back(i, l, c):
        rows = chunk_rows(c)
        for m in (DA, DB):
            cols = slice((m - DA) * units // 2, (m - DA + 1) * units // 2)
            grad = dot(gtok[rows], flat_rows(full[m][l]))
            slope[l, rows, cols] = (grad * slope[l, rows, cols].astype(F32)).astype(BF)

        low, high = halves(slope, l, rows)
        send_product(i, l, c, (low, UA), (high, UB))

    def weight_grad(l, m, source, right, start=0):
        gather_drain(l, m)
        span = 2 * local if m == QK else full[m].shape[-1]
        grad = dot_tn(source[...], right[l, :, start : start + span]).astype(BF)
        grad = grad.reshape(nz, ny, block, span)
        if m == QK:
            full[m][l, :, :, 0] = grad[..., 0:local]
            full[m][l, :, :, 1] = grad[..., local:span]
        else:
            full[m][l] = grad
        sum_start(l, m)

    def attend_back(l):
        for j in range(local // LANES):
            q_cols, k_cols, v_cols = head_columns(j)
            grad = both_heads(gmix[:, q_cols])
            low = jnp.concatenate([prob[l, 2 * j], prob[l, 2 * j + 1]], 1)
            wide = low.astype(F32)
            product = wide * dot_nt(packed[l, :, v_cols], grad)
            total = jnp.sum(product, 0, keepdims=True)
            back = (product - wide * total).astype(BF)
            packed[l, :, v_cols] = dot(low, grad).astype(BF)
            g_key = dot(back, both_heads(packed[l, :, q_cols]))
            g_query = one_head(dot_tn(back, packed[l, :, k_cols]))
            packed[l, :, q_cols] = (g_query * scale).astype(BF)
            packed[l, :, k_cols] = (g_key * scale).astype(BF)

    def middle_back(i, l, c):
        rows = chunk_rows(c)
        arrive(i, c)

        def one(r):
            sub = sub_rows(c, r)
            grad = gsum[sub] + both(i, c, r)
            normed = norm1[l, sub]
            count(l, 0, grad, normed)
            back = norm_back(grad, normed, roots[sub, l : l + 1], norm_of(l, 0)[0])
            gsum[sub] = back
            gtok[sub] = back.astype(BF)

        each(CHUNK // SUB, one)
        gmix[rows] = dot(gtok[rows], flat_rows(full[O][l])).astype(BF)

    def project_back(i, l, c):
        rows = chunk_rows(c)
        send_product(
            i,
            l,
            c,
            (lambda: packed[l, rows, 0 : 2 * local], QK),
            (lambda: packed[l, rows, 2 * local : 3 * local], V),
        )


    barrier = pltpu.get_barrier_semaphore()
    peers = [to_x, to_core, to_y] + [to_z(k) for k in range(1, nz)]
    for peer in peers:
        pl.semaphore_signal(barrier, inc=1, device_id=peer, device_id_type=MESH)
    entry = [
        pltpu.make_async_copy(src, dst, local_sem.at[4 + i])
        for i, (src, dst) in enumerate(
            (
                (x_ref.at[core], zin.at[0]),
                (go_ref.at[core], gtop),
                (segs_ref, segs),
            )
        )
    ]
    first_rows, top_rows, id_rows = entry
    for copy in entry:
        copy.start()
    ng[...] = jnp.zeros_like(ng)
    vectors = jnp.zeros((8, width), F32)
    full[N][core, z, y] = vectors
    full[N][core, z, y, 0:2, 0:block] = gain_ref[0].astype(F32)
    full[N][core, z, y, 2:4, 0:block] = shift_ref[0].astype(F32)
    full[N][core, z, y] = pltpu.roll(full[N][core, z, y], place * block, 1)
    pl.semaphore_wait(barrier, len(peers))

    gather_own(0, QK, V, N, O)
    gather_far(0, QK, V, N, O)
    gather_own(0, UA, UB, DA, DB)
    id_rows.wait()
    row = segs[pl.ds(core, 1)]
    mapped = jnp.zeros_like(row)
    for i in range(partner_ref.shape[1]):
        mapped = jnp.where(row == i, partner_ref[core, i], mapped)
    groups_ref[0:1] = row.astype(F32)
    groups_ref[1:2] = mapped.astype(F32)
    keys_ref[...] = jnp.broadcast_to(row.astype(F32), (LANES, length)).T
    gather_cross(0, V, N, O)
    gather_far(0, UA)
    gather_pass(0, QK, V, N, O)
    gather_far(0, UB)
    gather_late(0, QK, V, N, O)
    gather_end(0, QK, V, N)
    gather_own(1, QK, V, N, O, UA, UB, DA, DB)
    first_rows.wait()
    gather_norms(0)
    each(chunks, lambda c: project(0, c))
    attend(0, 0)
    gather_pass(0, UA)
    gather_far(0, DA)
    gather_end(0, O)
    attend_out(0, 0, 0)
    attend(0, 1)
    attend_out(0, 0, 1)
    gather_late(0, UA)
    gather_pass(0, UB)
    gather_far(0, DB)
    gather_end(0, UA)
    gather_late(0, UB)
    gather_pass(0, DA)
    gather_end(0, UB)
    expand(0, 0, 0)
    gather_late(0, DA)
    gather_pass(0, DB)
    gather_far(1, QK, V, N, O)
    gather_cross(1, V, N, O)
    expand(0, 0, 1)
    gather_late(0, DB)
    gather_end(0, DA, DB)
    gather_far(1, UA)
    each(chunks, lambda c: contract(1, 0, c))

    def into_second(c):
        arrive(1, c)
        gain, shift = norm_of(0, 1)

        def one(r):
            sub = sub_rows(c, r)
            normed, inverse = second_norm(1, 0, c, r)
            norm2[sub] = normed.astype(BF)
            roots[sub, 2:3] = inverse
            zin[1, sub] = (normed * gain + shift).astype(BF)

        each(CHUNK // SUB, one)

    gather_pass(1, QK, V, N, O)
    gather_far(1, UB)
    into_second(0)
    gather_late(1, QK, V, N, O)
    gather_pass(1, UA)
    gather_far(1, DA)
    into_second(1)
    gather_late(1, UA)
    out_start(0, 0, zin.at[1], lo_ref)
    gather_end(1, QK, V, N)
    gather_norms(1)
    each(chunks, lambda c: project(1, c))
    gather_pass(1, UB)
    gather_far(1, DB)
    attend(1, 0)
    gather_end(1, O)
    attend_out(2, 1, 0)
    gather_late(1, UB)
    gather_pass(1, DA)
    attend(1, 1)
    attend_out(2, 1, 1)
    gather_late(1, DA)
    gather_pass(1, DB)
    gather_end(1, UA, UB)
    expand(2, 1, 0)
    gather_late(1, DB)
    gather_end(1, DA, DB)
    contract(3, 1, 0)
    expand(2, 1, 1)
    contract(3, 1, 1)
    top_rows.wait()

    def over_top(c):
        arrive(3, c)
        gain, shift = norm_of(1, 1)

        def one(r):
            sub = sub_rows(c, r)
            normed, inverse = second_norm(3, 1, c, r)
            top_back(1, c, r, gtop[sub].astype(F32), normed, inverse)
            gtop[sub] = (normed * gain + shift).astype(BF)

        each(CHUNK // SUB, one)

    over_top(0)
    expand_back(4, 1, 0)
    over_top(1)
    expand_back(4, 1, 1)
    out_start(1, 1, gtop, lo_ref)
    weight_grad(1, DA, gtok, act)
    weight_grad(1, DB, gtok, act, units // 2)
    weight_grad(1, UA, hid.at[1], slope)
    weight_grad(1, UB, hid.at[1], slope, units // 2)
    middle_back(4, 1, 0)
    sum_first(1, DA)
    middle_back(4, 1, 1)
    sum_first(1, DB)
    attend_back(1)
    sum_second(1, DA)
    each(chunks, lambda c: project_back(5, 1, c))
    sum_first(1, UA)
    weight_grad(1, O, gtok, mixed)
    weight_grad(1, QK, zin.at[1], packed)
    weight_grad(1, V, zin.at[1], packed, 2 * local)
    vec_start(1)
    sum_relay(1, DA)
    sum_second(1, DB)
    sum_first(1, UB)
    sum_first(1, O)

    def under(c):
        arrive(5, c)

        def one(r):
            sub = sub_rows(c, r)
            low = (gsum[sub] + both(5, c, r)).astype(BF)
            gin[sub] = low
            top_back(0, c, r, low.astype(F32), norm2[sub].astype(F32), roots[sub, 2:3])

        each(CHUNK // SUB, one)
        expand_back(6, 0, c)

    sum_relay(1, DB)
    under(0)
    sum_second(1, UA)
    sum_first(1, QK)
    sum_first(1, V)
    under(1)
    out_start(1, 3, gin, ig_ref)
    weight_grad(0, DA, gtok, act)
    weight_grad(0, DB, gtok, act, units // 2)
    sum_relay(1, UA)
    sum_second(1, UB)
    weight_grad(0, UA, hid.at[0], slope)
    weight_grad(0, UB, hid.at[0], slope, units // 2)
    vec_first(1)
    sum_first(0, DA)
    middle_back(6, 0, 0)
    sum_first(0, DB)
    sum_relay(1, UB)
    sum_second(1, O)
    middle_back(6, 0, 1)
    attend_back(0)
    sum_second(0, DA)
    sum_second(1, QK)
    sum_relay(1, O)
    each(chunks, lambda c: project_back(7, 0, c))
    sum_first(0, UA)
    weight_grad(0, O, gtok, mixed)
    weight_grad(0, QK, zin.at[0], packed)
    weight_grad(0, V, zin.at[0], packed, 2 * local)
    vec_start(0)
    sum_relay(0, DA)
    sum_second(0, DB)
    sum_first(0, UB)
    sum_relay(1, QK)
    sum_second(1, V)
    vec_second(1)
    sum_first(0, O)
    sum_relay(0, DB)
    sum_second(0, UA)
    sum_first(0, QK)
    sum_first(0, V)
    vec_first(0)
    sum_relay(1, V)

    def bottom(c):
        arrive(7, c)

        def one(r):
            sub = sub_rows(c, r)
            gtop[sub] = (gsum[sub] + both(7, c, r)).astype(BF)

        each(CHUNK // SUB, one)

    out_wait(1, 1, gtop, lo_ref)
    bottom(0)
    sum_relay(0, UA)
    sum_second(0, UB)
    sum_second(0, O)
    bottom(1)
    out_start(0, 2, gtop, ig_ref)
    sum_relay(0, UB)
    sum_relay(0, O)
    sum_second(0, QK)
    sum_second(0, V)
    vec_second(0)
    sum_relay(0, QK)
    sum_relay(0, V)
    for l in (1, 0):
        for m in (DA, DB, UA, UB, O, QK, V):
            sum_last(l, m)
        vec_last(l)
    for l in range(2):
        for m in range(PIECES):
            sum_drain(l, m)
        vec_drain(l)
        gather_drain(l, N)
    for m in range(PIECES):
        result_out(m).wait()
    norm_out().wait()
    out_wait(0, 0, zin.at[1], lo_ref)
    out_wait(0, 2, gtop, ig_ref)
    out_wait(1, 3, gin, ig_ref)


def fused(sizes, x, grad, segments, partner, gains, shifts, shards_in):
    nz, ny, length, width, local, units, eps, scale = sizes
    block = width // (nz * ny)
    chunks = length // CHUNK
    tiles = ((2, block, local),) + ((block, local),) * 2 + ((block, units // 2),) * 4
    dma = pltpu.SemaphoreType.DMA
    vmem = pltpu.VMEM
    scratch = [vmem((2, nz, ny) + tile, BF) for tile in tiles]
    scratch += [vmem((2, nz, ny, 8, width), F32)]
    scratch += [vmem((nz, ny) + tile, BF) for tile in tiles]
    scratch += [vmem((nz,) + tile, BF) for tile in tiles]
    scratch += [vmem((nz,) + tile, BF) for tile in tiles]
    scratch += [vmem(tile, F32) for tile in tiles]
    scratch += [
        vmem((length, LANES), F32),
        vmem((2, length), F32),
        vmem((2, length), jnp.int32),
        vmem((8, LANES), F32),
        vmem((8, width), F32),
        vmem((8, width), F32),
        vmem((nz - 1, 8, width), F32),
        vmem((4, 8, width), F32),
        vmem((2, length, width), BF),
        vmem((2, length, 3 * local), BF),
        vmem((2, local // HEAD, length, length), BF),
        vmem((2, length, local), BF),
        vmem((2, length, width), F32),
        vmem((2, length, width), BF),
        vmem((2, length, units), BF),
        vmem((2, length, units), BF),
        vmem((length, width), BF),
        vmem((length, 4), F32),
        vmem((length, width), F32),
        vmem((length, width), BF),
        vmem((length, local), BF),
        vmem((length, width), BF),
        vmem((length, width), BF),
        vmem((2, 8, width), F32),
        vmem((chunks, CHUNK, width), BF),
        vmem((2, chunks, CHUNK, width), BF),
        dma((10,)),
        dma((PIECES,)),
        dma((PIECES,)),
        dma((4,)),
        dma((4,)),
        dma((chunks,)),
        dma((2, chunks)),
        dma((PIECES + 1, 2, nz)),
        dma((PIECES + 1, 2, nz)),
        dma((PIECES + 1, nz)),
        dma((PIECES + 1, nz)),
        dma((PIECES + 1, 2 * nz)),
        dma((PIECES + 1, 2 * nz)),
        dma((PIECES + 1, 2)),
        dma((PIECES + 1, 2)),
        dma((PIECES + 1, nz)),
        dma((PIECES + 1, nz)),
        dma((PIECES + 1, nz - 1)),
        dma((PIECES + 1, nz)),
    ]
    anywhere = pl.BlockSpec(memory_space=pl.ANY)
    inside = pl.BlockSpec(memory_space=pltpu.VMEM)
    outs = (
        ((2, length, width), BF),
        ((2, length, width), BF),
        ((3, block, local), F32),
        ((block, local), F32),
        ((block, units), F32),
        ((block, units), F32),
        ((8, LANES), F32),
    )
    return pl.pallas_call(
        functools.partial(kernel, sizes),
        out_shape=[jax.ShapeDtypeStruct(*out) for out in outs],
        in_specs=[pl.BlockSpec(memory_space=pltpu.SMEM)] + [inside] * 2 + [anywhere] * 7,
        out_specs=[anywhere] * len(outs),
        scratch_shapes=scratch,
        compiler_params=pltpu.CompilerParams(
            collective_id=0, has_side_effects=True, vmem_limit_bytes=127 << 19
        ),
    )(partner, gains, shifts, x, grad, segments, *shards_in)


def place_results(*refs):
    count = (len(refs) - 2) // 3
    srcs, dsts, held = refs[:count], refs[count : 2 * count], refs[2 * count : 3 * count]
    into, out = refs[3 * count :]
    for i in range(count):
        pltpu.make_async_copy(srcs[i], held[i], into.at[i]).start()
    for i in range(count):
        pltpu.make_async_copy(srcs[i], held[i], into.at[i]).wait()
        pltpu.make_async_copy(held[i], dsts[i], out.at[i]).start()
    for i in range(count):
        pltpu.make_async_copy(held[i], dsts[i], out.at[i]).wait()


def placed_results(*items):
    dma = pltpu.SemaphoreType.DMA
    anywhere = pl.BlockSpec(memory_space=pl.ANY)
    return pl.pallas_call(
        place_results,
        out_shape=[jax.ShapeDtypeStruct(item.shape, item.dtype) for item in items],
        in_specs=[anywhere] * len(items),
        out_specs=[anywhere] * len(items),
        scratch_shapes=[pltpu.VMEM(item.shape, item.dtype) for item in items]
        + [dma((len(items),)), dma((len(items),))],
        compiler_params=pltpu.CompilerParams(vmem_limit_bytes=127 << 19),
    )(*items)


def kernel_shards(
    inputs, segments, partner, grad_output, w_qkv, w_out, w_up, w_down, norm_gain, norm_shift
):
    parts = lax.axis_size("dp")
    length, width = inputs.shape[1:]
    local, units = w_out.shape[1], w_up.shape[2]
    block = width // parts
    sizes = (parts // 2, 2, length, width, local, units, norm_eps, score_scale)
    shards_in = (w_qkv[0].transpose(1, 0, 2), w_out[0].T, w_up[0], w_down[0].T)
    outs = fused(
        sizes, inputs, grad_output, segments, partner, norm_gain, norm_shift, shards_in
    )
    *whole, norm = outs
    layer_outputs, input_grads, g_qkv, g_out, g_up, g_down = placed_results(*whole)
    return (
        layer_outputs[None],
        input_grads[None],
        g_qkv.transpose(1, 0, 2)[None],
        g_out.T[None],
        g_up[None],
        g_down.T[None],
        norm[None, 0:2, 0:block],
        norm[None, 2:4, 0:block],
    )


def solution(mesh):
    placed = (
        P("dp", None, None),
        P("dp", None),
        P("dp", None),
        P("dp", None, None),
        P("section", "dp", None, "tensor"),
        P("section", "tensor", "dp"),
        P("section", "dp", "tensor"),
        P("section", "tensor", "dp"),
        P("section", None, "dp"),
        P("section", None, "dp"),
    )
    block = WIDTH // mesh.shape["dp"]
    whole_tiles = block * mesh.shape["dp"] == WIDTH and block % 16 == 0
    return jax.shard_map(
        kernel_shards if whole_tiles else shards,
        mesh=mesh,
        in_specs=placed,
        out_specs=(
            P("section", "dp", None, None),
            P("section", "dp", None, None),
            P("section", "dp", None, "tensor"),
            P("section", "tensor", "dp"),
            P("section", "dp", "tensor"),
            P("section", "tensor", "dp"),
            P("section", None, "dp"),
            P("section", None, "dp"),
        ),
        check_vma=False,
    )
```

```python
import functools

import jax
import jax.numpy as jnp
from jax import lax
from jax.experimental import pallas as pl
from jax.experimental.pallas import tpu as pltpu
from jax.sharding import PartitionSpec as P

HEAD = 64
WIDTH = 768


norm_eps = 1e-06
score_scale = 0.125
masked_value = -1000000000.0


def partner_of(segment_ids, partner):
    table = jnp.arange(partner.shape[-1], dtype=jnp.int32)
    hits = segment_ids[..., None] == table
    return jnp.sum(jnp.where(hits, partner[None, :], 0), -1)


def layer_norm(values, gain, shift):
    center = values - jnp.mean(values, -1, keepdims=True)
    inverse = lax.rsqrt(jnp.mean(center * center, -1, keepdims=True) + norm_eps)
    normed = center * inverse
    return (normed * gain + shift, normed, inverse)


def norm_back(grad, normed, inverse, gain):
    scaled = grad * gain
    inner = (
        scaled
        - jnp.mean(scaled, -1, keepdims=True)
        - normed * jnp.mean(scaled * normed, -1, keepdims=True)
    )
    return inner * inverse


def gelu_slope(values):
    lower = 0.5 * (1.0 + lax.erf(values * 0.7071067811865476))
    density = jnp.exp(-0.5 * values * values) * 0.3989422804014327
    return lower + values * density


def swapped(value, axis):
    size = lax.axis_size(axis)
    return lax.ppermute(value, axis, [(i, size - 1 - i) for i in range(size)])


def tensor_sum(partial_value):
    low = partial_value.astype(jnp.bfloat16)
    return low.astype(jnp.float32) + swapped(low, "tensor").astype(jnp.float32)


def masked_scores(query, key, query_groups, key_groups):
    scores = (
        jnp.einsum("qhd,khd->hqk", query, key, preferred_element_type=jnp.float32) * score_scale
    )
    allowed = query_groups[:, None] == key_groups[None, :]
    return jnp.where(allowed[None], scores, masked_value)


def attend(query, key, value, query_groups, key_groups):
    scores = masked_scores(query, key, query_groups, key_groups)
    top = jnp.max(scores, -1, keepdims=True)
    expo = jnp.exp(scores - top)
    total = jnp.sum(expo, -1, keepdims=True)
    probs = (expo / total).astype(jnp.bfloat16)
    mixed = jnp.einsum("hqk,khd->qhd", probs, value, preferred_element_type=jnp.float32)
    return (mixed.astype(jnp.bfloat16), (top + jnp.log(total))[..., 0])


def attend_back(query, key, value, query_groups, key_groups, spread, grad_mixed):
    scores = masked_scores(query, key, query_groups, key_groups)
    probs = jnp.exp(scores - spread[..., None])
    probs_low = probs.astype(jnp.bfloat16)
    grad_probs = jnp.einsum("qhd,khd->hqk", grad_mixed, value, preferred_element_type=jnp.float32)
    grad_value = jnp.einsum(
        "hqk,qhd->khd", probs_low, grad_mixed, preferred_element_type=jnp.float32
    )
    row_dot = jnp.sum(probs * grad_probs, -1, keepdims=True)
    grad_scores = (probs * (grad_probs - row_dot)).astype(jnp.bfloat16)
    grad_query = (
        jnp.einsum("hqk,khd->qhd", grad_scores, key, preferred_element_type=jnp.float32)
        * score_scale
    )
    grad_key = (
        jnp.einsum("hqk,qhd->khd", grad_scores, query, preferred_element_type=jnp.float32)
        * score_scale
    )
    return jnp.stack(
        [
            grad_query.astype(jnp.bfloat16),
            grad_key.astype(jnp.bfloat16),
            grad_value.astype(jnp.bfloat16),
        ],
        1,
    )


def layer_forward(flat, weights, query_groups, key_groups):
    w_qkv, w_out, w_up, w_down, gains, shifts = weights
    length = flat.shape[0]
    local = w_qkv.shape[2]
    packed = jnp.einsum("nd,dcm->ncm", flat, w_qkv, preferred_element_type=jnp.float32).astype(
        jnp.bfloat16
    )
    heads = packed.reshape(length, 3, local // HEAD, HEAD)
    mixed, spread = attend(heads[:, 0], heads[:, 1], heads[:, 2], query_groups, key_groups)
    mixed_flat = mixed.reshape(length, local)
    attn_out = tensor_sum(jnp.dot(mixed_flat, w_out, preferred_element_type=jnp.float32))
    hidden, normed_first, inverse_first = layer_norm(
        flat.astype(jnp.float32) + attn_out, gains[0], shifts[0]
    )
    hidden_low = hidden.astype(jnp.bfloat16)
    pre = jnp.dot(hidden_low, w_up, preferred_element_type=jnp.float32)
    act = jax.nn.gelu(pre, approximate=False).astype(jnp.bfloat16)
    ffn_out = tensor_sum(jnp.dot(act, w_down, preferred_element_type=jnp.float32))
    result, normed_second, inverse_second = layer_norm(hidden + ffn_out, gains[1], shifts[1])
    kept = (
        flat,
        heads,
        spread,
        mixed_flat,
        normed_first,
        inverse_first,
        hidden_low,
        pre,
        act,
        normed_second,
        inverse_second,
    )
    return (result.astype(jnp.bfloat16), kept)


def layer_backward(grad_result, kept, weights, query_groups, key_groups):
    w_qkv, w_out, w_up, w_down, gains, shifts = weights
    (
        flat,
        heads,
        spread,
        mixed_flat,
        normed_first,
        inverse_first,
        hidden_low,
        pre,
        act,
        normed_second,
        inverse_second,
    ) = kept
    length = flat.shape[0]
    local = w_qkv.shape[2]
    gain_second = jnp.sum(grad_result * normed_second, 0)
    shift_second = jnp.sum(grad_result, 0)
    grad_sum2 = norm_back(grad_result, normed_second, inverse_second, gains[1])
    grad_ffn = grad_sum2.astype(jnp.bfloat16)
    grad_down = jnp.einsum("nf,nd->fd", act, grad_ffn, preferred_element_type=jnp.float32)
    grad_act = jnp.einsum("nd,fd->nf", grad_ffn, w_down, preferred_element_type=jnp.float32)
    grad_pre = (grad_act * gelu_slope(pre)).astype(jnp.bfloat16)
    grad_up = jnp.einsum("nd,nf->df", hidden_low, grad_pre, preferred_element_type=jnp.float32)
    grad_hidden = grad_sum2 + tensor_sum(
        jnp.einsum("nf,df->nd", grad_pre, w_up, preferred_element_type=jnp.float32)
    )
    gain_first = jnp.sum(grad_hidden * normed_first, 0)
    shift_first = jnp.sum(grad_hidden, 0)
    grad_resid = norm_back(grad_hidden, normed_first, inverse_first, gains[0])
    grad_attn = grad_resid.astype(jnp.bfloat16)
    grad_out = jnp.einsum("nm,nd->md", mixed_flat, grad_attn, preferred_element_type=jnp.float32)
    grad_mixed = jnp.einsum(
        "nd,md->nm", grad_attn, w_out, preferred_element_type=jnp.float32
    ).astype(jnp.bfloat16)
    grad_mixed = grad_mixed.reshape(length, local // HEAD, HEAD)
    grad_heads = attend_back(
        heads[:, 0], heads[:, 1], heads[:, 2], query_groups, key_groups, spread, grad_mixed
    )
    grad_packed = grad_heads.reshape(length, 3, local)
    grad_qkv = jnp.einsum("nd,ncm->dcm", flat, grad_packed, preferred_element_type=jnp.float32)
    grad_input = grad_resid + tensor_sum(
        jnp.einsum("ncm,dcm->nd", grad_packed, w_qkv, preferred_element_type=jnp.float32)
    )
    grads = (
        grad_qkv.astype(jnp.bfloat16),
        grad_out.astype(jnp.bfloat16),
        grad_up.astype(jnp.bfloat16),
        grad_down.astype(jnp.bfloat16),
        jnp.stack([gain_first, gain_second]),
        jnp.stack([shift_first, shift_second]),
    )
    return (grads, grad_input.astype(jnp.bfloat16))


def shards(
    inputs, segments, partner, grad_output, w_qkv, w_out, w_up, w_down, norm_gain, norm_shift
):
    core = lax.axis_index("section")
    rows = inputs.shape[0] // lax.axis_size("section")

    def per_row(row):
        key_groups = lax.dynamic_index_in_dim(segments, row, 0, False)
        mapped = partner_of(key_groups, lax.dynamic_index_in_dim(partner, row, 0, False))
        flat = lax.dynamic_index_in_dim(inputs, row, 0, False)
        first, kept_first = layer_forward(flat, layers[0], key_groups, key_groups)
        second, kept_second = layer_forward(first, layers[1], mapped, key_groups)
        grad_top = lax.dynamic_index_in_dim(grad_output, row, 0, False).astype(jnp.float32)
        grads_second, grad_mid = layer_backward(
            grad_top, kept_second, layers[1], mapped, key_groups
        )
        grads_first, grad_low = layer_backward(
            grad_mid.astype(jnp.float32), kept_first, layers[0], key_groups, key_groups
        )
        return (first, second, grad_low, grad_mid, grads_first, grads_second)

    def gathered(shard, axis):
        own = lax.all_gather(shard[0], "dp", axis=axis, tiled=True)
        other = swapped(own, "section")
        return (jnp.where(core == 0, own, other), jnp.where(core == 0, other, own))

    pairs = [
        gathered(w_qkv, 0),
        gathered(w_out, 1),
        gathered(w_up, 0),
        gathered(w_down, 1),
        gathered(norm_gain, 1),
        gathered(norm_shift, 1),
    ]
    layers = [
        [pair[layer].astype(jnp.float32) if place > 3 else pair[layer] for place, pair in enumerate(pairs)]
        for layer in range(2)
    ]
    done = [per_row(core * rows + step) for step in range(rows)]

    def summed(first, second, axis):
        mine = jnp.where(core == 0, first, second)
        away = jnp.where(core == 0, second, first)
        both = mine.astype(jnp.float32) + swapped(away, "section").astype(jnp.float32)
        return lax.psum_scatter(both.astype(first.dtype), "dp", scatter_dimension=axis, tiled=True).astype(jnp.float32)

    def total(layer, place):
        value = done[0][4 + layer][place]
        for item in done[1:]:
            value = (value.astype(jnp.float32) + item[4 + layer][place].astype(jnp.float32)).astype(value.dtype)
        return value

    axes = (0, 1, 0, 1, 1, 1)
    sums = [summed(total(0, place), total(1, place), axis) for place, axis in enumerate(axes)]

    def regrouped(first, second):
        mine = jnp.where(core == 0, first, second)
        other = swapped(jnp.where(core == 0, second, first), "section")
        return jnp.where(
            core == 0, jnp.concatenate([mine, other]), jnp.concatenate([other, mine])
        )

    layer_outputs = regrouped(
        jnp.stack([item[0] for item in done]), jnp.stack([item[1] for item in done])
    )
    input_grads = regrouped(
        jnp.stack([item[2] for item in done]), jnp.stack([item[3] for item in done])
    )
    return (layer_outputs[None], input_grads[None]) + tuple(value[None] for value in sums)


MESH = pl.DeviceIdType.MESH
BF = jnp.bfloat16
F32 = jnp.float32
CHUNK = 256
SUB = 128
TILE = 256
LANES = 128
QK, V, O, UA, UB, DA, DB, N = range(8)
PIECES = N
AHEAD = -1
Y_FIRST = (DB, N)
NT = (((1,), (1,)), ((), ()))
TN = (((0,), (0,)), ((), ()))


def dot(left, right):
    return jnp.dot(left, right, preferred_element_type=F32)


def dot_nt(left, right):
    return lax.dot_general(left, right, NT, preferred_element_type=F32)


def dot_tn(left, right):
    return lax.dot_general(left, right, TN, preferred_element_type=F32)


def flat_rows(value):
    return value.reshape(-1, value.shape[-1])


def kernel(
    sizes,
    partner_ref,
    gain_ref,
    shift_ref,
    x_ref,
    go_ref,
    segs_ref,
    sq,
    so,
    su,
    sd,
    lo_ref,
    ig_ref,
    oq,
    oo,
    ou,
    od,
    on,
    *refs,
):
    nz, ny, length, width, local, units, eps, scale = sizes
    block = width // (nz * ny)
    full, refs = refs[: PIECES + 1], refs[PIECES + 1 :]
    summed, refs = refs[:PIECES], refs[PIECES:]
    from_y, refs = refs[:PIECES], refs[PIECES:]
    from_z, refs = refs[:PIECES], refs[PIECES:]
    result, refs = refs[:PIECES], refs[PIECES:]
    (
        keys_ref,
        groups_ref,
        segs,
        out_norm,
        rn,
        yn,
        vn,
        ng,
        zin,
        packed,
        prob,
        mixed,
        norm1,
        hid,
        act,
        slope,
        norm2,
        roots,
        gsum,
        gtok,
        gmix,
        gtop,
        gin,
        norms,
        xs,
        xr,
        token,
        local_sem,
        own_sem,
        done_sem,
        out_send,
        out_recv,
        xs_sem,
        xr_sem,
        az_s,
        az_r,
        ay_s,
        ay_r,
        ac_s,
        ac_r,
        gc_s,
        gc_r,
        gy_s,
        gy_r,
        gz_s,
        gz_r,
    ) = refs
    chunks = length // CHUNK
    core = lax.axis_index("section")
    place = lax.axis_index("dp")
    side = lax.axis_index("tensor")
    z, y = place // ny, lax.rem(place, ny)
    other_y = 1 - y
    to_x = {"tensor": 1 - side}
    to_core = {"section": 1 - core}
    to_y = {"dp": z * ny + other_y}

    def turn(k):
        return lax.rem(z + k + nz, nz)

    def to_z(k):
        return {"dp": turn(k) * ny + y}

    half = units // 2
    shard = {
        QK: sq.at[0:2],
        V: sq.at[2],
        O: so,
        UA: su.at[:, 0:half],
        UB: su.at[:, half:units],
        DA: sd.at[:, 0:half],
        DB: sd.at[:, half:units],
    }
    target = {
        QK: oq.at[0:2],
        V: oq.at[2],
        UA: ou.at[:, 0:half],
        UB: ou.at[:, half:units],
        O: oo,
        DA: od.at[:, 0:half],
        DB: od.at[:, half:units],
    }

    def remote(src, dst, send, recv, target):
        return pltpu.make_async_remote_copy(
            src_ref=src,
            dst_ref=dst,
            send_sem=send,
            recv_sem=recv,
            device_id=target,
            device_id_type=MESH,
        )

    def each(count, body):
        lax.fori_loop(0, count, lambda i, none: (body(i), none)[1], 0)

    at_end = jnp.logical_or(z == 0, z == nz - 1)
    middle = jnp.logical_not(at_end)
    far_end = jnp.where(z < nz // 2, 0, nz - 1)
    far_origin = nz - 1 - far_end
    near_z = {"dp": jnp.where(z == 0, 1, nz - 2) * ny + y}
    end_z = {"dp": far_end * ny + y}

    def is_far(k):
        return jnp.logical_or(
            jnp.logical_and(z == 0, k == nz - 1), jnp.logical_and(z == nz - 1, k == 1)
        )

    def is_late(k):
        return jnp.logical_or(
            jnp.logical_and(z == 0, k == 1), jnp.logical_and(z == nz - 1, k == nz - 1)
        )

    def offsets(body):
        lax.fori_loop(1, nz, lambda k, none: (body(k), none)[1], 0)


    def column(c):
        return (y, other_y)[c]

    def lines(m):
        return (0, 1) if m in Y_FIRST else (0,)

    def gather_z(l, m, k, c, src=None):
        ref = full[m].at[l, z, column(c)]
        return remote(
            ref if src is None else src,
            ref,
            az_s.at[m, c, k - 1],
            az_r.at[m, c, k - 1],
            to_z(k),
        )

    def gather_relay(l, m, c):
        ref = full[m].at[l, far_origin, column(c)]
        slot = jnp.where(z == 1, 0, nz - 2)
        return remote(ref, ref, az_s.at[m, c, nz - 1], az_r.at[m, c, slot], end_z)

    def gather_y(l, m, k, src=None):
        ref = full[m].at[l, turn(-k), y]
        return remote(ref if src is None else src, ref, ay_s.at[m, k], ay_r.at[m, k], to_y)

    def gather_core(l, m, k, c, src=None):
        ref = full[m].at[l, turn(-k), column(c)]
        slot = k + c * nz
        return remote(
            ref if src is None else src, ref, ac_s.at[m, slot], ac_r.at[m, slot], to_core
        )

    def own_copy(l, m):
        return pltpu.make_async_copy(shard[m], full[m].at[l, z, y], own_sem.at[m])

    def gather_own(l, *mats):
        @pl.when(core == l)
        def _():
            for m in mats:
                if m in shard:
                    own_copy(l, m).start()
                gather_y(l, m, 0, shard.get(m)).start()
                gather_core(l, m, 0, 0, shard.get(m)).start()

    def gather_far(l, *mats):
        @pl.when(core == l)
        def _():
            for m in mats:

                def one(k):
                    @pl.when(jnp.logical_not(is_far(k)))
                    def _():
                        gather_z(l, m, k, 0, shard.get(m)).start()

                offsets(one)

    def gather_cross(l, *mats):
        @pl.when(core == l)
        def _():
            for m in mats:
                gather_y(l, m, 0).wait_recv()
                gather_core(l, m, 0, 1).start()

                def one(k):
                    @pl.when(jnp.logical_not(is_far(k)))
                    def _():
                        gather_z(l, m, k, 1).start()

                offsets(one)

    def gather_hand(l, m, k, c):
        gather_z(l, m, k, c).wait_recv()
        gather_core(l, m, k, c).start()
        if m not in Y_FIRST:
            gather_y(l, m, k).start()

    def gather_pass(l, *mats):
        @pl.when(core == l)
        def _():
            for m in mats:
                for c in lines(m):

                    def one(k):
                        @pl.when(jnp.logical_not(is_late(k)))
                        def _():
                            gather_hand(l, m, k, c)

                        @pl.when(jnp.logical_and(middle, k == nz // 2))
                        def _():
                            gather_relay(l, m, c).start()

                    offsets(one)

    def gather_late(l, *mats):
        @pl.when(jnp.logical_and(core == l, at_end))
        def _():
            for m in mats:
                for c in lines(m):
                    gather_hand(l, m, jnp.where(z == 0, 1, nz - 1), c)

    def gather_near(l, m):
        @pl.when(core != l)
        def _():
            each(nz, lambda k: gather_core(l, m, k, 0).wait_recv())

    def gather_end(l, *mats, near=True):
        @pl.when(core == l)
        def _():
            for m in mats:
                if m in shard:
                    own_copy(l, m).wait()
                if m not in Y_FIRST:

                    def one(k):
                        gather_y(l, m, k).wait_recv()
                        gather_core(l, m, k, 1).start()

                    each(nz, one)

        for m in mats:
            if near:
                gather_near(l, m)

        @pl.when(core != l)
        def _():
            for m in mats:
                each(nz, lambda k: gather_core(l, m, k, 1).wait_recv())

    def gather_drain(l, m):
        @pl.when(core == l)
        def _():
            for c in lines(m):

                def one(k):
                    @pl.when(jnp.logical_not(is_far(k)))
                    def _():
                        gather_z(l, m, k, c).wait_send()

                offsets(one)

                @pl.when(middle)
                def _():
                    gather_relay(l, m, c).wait_send()

            gather_y(l, m, 0).wait_send()
            if m not in Y_FIRST:
                offsets(lambda k: gather_y(l, m, k).wait_send())

            def core_sent(k):
                gather_core(l, m, k, 0).wait_send()
                gather_core(l, m, k, 1).wait_send()

            each(nz, core_sent)


    def sum_core(l, m, part):
        column = (other_y, y)[part]
        return remote(
            full[m].at[l, :, column],
            summed[m].at[:, column],
            gc_s.at[m, part],
            gc_r.at[m, part],
            to_core,
        )

    def sum_y(l, m, k):
        return remote(
            full[m].at[l, k, other_y], from_y[m].at[k], gy_s.at[m, k], gy_r.at[m, k], to_y
        )

    def sum_z(l, m, k):
        return remote(
            full[m].at[l, turn(k), y],
            from_z[m].at[k - 1],
            gz_s.at[m, k - 1],
            gz_r.at[m, k - 1],
            to_z(k),
        )

    def sum_near(l, m, k):
        return remote(
            full[m].at[l, turn(k), y],
            from_z[m].at[nz - 1],
            gz_s.at[m, k - 1],
            gz_r.at[m, nz - 1],
            near_z,
        )

    def sum_start(l, m):
        @pl.when(core != l)
        def _():
            sum_core(l, m, 0).start()
            sum_core(l, m, 1).start()

    def sum_first(l, m):
        @pl.when(core == l)
        def _():
            sum_core(l, m, 0).wait_recv()

            def one(k):
                both = full[m][l, k, other_y].astype(F32) + summed[m][k, other_y].astype(F32)
                full[m][l, k, other_y] = both.astype(BF)
                sum_y(l, m, k).start()

            each(nz, one)

    def sum_second(l, m):
        @pl.when(core == l)
        def _():
            sum_core(l, m, 1).wait_recv()

            def total(k):
                at = turn(k)
                sum_y(l, m, at).wait_recv()
                both = full[m][l, at, y].astype(F32) + summed[m][at, y].astype(F32)
                return both + from_y[m][at].astype(F32)

            def one(k):
                full[m][l, turn(k), y] = total(k).astype(BF)
                far = is_far(k)
                held = jnp.logical_and(middle, k == nz // 2)

                @pl.when(far)
                def _():
                    sum_near(l, m, k).start()

                @pl.when(jnp.logical_not(jnp.logical_or(far, held)))
                def _():
                    sum_z(l, m, k).start()

            offsets(one)
            result[m][...] = total(0)

    def sum_relay(l, m):
        @pl.when(jnp.logical_and(core == l, middle))
        def _():
            k = nz // 2
            sum_near(l, m, k).wait_recv()
            both = full[m][l, turn(k), y].astype(F32) + from_z[m][nz - 1].astype(F32)
            full[m][l, turn(k), y] = both.astype(BF)
            sum_z(l, m, k).start()

    def sum_last(l, m):
        @pl.when(core == l)
        def _():
            def one(k):
                @pl.when(jnp.logical_not(is_late(k)))
                def _():
                    sum_z(l, m, k).wait_recv()
                    result[m][...] += from_z[m][k - 1].astype(F32)

            offsets(one)
            result_out(m).start()

    def result_out(m):
        return pltpu.make_async_copy(result[m], target[m], done_sem.at[m])

    def sum_drain(l, m):
        @pl.when(core != l)
        def _():
            sum_core(l, m, 0).wait_send()
            sum_core(l, m, 1).wait_send()

        @pl.when(core == l)
        def _():
            each(nz, lambda k: sum_y(l, m, k).wait_send())
            offsets(lambda k: sum_z(l, m, k).wait_send())


    def vec_core(l):
        return remote(ng.at[l], rn, gc_s.at[PIECES, 0], gc_r.at[PIECES, 0], to_core)

    def vec_y(l):
        return remote(ng.at[2], yn, gy_s.at[PIECES, 0], gy_r.at[PIECES, 0], to_y)

    def vec_z(l, k):
        return remote(
            ng.at[3], vn.at[k - 1], gz_s.at[PIECES, k - 1], gz_r.at[PIECES, k - 1], to_z(k)
        )

    def vec_start(l):
        @pl.when(core != l)
        def _():
            vec_core(l).start()

    def vec_first(l):
        @pl.when(core == l)
        def _():
            vec_core(l).wait_recv()
            ng[2] = ng[l] + rn[...]
            vec_y(l).start()

    def vec_second(l):
        @pl.when(core == l)
        def _():
            vec_y(l).wait_recv()
            ng[3] = ng[2] + yn[...]
            for k in range(1, nz):
                vec_z(l, k).start()

    def vec_last(l):
        @pl.when(core == l)
        def _():
            total = ng[3]
            for k in range(1, nz):
                vec_z(l, k).wait_recv()
                total = total + vn[k - 1]
            turned = pltpu.roll(total, lax.rem(place * -block + width, width), 1)
            out_norm[...] = turned[:, 0:LANES]
            norm_out().start()

    def norm_out():
        return pltpu.make_async_copy(out_norm, on, local_sem.at[9])

    def vec_drain(l):
        @pl.when(core != l)
        def _():
            vec_core(l).wait_send()

        @pl.when(core == l)
        def _():
            vec_y(l).wait_send()
            for k in range(1, nz):
                vec_z(l, k).wait_send()


    def exchange(i, c):
        return remote(xs.at[c], xr.at[i % 2, c], xs_sem.at[c], xr_sem.at[i % 2, c], to_x)

    def send(i, c):
        exchange(i, c).start()

    def arrive(i, c):
        exchange(i, c).wait()

    def both(i, c, r):
        rows = pl.ds(r * SUB, SUB)
        return xs[c, rows].astype(F32) + xr[i % 2, c, rows].astype(F32)

    def chunk_rows(c):
        return pl.ds(pl.multiple_of(c * CHUNK, CHUNK), CHUNK)

    def sub_rows(c, r):
        return pl.ds(pl.multiple_of(c * CHUNK + r * SUB, SUB), SUB)

    def columns(j, span):
        return pl.ds(pl.multiple_of(j * span, LANES), span)


    def out_copy(l, which, src, dst):
        def away():
            return remote(src, dst.at[core], out_send.at[which], out_recv.at[which], to_core)

        def here():
            return pltpu.make_async_copy(src, dst.at[core], local_sem.at[which])

        return here, away

    def out_start(l, which, src, dst):
        here, away = out_copy(l, which, src, dst)

        @pl.when(core == l)
        def _():
            here().start()

        @pl.when(core != l)
        def _():
            away().start()

    def out_wait(l, which, src, dst):
        here, away = out_copy(l, which, src, dst)

        @pl.when(core == l)
        def _():
            here().wait()
            remote(
                src, dst.at[1 - core], out_send.at[which], out_recv.at[which], to_core
            ).wait_recv()

        @pl.when(core != l)
        def _():
            away().wait_send()


    def weight(l, m):
        if m == QK:
            pair = full[m][l, :, :, 0], full[m][l, :, :, 1]
            return jnp.concatenate([flat_rows(one) for one in pair], 1)
        return flat_rows(full[m][l])

    def project(l, c):
        rows = chunk_rows(c)
        for m, span in ((QK, slice(0, 2 * local)), (V, slice(2 * local, 3 * local))):
            packed[l, rows, span] = dot(zin[l, rows], weight(l, m)).astype(BF)

    low_lane = lax.broadcasted_iota(jnp.int32, (1, LANES), 1) < LANES // 2

    def both_heads(value):
        none = jnp.zeros_like(value)
        return jnp.concatenate(
            [jnp.where(low_lane, value, none), jnp.where(low_lane, none, value)], 0
        )

    def one_head(value):
        half = value.shape[0] // 2
        return jnp.where(low_lane, value[:half], value[half:])

    def head_columns(j):
        return tuple(
            slice(part * local + j * LANES, part * local + (j + 1) * LANES)
            for part in range(3)
        )

    def attend(l, c):
        rows = slice(c * CHUNK, (c + 1) * CHUNK)
        keys = jnp.concatenate([keys_ref[...]] * (2 * CHUNK // LANES), 1)
        groups = jnp.concatenate([groups_ref[l : l + 1, rows]] * 2, 1)
        allowed = keys == groups
        for j in range(local // LANES):
            q_cols, k_cols, v_cols = head_columns(j)
            query = both_heads(packed[l, rows, q_cols] * scale)
            scores = jnp.where(allowed, dot_nt(packed[l, :, k_cols], query), -1e9)
            expo = jnp.exp(scores - jnp.max(scores, 0, keepdims=True))
            low = (expo * (1.0 / jnp.sum(expo, 0, keepdims=True))).astype(BF)
            prob[l, 2 * j, :, rows] = low[:, :CHUNK]
            prob[l, 2 * j + 1, :, rows] = low[:, CHUNK:]
            mixed[l, rows, q_cols] = one_head(dot_tn(low, packed[l, :, v_cols])).astype(BF)

    def send_product(i, l, c, *pairs):
        total = 0.0
        for left, m in pairs:
            total = total + dot_nt(left(), weight(l, m))
        xs[c] = total.astype(BF)
        if i == AHEAD and c == 0:

            @pl.when(core == 1)
            def _():
                pl.semaphore_wait(token, 1)

        send(i, c)

    def attend_out(i, l, c):
        send_product(i, l, c, (lambda: mixed[l, chunk_rows(c)], O))

    def gather_norms(l):
        norms[l] = jnp.sum(flat_rows(full[PIECES][l]).reshape(nz * ny, 8, width), 0)

    def norm_of(l, which):
        return norms[l, which : which + 1], norms[l, 2 + which : 3 + which]

    def normalize(value):
        center = value - jnp.mean(value, -1, keepdims=True)
        inverse = lax.rsqrt(jnp.mean(center * center, -1, keepdims=True) + eps)
        return center * inverse, inverse

    def expand(i, l, c):
        rows = chunk_rows(c)
        arrive(i, c)
        gain, shift = norm_of(l, 0)

        def one(r):
            sub = sub_rows(c, r)
            normed, inverse = normalize(zin[l, sub].astype(F32) + both(i, c, r))
            norm1[l, sub] = normed
            roots[sub, l : l + 1] = inverse
            hid[l, sub] = (normed * gain + shift).astype(BF)

        each(CHUNK // SUB, one)

        for m in (UA, UB):
            for part in range(units // 2 // TILE):
                cols = slice(part * TILE, (part + 1) * TILE)
                pre = dot(hid[l, rows], flat_rows(full[m][l, :, :, :, cols]))
                lower = 0.5 + 0.5 * lax.erf(pre * 0.7071067811865476)
                density = jnp.exp(-0.5 * pre * pre) * 0.3989422804014327
                start = (m - UA) * units // 2 + part * TILE
                act[l, rows, start : start + TILE] = (pre * lower).astype(BF)
                slope[l, rows, start : start + TILE] = (lower + pre * density).astype(BF)

    def halves(ref, l, rows):
        low, high = slice(0, units // 2), slice(units // 2, units)
        return (lambda: ref[l, rows, low]), (lambda: ref[l, rows, high])

    def contract(i, l, c):
        low, high = halves(act, l, chunk_rows(c))
        send_product(i, l, c, (low, DA), (high, DB))

    def second_norm(i, l, c, r):
        sub = sub_rows(c, r)
        gain, shift = norm_of(l, 0)
        hidden = norm1[l, sub] * gain + shift
        return normalize(hidden + both(i, c, r))

    def norm_back(grad, normed, inverse, gain):
        scaled = grad * gain
        inner = (
            scaled
            - jnp.mean(scaled, -1, keepdims=True)
            - normed * jnp.mean(scaled * normed, -1, keepdims=True)
        )
        return inner * inverse

    def count(l, which, grad, normed):
        ng[l, which : which + 1] += jnp.sum(grad * normed, 0, keepdims=True)
        ng[l, 2 + which : 3 + which] += jnp.sum(grad, 0, keepdims=True)

    def top_back(l, c, r, grad, normed, inverse):
        sub = sub_rows(c, r)
        count(l, 1, grad, normed)
        back = norm_back(grad, normed, inverse, norm_of(l, 1)[0])
        gsum[sub] = back
        gtok[sub] = back.astype(BF)

    def expand_back(i, l, c):
        rows = chunk_rows(c)
        for m in (DA, DB):
            cols = slice((m - DA) * units // 2, (m - DA + 1) * units // 2)
            grad = dot(gtok[rows], flat_rows(full[m][l]))
            slope[l, rows, cols] = (grad * slope[l, rows, cols].astype(F32)).astype(BF)

        low, high = halves(slope, l, rows)
        send_product(i, l, c, (low, UA), (high, UB))

    def weight_grad(l, m, source, right, start=0):
        gather_drain(l, m)
        span = 2 * local if m == QK else full[m].shape[-1]
        grad = dot_tn(source[...], right[l, :, start : start + span]).astype(BF)
        grad = grad.reshape(nz, ny, block, span)
        if m == QK:
            full[m][l, :, :, 0] = grad[..., 0:local]
            full[m][l, :, :, 1] = grad[..., local:span]
        else:
            full[m][l] = grad
        sum_start(l, m)

    def attend_back(l):
        for j in range(local // LANES):
            q_cols, k_cols, v_cols = head_columns(j)
            grad = both_heads(gmix[:, q_cols])
            low = jnp.concatenate([prob[l, 2 * j], prob[l, 2 * j + 1]], 1)
            wide = low.astype(F32)
            product = wide * dot_nt(packed[l, :, v_cols], grad)
            total = jnp.sum(product, 0, keepdims=True)
            back = (product - wide * total).astype(BF)
            packed[l, :, v_cols] = dot(low, grad).astype(BF)
            g_key = dot(back, both_heads(packed[l, :, q_cols]))
            g_query = one_head(dot_tn(back, packed[l, :, k_cols]))
            packed[l, :, q_cols] = (g_query * scale).astype(BF)
            packed[l, :, k_cols] = (g_key * scale).astype(BF)

    def middle_back(i, l, c):
        rows = chunk_rows(c)
        arrive(i, c)

        def one(r):
            sub = sub_rows(c, r)
            grad = gsum[sub] + both(i, c, r)
            normed = norm1[l, sub]
            count(l, 0, grad, normed)
            back = norm_back(grad, normed, roots[sub, l : l + 1], norm_of(l, 0)[0])
            gsum[sub] = back
            gtok[sub] = back.astype(BF)

        each(CHUNK // SUB, one)
        gmix[rows] = dot(gtok[rows], flat_rows(full[O][l])).astype(BF)

    def project_back(i, l, c):
        rows = chunk_rows(c)
        send_product(
            i,
            l,
            c,
            (lambda: packed[l, rows, 0 : 2 * local], QK),
            (lambda: packed[l, rows, 2 * local : 3 * local], V),
        )


    barrier = pltpu.get_barrier_semaphore()
    peers = [to_x, to_core, to_y] + [to_z(k) for k in range(1, nz)]
    for peer in peers:
        pl.semaphore_signal(barrier, inc=1, device_id=peer, device_id_type=MESH)
    entry = [
        pltpu.make_async_copy(src, dst, local_sem.at[4 + i])
        for i, (src, dst) in enumerate(
            (
                (x_ref.at[core], zin.at[0]),
                (go_ref.at[core], gtop),
                (segs_ref, segs),
            )
        )
    ]
    first_rows, top_rows, id_rows = entry
    for copy in entry:
        copy.start()
    ng[...] = jnp.zeros_like(ng)
    vectors = jnp.zeros((8, width), F32)
    full[N][core, z, y] = vectors
    full[N][core, z, y, 0:2, 0:block] = gain_ref[0].astype(F32)
    full[N][core, z, y, 2:4, 0:block] = shift_ref[0].astype(F32)
    full[N][core, z, y] = pltpu.roll(full[N][core, z, y], place * block, 1)
    pl.semaphore_wait(barrier, len(peers))

    gather_own(0, QK, V, N, O)
    gather_far(0, QK, V)
    gather_own(0, UA, UB, DA, DB)
    id_rows.wait()
    row = segs[pl.ds(core, 1)]
    mapped = jnp.zeros_like(row)
    for i in range(partner_ref.shape[1]):
        mapped = jnp.where(row == i, partner_ref[core, i], mapped)
    groups_ref[0:1] = row.astype(F32)
    groups_ref[1:2] = mapped.astype(F32)
    keys_ref[...] = jnp.broadcast_to(row.astype(F32), (LANES, length)).T
    gather_pass(0, QK)
    gather_far(0, O, N)
    gather_cross(0, N)
    gather_pass(0, V)
    gather_far(0, UA)
    gather_pass(0, N, O)
    gather_far(0, UB)
    gather_late(0, QK, V, N, O)
    gather_end(0, QK, V, N)
    gather_own(1, QK, V, N, O, UA, UB, DA, DB)
    first_rows.wait()
    gather_norms(0)
    each(chunks, lambda c: project(0, c))
    attend(0, 0)
    gather_pass(0, UA)
    gather_far(0, DA)
    gather_end(0, O)
    attend_out(0, 0, 0)
    attend(0, 1)
    attend_out(0, 0, 1)
    gather_late(0, UA)
    gather_pass(0, UB)
    gather_far(0, DB)
    gather_cross(0, DB)
    gather_end(0, UA)
    gather_late(0, UB)
    gather_pass(0, DA)
    gather_end(0, UB)
    expand(0, 0, 0)
    gather_late(0, DA)
    gather_far(1, QK, V, N, O)
    gather_cross(1, N)
    gather_pass(0, DB)
    expand(0, 0, 1)
    gather_late(0, DB)
    gather_end(0, DA, DB)
    gather_far(1, UA)
    each(chunks, lambda c: contract(1, 0, c))

    def into_second(c):
        arrive(1, c)
        gain, shift = norm_of(0, 1)

        def one(r):
            sub = sub_rows(c, r)
            normed, inverse = second_norm(1, 0, c, r)
            norm2[sub] = normed.astype(BF)
            roots[sub, 2:3] = inverse
            zin[1, sub] = (normed * gain + shift).astype(BF)

        each(CHUNK // SUB, one)

    gather_pass(1, QK, V, N, O)
    gather_far(1, UB)
    into_second(0)
    gather_late(1, QK, V, N, O)
    gather_pass(1, UA)
    gather_far(1, DA)
    into_second(1)
    gather_late(1, UA)
    out_start(0, 0, zin.at[1], lo_ref)
    gather_end(1, QK, V, N)
    gather_norms(1)
    each(chunks, lambda c: project(1, c))
    gather_pass(1, UB)
    gather_far(1, DB)
    gather_cross(1, DB)
    attend(1, 0)
    gather_end(1, O)
    attend_out(2, 1, 0)
    gather_late(1, UB)
    gather_pass(1, DA)
    attend(1, 1)
    attend_out(2, 1, 1)
    gather_late(1, DA)
    gather_pass(1, DB)
    gather_end(1, UA, UB)
    expand(2, 1, 0)
    gather_late(1, DB)
    gather_end(1, DA, DB)
    contract(3, 1, 0)
    expand(2, 1, 1)
    contract(3, 1, 1)
    top_rows.wait()

    def over_top(c):
        arrive(3, c)
        if c == 0 and AHEAD == 3:

            @pl.when(core == 0)
            def _():
                pl.semaphore_signal(token, inc=1, device_id=to_core, device_id_type=MESH)

        gain, shift = norm_of(1, 1)

        def one(r):
            sub = sub_rows(c, r)
            normed, inverse = second_norm(3, 1, c, r)
            top_back(1, c, r, gtop[sub].astype(F32), normed, inverse)
            gtop[sub] = (normed * gain + shift).astype(BF)

        each(CHUNK // SUB, one)

    over_top(0)
    expand_back(4, 1, 0)
    over_top(1)
    expand_back(4, 1, 1)
    out_start(1, 1, gtop, lo_ref)
    weight_grad(1, DA, gtok, act)
    weight_grad(1, DB, gtok, act, units // 2)
    weight_grad(1, UA, hid.at[1], slope)
    weight_grad(1, UB, hid.at[1], slope, units // 2)
    middle_back(4, 1, 0)
    sum_first(1, DA)
    sum_first(1, DB)
    middle_back(4, 1, 1)
    attend_back(1)
    sum_first(1, UA)
    sum_first(1, UB)
    each(chunks, lambda c: project_back(5, 1, c))
    weight_grad(1, O, gtok, mixed)
    weight_grad(1, QK, zin.at[1], packed)
    weight_grad(1, V, zin.at[1], packed, 2 * local)
    vec_start(1)
    sum_second(1, DA)
    sum_second(1, DB)
    sum_first(1, O)
    sum_first(1, QK)
    sum_first(1, V)

    def under(c):
        arrive(5, c)

        def one(r):
            sub = sub_rows(c, r)
            low = (gsum[sub] + both(5, c, r)).astype(BF)
            gin[sub] = low
            top_back(0, c, r, low.astype(F32), norm2[sub].astype(F32), roots[sub, 2:3])

        each(CHUNK // SUB, one)
        expand_back(6, 0, c)

    under(0)
    sum_second(1, UA)
    sum_second(1, UB)
    under(1)
    out_start(1, 3, gin, ig_ref)
    weight_grad(0, DA, gtok, act)
    weight_grad(0, DB, gtok, act, units // 2)
    weight_grad(0, UA, hid.at[0], slope)
    weight_grad(0, UB, hid.at[0], slope, units // 2)
    sum_relay(1, DA)
    sum_relay(1, DB)
    vec_first(1)
    sum_first(0, DA)
    middle_back(6, 0, 0)
    sum_first(0, DB)
    sum_relay(1, UA)
    sum_relay(1, UB)
    sum_second(1, O)
    sum_second(1, QK)
    sum_second(1, V)
    middle_back(6, 0, 1)
    sum_first(0, UA)
    attend_back(0)
    sum_second(0, DA)
    each(chunks, lambda c: project_back(7, 0, c))
    sum_first(0, UB)
    weight_grad(0, O, gtok, mixed)
    weight_grad(0, QK, zin.at[0], packed)
    weight_grad(0, V, zin.at[0], packed, 2 * local)
    vec_start(0)
    sum_relay(1, O)
    sum_relay(1, QK)
    sum_relay(1, V)
    vec_second(1)
    sum_second(0, DB)
    sum_relay(0, DA)
    sum_first(0, O)
    sum_first(0, QK)
    sum_first(0, V)
    vec_first(0)
    sum_second(0, UA)
    sum_relay(0, DB)

    def bottom(c):
        arrive(7, c)

        def one(r):
            sub = sub_rows(c, r)
            gtop[sub] = (gsum[sub] + both(7, c, r)).astype(BF)

        each(CHUNK // SUB, one)

    out_wait(1, 1, gtop, lo_ref)
    bottom(0)
    sum_second(0, UB)
    sum_relay(0, UA)
    bottom(1)
    out_start(0, 2, gtop, ig_ref)
    sum_second(0, O)
    sum_second(0, QK)
    sum_relay(0, UB)
    sum_second(0, V)
    vec_second(0)
    sum_relay(0, O)
    sum_relay(0, QK)
    sum_relay(0, V)
    for l in (1, 0):
        for m in (DA, DB, UA, UB, O, QK, V):
            sum_last(l, m)
        vec_last(l)
    for l in range(2):
        for m in range(PIECES):
            sum_drain(l, m)
        vec_drain(l)
        gather_drain(l, N)
    for m in range(PIECES):
        result_out(m).wait()
    norm_out().wait()
    out_wait(0, 0, zin.at[1], lo_ref)
    out_wait(0, 2, gtop, ig_ref)
    out_wait(1, 3, gin, ig_ref)


def fused(sizes, x, grad, segments, partner, gains, shifts, shards_in):
    nz, ny, length, width, local, units, eps, scale = sizes
    block = width // (nz * ny)
    chunks = length // CHUNK
    tiles = ((2, block, local),) + ((block, local),) * 2 + ((block, units // 2),) * 4
    dma = pltpu.SemaphoreType.DMA
    vmem = pltpu.VMEM
    scratch = [vmem((2, nz, ny) + tile, BF) for tile in tiles]
    scratch += [vmem((2, nz, ny, 8, width), F32)]
    scratch += [vmem((nz, ny) + tile, BF) for tile in tiles]
    scratch += [vmem((nz,) + tile, BF) for tile in tiles]
    scratch += [vmem((nz,) + tile, BF) for tile in tiles]
    scratch += [vmem(tile, F32) for tile in tiles]
    scratch += [
        vmem((length, LANES), F32),
        vmem((2, length), F32),
        vmem((2, length), jnp.int32),
        vmem((8, LANES), F32),
        vmem((8, width), F32),
        vmem((8, width), F32),
        vmem((nz - 1, 8, width), F32),
        vmem((4, 8, width), F32),
        vmem((2, length, width), BF),
        vmem((2, length, 3 * local), BF),
        vmem((2, local // HEAD, length, length), BF),
        vmem((2, length, local), BF),
        vmem((2, length, width), F32),
        vmem((2, length, width), BF),
        vmem((2, length, units), BF),
        vmem((2, length, units), BF),
        vmem((length, width), BF),
        vmem((length, 4), F32),
        vmem((length, width), F32),
        vmem((length, width), BF),
        vmem((length, local), BF),
        vmem((length, width), BF),
        vmem((length, width), BF),
        vmem((2, 8, width), F32),
        vmem((chunks, CHUNK, width), BF),
        vmem((2, chunks, CHUNK, width), BF),
        pltpu.SemaphoreType.REGULAR,
        dma((10,)),
        dma((PIECES,)),
        dma((PIECES,)),
        dma((4,)),
        dma((4,)),
        dma((chunks,)),
        dma((2, chunks)),
        dma((PIECES + 1, 2, nz)),
        dma((PIECES + 1, 2, nz)),
        dma((PIECES + 1, nz)),
        dma((PIECES + 1, nz)),
        dma((PIECES + 1, 2 * nz)),
        dma((PIECES + 1, 2 * nz)),
        dma((PIECES + 1, 2)),
        dma((PIECES + 1, 2)),
        dma((PIECES + 1, nz)),
        dma((PIECES + 1, nz)),
        dma((PIECES + 1, nz - 1)),
        dma((PIECES + 1, nz)),
    ]
    anywhere = pl.BlockSpec(memory_space=pl.ANY)
    inside = pl.BlockSpec(memory_space=pltpu.VMEM)
    outs = (
        ((2, length, width), BF),
        ((2, length, width), BF),
        ((3, block, local), F32),
        ((block, local), F32),
        ((block, units), F32),
        ((block, units), F32),
        ((8, LANES), F32),
    )
    return pl.pallas_call(
        functools.partial(kernel, sizes),
        out_shape=[jax.ShapeDtypeStruct(*out) for out in outs],
        in_specs=[pl.BlockSpec(memory_space=pltpu.SMEM)] + [inside] * 2 + [anywhere] * 7,
        out_specs=[anywhere] * len(outs),
        scratch_shapes=scratch,
        compiler_params=pltpu.CompilerParams(
            collective_id=0, has_side_effects=True, vmem_limit_bytes=127 << 19
        ),
    )(partner, gains, shifts, x, grad, segments, *shards_in)


def place_results(*refs):
    count = (len(refs) - 2) // 3
    srcs, dsts, held = refs[:count], refs[count : 2 * count], refs[2 * count : 3 * count]
    into, out = refs[3 * count :]
    for i in range(count):
        pltpu.make_async_copy(srcs[i], held[i], into.at[i]).start()
    for i in range(count):
        pltpu.make_async_copy(srcs[i], held[i], into.at[i]).wait()
        pltpu.make_async_copy(held[i], dsts[i], out.at[i]).start()
    for i in range(count):
        pltpu.make_async_copy(held[i], dsts[i], out.at[i]).wait()


def placed_results(*items):
    dma = pltpu.SemaphoreType.DMA
    anywhere = pl.BlockSpec(memory_space=pl.ANY)
    return pl.pallas_call(
        place_results,
        out_shape=[jax.ShapeDtypeStruct(item.shape, item.dtype) for item in items],
        in_specs=[anywhere] * len(items),
        out_specs=[anywhere] * len(items),
        scratch_shapes=[pltpu.VMEM(item.shape, item.dtype) for item in items]
        + [dma((len(items),)), dma((len(items),))],
        compiler_params=pltpu.CompilerParams(vmem_limit_bytes=127 << 19),
    )(*items)


def kernel_shards(
    inputs, segments, partner, grad_output, w_qkv, w_out, w_up, w_down, norm_gain, norm_shift
):
    parts = lax.axis_size("dp")
    length, width = inputs.shape[1:]
    local, units = w_out.shape[1], w_up.shape[2]
    block = width // parts
    sizes = (parts // 2, 2, length, width, local, units, norm_eps, score_scale)
    shards_in = (w_qkv[0].transpose(1, 0, 2), w_out[0].T, w_up[0], w_down[0].T)
    outs = fused(
        sizes, inputs, grad_output, segments, partner, norm_gain, norm_shift, shards_in
    )
    *whole, norm = outs
    layer_outputs, input_grads, g_qkv, g_out, g_up, g_down = placed_results(*whole)
    return (
        layer_outputs[None],
        input_grads[None],
        g_qkv.transpose(1, 0, 2)[None],
        g_out.T[None],
        g_up[None],
        g_down.T[None],
        norm[None, 0:2, 0:block],
        norm[None, 2:4, 0:block],
    )


def solution(mesh):
    placed = (
        P("dp", None, None),
        P("dp", None),
        P("dp", None),
        P("dp", None, None),
        P("section", "dp", None, "tensor"),
        P("section", "tensor", "dp"),
        P("section", "dp", "tensor"),
        P("section", "tensor", "dp"),
        P("section", None, "dp"),
        P("section", None, "dp"),
    )
    block = WIDTH // mesh.shape["dp"]
    whole_tiles = block * mesh.shape["dp"] == WIDTH and block % 16 == 0
    return jax.shard_map(
        kernel_shards if whole_tiles else shards,
        mesh=mesh,
        in_specs=placed,
        out_specs=(
            P("section", "dp", None, None),
            P("section", "dp", None, None),
            P("section", "dp", None, "tensor"),
            P("section", "tensor", "dp"),
            P("section", "dp", "tensor"),
            P("section", "tensor", "dp"),
            P("section", None, "dp"),
            P("section", None, "dp"),
        ),
        check_vma=False,
    )
```

```python
import functools

import jax
import jax.numpy as jnp
from jax import lax
from jax.experimental import pallas as pl
from jax.experimental.pallas import tpu as pltpu
from jax.sharding import PartitionSpec as P

HEAD = 64
WIDTH = 768


norm_eps = 1e-06
score_scale = 0.125
masked_value = -1000000000.0


def partner_of(segment_ids, partner):
    table = jnp.arange(partner.shape[-1], dtype=jnp.int32)
    hits = segment_ids[..., None] == table
    return jnp.sum(jnp.where(hits, partner[None, :], 0), -1)


def layer_norm(values, gain, shift):
    center = values - jnp.mean(values, -1, keepdims=True)
    inverse = lax.rsqrt(jnp.mean(center * center, -1, keepdims=True) + norm_eps)
    normed = center * inverse
    return (normed * gain + shift, normed, inverse)


def norm_back(grad, normed, inverse, gain):
    scaled = grad * gain
    inner = (
        scaled
        - jnp.mean(scaled, -1, keepdims=True)
        - normed * jnp.mean(scaled * normed, -1, keepdims=True)
    )
    return inner * inverse


def gelu_slope(values):
    lower = 0.5 * (1.0 + lax.erf(values * 0.7071067811865476))
    density = jnp.exp(-0.5 * values * values) * 0.3989422804014327
    return lower + values * density


def swapped(value, axis):
    size = lax.axis_size(axis)
    return lax.ppermute(value, axis, [(i, size - 1 - i) for i in range(size)])


def tensor_sum(partial_value):
    low = partial_value.astype(jnp.bfloat16)
    return low.astype(jnp.float32) + swapped(low, "tensor").astype(jnp.float32)


def masked_scores(query, key, query_groups, key_groups):
    scores = (
        jnp.einsum("qhd,khd->hqk", query, key, preferred_element_type=jnp.float32) * score_scale
    )
    allowed = query_groups[:, None] == key_groups[None, :]
    return jnp.where(allowed[None], scores, masked_value)


def attend(query, key, value, query_groups, key_groups):
    scores = masked_scores(query, key, query_groups, key_groups)
    top = jnp.max(scores, -1, keepdims=True)
    expo = jnp.exp(scores - top)
    total = jnp.sum(expo, -1, keepdims=True)
    probs = (expo / total).astype(jnp.bfloat16)
    mixed = jnp.einsum("hqk,khd->qhd", probs, value, preferred_element_type=jnp.float32)
    return (mixed.astype(jnp.bfloat16), (top + jnp.log(total))[..., 0])


def attend_back(query, key, value, query_groups, key_groups, spread, grad_mixed):
    scores = masked_scores(query, key, query_groups, key_groups)
    probs = jnp.exp(scores - spread[..., None])
    probs_low = probs.astype(jnp.bfloat16)
    grad_probs = jnp.einsum("qhd,khd->hqk", grad_mixed, value, preferred_element_type=jnp.float32)
    grad_value = jnp.einsum(
        "hqk,qhd->khd", probs_low, grad_mixed, preferred_element_type=jnp.float32
    )
    row_dot = jnp.sum(probs * grad_probs, -1, keepdims=True)
    grad_scores = (probs * (grad_probs - row_dot)).astype(jnp.bfloat16)
    grad_query = (
        jnp.einsum("hqk,khd->qhd", grad_scores, key, preferred_element_type=jnp.float32)
        * score_scale
    )
    grad_key = (
        jnp.einsum("hqk,qhd->khd", grad_scores, query, preferred_element_type=jnp.float32)
        * score_scale
    )
    return jnp.stack(
        [
            grad_query.astype(jnp.bfloat16),
            grad_key.astype(jnp.bfloat16),
            grad_value.astype(jnp.bfloat16),
        ],
        1,
    )


def layer_forward(flat, weights, query_groups, key_groups):
    w_qkv, w_out, w_up, w_down, gains, shifts = weights
    length = flat.shape[0]
    local = w_qkv.shape[2]
    packed = jnp.einsum("nd,dcm->ncm", flat, w_qkv, preferred_element_type=jnp.float32).astype(
        jnp.bfloat16
    )
    heads = packed.reshape(length, 3, local // HEAD, HEAD)
    mixed, spread = attend(heads[:, 0], heads[:, 1], heads[:, 2], query_groups, key_groups)
    mixed_flat = mixed.reshape(length, local)
    attn_out = tensor_sum(jnp.dot(mixed_flat, w_out, preferred_element_type=jnp.float32))
    hidden, normed_first, inverse_first = layer_norm(
        flat.astype(jnp.float32) + attn_out, gains[0], shifts[0]
    )
    hidden_low = hidden.astype(jnp.bfloat16)
    pre = jnp.dot(hidden_low, w_up, preferred_element_type=jnp.float32)
    act = jax.nn.gelu(pre, approximate=False).astype(jnp.bfloat16)
    ffn_out = tensor_sum(jnp.dot(act, w_down, preferred_element_type=jnp.float32))
    result, normed_second, inverse_second = layer_norm(hidden + ffn_out, gains[1], shifts[1])
    kept = (
        flat,
        heads,
        spread,
        mixed_flat,
        normed_first,
        inverse_first,
        hidden_low,
        pre,
        act,
        normed_second,
        inverse_second,
    )
    return (result.astype(jnp.bfloat16), kept)


def layer_backward(grad_result, kept, weights, query_groups, key_groups):
    w_qkv, w_out, w_up, w_down, gains, shifts = weights
    (
        flat,
        heads,
        spread,
        mixed_flat,
        normed_first,
        inverse_first,
        hidden_low,
        pre,
        act,
        normed_second,
        inverse_second,
    ) = kept
    length = flat.shape[0]
    local = w_qkv.shape[2]
    gain_second = jnp.sum(grad_result * normed_second, 0)
    shift_second = jnp.sum(grad_result, 0)
    grad_sum2 = norm_back(grad_result, normed_second, inverse_second, gains[1])
    grad_ffn = grad_sum2.astype(jnp.bfloat16)
    grad_down = jnp.einsum("nf,nd->fd", act, grad_ffn, preferred_element_type=jnp.float32)
    grad_act = jnp.einsum("nd,fd->nf", grad_ffn, w_down, preferred_element_type=jnp.float32)
    grad_pre = (grad_act * gelu_slope(pre)).astype(jnp.bfloat16)
    grad_up = jnp.einsum("nd,nf->df", hidden_low, grad_pre, preferred_element_type=jnp.float32)
    grad_hidden = grad_sum2 + tensor_sum(
        jnp.einsum("nf,df->nd", grad_pre, w_up, preferred_element_type=jnp.float32)
    )
    gain_first = jnp.sum(grad_hidden * normed_first, 0)
    shift_first = jnp.sum(grad_hidden, 0)
    grad_resid = norm_back(grad_hidden, normed_first, inverse_first, gains[0])
    grad_attn = grad_resid.astype(jnp.bfloat16)
    grad_out = jnp.einsum("nm,nd->md", mixed_flat, grad_attn, preferred_element_type=jnp.float32)
    grad_mixed = jnp.einsum(
        "nd,md->nm", grad_attn, w_out, preferred_element_type=jnp.float32
    ).astype(jnp.bfloat16)
    grad_mixed = grad_mixed.reshape(length, local // HEAD, HEAD)
    grad_heads = attend_back(
        heads[:, 0], heads[:, 1], heads[:, 2], query_groups, key_groups, spread, grad_mixed
    )
    grad_packed = grad_heads.reshape(length, 3, local)
    grad_qkv = jnp.einsum("nd,ncm->dcm", flat, grad_packed, preferred_element_type=jnp.float32)
    grad_input = grad_resid + tensor_sum(
        jnp.einsum("ncm,dcm->nd", grad_packed, w_qkv, preferred_element_type=jnp.float32)
    )
    grads = (
        grad_qkv.astype(jnp.bfloat16),
        grad_out.astype(jnp.bfloat16),
        grad_up.astype(jnp.bfloat16),
        grad_down.astype(jnp.bfloat16),
        jnp.stack([gain_first, gain_second]),
        jnp.stack([shift_first, shift_second]),
    )
    return (grads, grad_input.astype(jnp.bfloat16))


def shards(
    inputs, segments, partner, grad_output, w_qkv, w_out, w_up, w_down, norm_gain, norm_shift
):
    core = lax.axis_index("section")
    rows = inputs.shape[0] // lax.axis_size("section")

    def per_row(row):
        key_groups = lax.dynamic_index_in_dim(segments, row, 0, False)
        mapped = partner_of(key_groups, lax.dynamic_index_in_dim(partner, row, 0, False))
        flat = lax.dynamic_index_in_dim(inputs, row, 0, False)
        first, kept_first = layer_forward(flat, layers[0], key_groups, key_groups)
        second, kept_second = layer_forward(first, layers[1], mapped, key_groups)
        grad_top = lax.dynamic_index_in_dim(grad_output, row, 0, False).astype(jnp.float32)
        grads_second, grad_mid = layer_backward(
            grad_top, kept_second, layers[1], mapped, key_groups
        )
        grads_first, grad_low = layer_backward(
            grad_mid.astype(jnp.float32), kept_first, layers[0], key_groups, key_groups
        )
        return (first, second, grad_low, grad_mid, grads_first, grads_second)

    def gathered(shard, axis):
        own = lax.all_gather(shard[0], "dp", axis=axis, tiled=True)
        other = swapped(own, "section")
        return (jnp.where(core == 0, own, other), jnp.where(core == 0, other, own))

    pairs = [
        gathered(w_qkv, 0),
        gathered(w_out, 1),
        gathered(w_up, 0),
        gathered(w_down, 1),
        gathered(norm_gain, 1),
        gathered(norm_shift, 1),
    ]
    layers = [
        [pair[layer].astype(jnp.float32) if place > 3 else pair[layer] for place, pair in enumerate(pairs)]
        for layer in range(2)
    ]
    done = [per_row(core * rows + step) for step in range(rows)]

    def summed(first, second, axis):
        mine = jnp.where(core == 0, first, second)
        away = jnp.where(core == 0, second, first)
        both = mine.astype(jnp.float32) + swapped(away, "section").astype(jnp.float32)
        return lax.psum_scatter(both.astype(first.dtype), "dp", scatter_dimension=axis, tiled=True).astype(jnp.float32)

    def total(layer, place):
        value = done[0][4 + layer][place]
        for item in done[1:]:
            value = (value.astype(jnp.float32) + item[4 + layer][place].astype(jnp.float32)).astype(value.dtype)
        return value

    axes = (0, 1, 0, 1, 1, 1)
    sums = [summed(total(0, place), total(1, place), axis) for place, axis in enumerate(axes)]

    def regrouped(first, second):
        mine = jnp.where(core == 0, first, second)
        other = swapped(jnp.where(core == 0, second, first), "section")
        return jnp.where(
            core == 0, jnp.concatenate([mine, other]), jnp.concatenate([other, mine])
        )

    layer_outputs = regrouped(
        jnp.stack([item[0] for item in done]), jnp.stack([item[1] for item in done])
    )
    input_grads = regrouped(
        jnp.stack([item[2] for item in done]), jnp.stack([item[3] for item in done])
    )
    return (layer_outputs[None], input_grads[None]) + tuple(value[None] for value in sums)


MESH = pl.DeviceIdType.MESH
BF = jnp.bfloat16
F32 = jnp.float32
CHUNK = 256
SUB = 256
TILE = 256
LANES = 128
QK, V, O, UA, UB, DA, DB, N = range(8)
PIECES = N
AHEAD = -1
Y_FIRST = (DB, N)
NT = (((1,), (1,)), ((), ()))
TN = (((0,), (0,)), ((), ()))


def dot(left, right):
    return jnp.dot(left, right, preferred_element_type=F32)


def dot_nt(left, right):
    return lax.dot_general(left, right, NT, preferred_element_type=F32)


def dot_tn(left, right):
    return lax.dot_general(left, right, TN, preferred_element_type=F32)


def flat_rows(value):
    return value.reshape(-1, value.shape[-1])


def kernel(
    sizes,
    partner_ref,
    gain_ref,
    shift_ref,
    x_ref,
    go_ref,
    segs_ref,
    sq,
    so,
    su,
    sd,
    lo_ref,
    ig_ref,
    oq,
    oo,
    ou,
    od,
    on,
    *refs,
):
    nz, ny, length, width, local, units, eps, scale = sizes
    block = width // (nz * ny)
    full, refs = refs[: PIECES + 1], refs[PIECES + 1 :]
    summed, refs = refs[:PIECES], refs[PIECES:]
    from_y, refs = refs[:PIECES], refs[PIECES:]
    from_z, refs = refs[:PIECES], refs[PIECES:]
    result, refs = refs[:PIECES], refs[PIECES:]
    (
        keys_ref,
        groups_ref,
        segs,
        out_norm,
        rn,
        yn,
        vn,
        ng,
        zin,
        packed,
        prob,
        mixed,
        norm1,
        hid,
        act,
        slope,
        norm2,
        roots,
        gsum,
        gtok,
        gmix,
        gtop,
        gin,
        norms,
        xs,
        xr,
        token,
        local_sem,
        own_sem,
        done_sem,
        out_send,
        out_recv,
        xs_sem,
        xr_sem,
        az_s,
        az_r,
        ay_s,
        ay_r,
        ac_s,
        ac_r,
        gc_s,
        gc_r,
        gy_s,
        gy_r,
        gz_s,
        gz_r,
    ) = refs
    chunks = length // CHUNK
    core = lax.axis_index("section")
    place = lax.axis_index("dp")
    side = lax.axis_index("tensor")
    z, y = place // ny, lax.rem(place, ny)
    other_y = 1 - y
    to_x = {"tensor": 1 - side}
    to_core = {"section": 1 - core}
    to_y = {"dp": z * ny + other_y}

    def turn(k):
        return lax.rem(z + k + nz, nz)

    def to_z(k):
        return {"dp": turn(k) * ny + y}

    half = units // 2
    shard = {
        QK: sq.at[0:2],
        V: sq.at[2],
        O: so,
        UA: su.at[:, 0:half],
        UB: su.at[:, half:units],
        DA: sd.at[:, 0:half],
        DB: sd.at[:, half:units],
    }
    target = {
        QK: oq.at[0:2],
        V: oq.at[2],
        UA: ou.at[:, 0:half],
        UB: ou.at[:, half:units],
        O: oo,
        DA: od.at[:, 0:half],
        DB: od.at[:, half:units],
    }

    def remote(src, dst, send, recv, target):
        return pltpu.make_async_remote_copy(
            src_ref=src,
            dst_ref=dst,
            send_sem=send,
            recv_sem=recv,
            device_id=target,
            device_id_type=MESH,
        )

    def each(count, body):
        lax.fori_loop(0, count, lambda i, none: (body(i), none)[1], 0)

    at_end = jnp.logical_or(z == 0, z == nz - 1)
    middle = jnp.logical_not(at_end)
    far_end = jnp.where(z < nz // 2, 0, nz - 1)
    far_origin = nz - 1 - far_end
    near_z = {"dp": jnp.where(z == 0, 1, nz - 2) * ny + y}
    end_z = {"dp": far_end * ny + y}

    def is_far(k):
        return jnp.logical_or(
            jnp.logical_and(z == 0, k == nz - 1), jnp.logical_and(z == nz - 1, k == 1)
        )

    def is_late(k):
        return jnp.logical_or(
            jnp.logical_and(z == 0, k == 1), jnp.logical_and(z == nz - 1, k == nz - 1)
        )

    def offsets(body):
        lax.fori_loop(1, nz, lambda k, none: (body(k), none)[1], 0)


    def column(c):
        return (y, other_y)[c]

    def lines(m):
        return (0, 1) if m in Y_FIRST else (0,)

    def gather_z(l, m, k, c, src=None):
        ref = full[m].at[l, z, column(c)]
        return remote(
            ref if src is None else src,
            ref,
            az_s.at[m, c, k - 1],
            az_r.at[m, c, k - 1],
            to_z(k),
        )

    def gather_relay(l, m, c):
        ref = full[m].at[l, far_origin, column(c)]
        slot = jnp.where(z == 1, 0, nz - 2)
        return remote(ref, ref, az_s.at[m, c, nz - 1], az_r.at[m, c, slot], end_z)

    def gather_y(l, m, k, src=None):
        ref = full[m].at[l, turn(-k), y]
        return remote(ref if src is None else src, ref, ay_s.at[m, k], ay_r.at[m, k], to_y)

    def gather_core(l, m, k, c, src=None):
        ref = full[m].at[l, turn(-k), column(c)]
        slot = k + c * nz
        return remote(
            ref if src is None else src, ref, ac_s.at[m, slot], ac_r.at[m, slot], to_core
        )

    def own_copy(l, m):
        return pltpu.make_async_copy(shard[m], full[m].at[l, z, y], own_sem.at[m])

    def gather_own(l, *mats):
        @pl.when(core == l)
        def _():
            for m in mats:
                if m in shard:
                    own_copy(l, m).start()
                gather_y(l, m, 0, shard.get(m)).start()
                gather_core(l, m, 0, 0, shard.get(m)).start()

    def gather_far(l, *mats):
        @pl.when(core == l)
        def _():
            for m in mats:

                def one(k):
                    @pl.when(jnp.logical_not(is_far(k)))
                    def _():
                        gather_z(l, m, k, 0, shard.get(m)).start()

                offsets(one)

    def gather_cross(l, *mats):
        @pl.when(core == l)
        def _():
            for m in mats:
                gather_y(l, m, 0).wait_recv()
                gather_core(l, m, 0, 1).start()

                def one(k):
                    @pl.when(jnp.logical_not(is_far(k)))
                    def _():
                        gather_z(l, m, k, 1).start()

                offsets(one)

    def gather_hand(l, m, k, c):
        gather_z(l, m, k, c).wait_recv()
        gather_core(l, m, k, c).start()
        if m not in Y_FIRST:
            gather_y(l, m, k).start()

    def gather_pass(l, *mats):
        @pl.when(core == l)
        def _():
            for m in mats:
                for c in lines(m):

                    def one(k):
                        @pl.when(jnp.logical_not(is_late(k)))
                        def _():
                            gather_hand(l, m, k, c)

                        @pl.when(jnp.logical_and(middle, k == nz // 2))
                        def _():
                            gather_relay(l, m, c).start()

                    offsets(one)

    def gather_late(l, *mats):
        @pl.when(jnp.logical_and(core == l, at_end))
        def _():
            for m in mats:
                for c in lines(m):
                    gather_hand(l, m, jnp.where(z == 0, 1, nz - 1), c)

    def gather_near(l, m):
        @pl.when(core != l)
        def _():
            each(nz, lambda k: gather_core(l, m, k, 0).wait_recv())

    def gather_end(l, *mats, near=True):
        @pl.when(core == l)
        def _():
            for m in mats:
                if m in shard:
                    own_copy(l, m).wait()
                if m not in Y_FIRST:

                    def one(k):
                        gather_y(l, m, k).wait_recv()
                        gather_core(l, m, k, 1).start()

                    each(nz, one)

        for m in mats:
            if near:
                gather_near(l, m)

        @pl.when(core != l)
        def _():
            for m in mats:
                each(nz, lambda k: gather_core(l, m, k, 1).wait_recv())

    def gather_drain(l, m):
        @pl.when(core == l)
        def _():
            for c in lines(m):

                def one(k):
                    @pl.when(jnp.logical_not(is_far(k)))
                    def _():
                        gather_z(l, m, k, c).wait_send()

                offsets(one)

                @pl.when(middle)
                def _():
                    gather_relay(l, m, c).wait_send()

            gather_y(l, m, 0).wait_send()
            if m not in Y_FIRST:
                offsets(lambda k: gather_y(l, m, k).wait_send())

            def core_sent(k):
                gather_core(l, m, k, 0).wait_send()
                gather_core(l, m, k, 1).wait_send()

            each(nz, core_sent)


    def sum_core(l, m, part):
        column = (other_y, y)[part]
        return remote(
            full[m].at[l, :, column],
            summed[m].at[:, column],
            gc_s.at[m, part],
            gc_r.at[m, part],
            to_core,
        )

    def sum_y(l, m, k):
        return remote(
            full[m].at[l, k, other_y], from_y[m].at[k], gy_s.at[m, k], gy_r.at[m, k], to_y
        )

    def sum_z(l, m, k):
        return remote(
            full[m].at[l, turn(k), y],
            from_z[m].at[k - 1],
            gz_s.at[m, k - 1],
            gz_r.at[m, k - 1],
            to_z(k),
        )

    def sum_near(l, m, k):
        return remote(
            full[m].at[l, turn(k), y],
            from_z[m].at[nz - 1],
            gz_s.at[m, k - 1],
            gz_r.at[m, nz - 1],
            near_z,
        )

    def sum_start(l, m):
        @pl.when(core != l)
        def _():
            sum_core(l, m, 0).start()
            sum_core(l, m, 1).start()

    def sum_first(l, m):
        @pl.when(core == l)
        def _():
            sum_core(l, m, 0).wait_recv()

            def one(k):
                both = full[m][l, k, other_y].astype(F32) + summed[m][k, other_y].astype(F32)
                full[m][l, k, other_y] = both.astype(BF)
                sum_y(l, m, k).start()

            each(nz, one)

    def sum_second(l, m):
        @pl.when(core == l)
        def _():
            sum_core(l, m, 1).wait_recv()

            def total(k):
                at = turn(k)
                sum_y(l, m, at).wait_recv()
                both = full[m][l, at, y].astype(F32) + summed[m][at, y].astype(F32)
                return both + from_y[m][at].astype(F32)

            def one(k):
                full[m][l, turn(k), y] = total(k).astype(BF)
                far = is_far(k)
                held = jnp.logical_and(middle, k == nz // 2)

                @pl.when(far)
                def _():
                    sum_near(l, m, k).start()

                @pl.when(jnp.logical_not(jnp.logical_or(far, held)))
                def _():
                    sum_z(l, m, k).start()

            offsets(one)
            result[m][...] = total(0)

    def sum_relay(l, m):
        @pl.when(jnp.logical_and(core == l, middle))
        def _():
            k = nz // 2
            sum_near(l, m, k).wait_recv()
            both = full[m][l, turn(k), y].astype(F32) + from_z[m][nz - 1].astype(F32)
            full[m][l, turn(k), y] = both.astype(BF)
            sum_z(l, m, k).start()

    def sum_last(l, m):
        @pl.when(core == l)
        def _():
            def one(k):
                @pl.when(jnp.logical_not(is_late(k)))
                def _():
                    sum_z(l, m, k).wait_recv()
                    result[m][...] += from_z[m][k - 1].astype(F32)

            offsets(one)
            result_out(m).start()

    def result_out(m):
        return pltpu.make_async_copy(result[m], target[m], done_sem.at[m])

    def sum_drain(l, m):
        @pl.when(core != l)
        def _():
            sum_core(l, m, 0).wait_send()
            sum_core(l, m, 1).wait_send()

        @pl.when(core == l)
        def _():
            each(nz, lambda k: sum_y(l, m, k).wait_send())
            offsets(lambda k: sum_z(l, m, k).wait_send())


    def vec_core(l):
        return remote(ng.at[l], rn, gc_s.at[PIECES, 0], gc_r.at[PIECES, 0], to_core)

    def vec_y(l):
        return remote(ng.at[2], yn, gy_s.at[PIECES, 0], gy_r.at[PIECES, 0], to_y)

    def vec_z(l, k):
        return remote(
            ng.at[3], vn.at[k - 1], gz_s.at[PIECES, k - 1], gz_r.at[PIECES, k - 1], to_z(k)
        )

    def vec_start(l):
        @pl.when(core != l)
        def _():
            vec_core(l).start()

    def vec_first(l):
        @pl.when(core == l)
        def _():
            vec_core(l).wait_recv()
            ng[2] = ng[l] + rn[...]
            vec_y(l).start()

    def vec_second(l):
        @pl.when(core == l)
        def _():
            vec_y(l).wait_recv()
            ng[3] = ng[2] + yn[...]
            for k in range(1, nz):
                vec_z(l, k).start()

    def vec_last(l):
        @pl.when(core == l)
        def _():
            total = ng[3]
            for k in range(1, nz):
                vec_z(l, k).wait_recv()
                total = total + vn[k - 1]
            turned = pltpu.roll(total, lax.rem(place * -block + width, width), 1)
            out_norm[...] = turned[:, 0:LANES]
            norm_out().start()

    def norm_out():
        return pltpu.make_async_copy(out_norm, on, local_sem.at[9])

    def vec_drain(l):
        @pl.when(core != l)
        def _():
            vec_core(l).wait_send()

        @pl.when(core == l)
        def _():
            vec_y(l).wait_send()
            for k in range(1, nz):
                vec_z(l, k).wait_send()


    def exchange(i, c):
        return remote(xs.at[c], xr.at[i % 2, c], xs_sem.at[c], xr_sem.at[i % 2, c], to_x)

    def send(i, c):
        exchange(i, c).start()

    def arrive(i, c):
        exchange(i, c).wait()

    def both(i, c, r):
        rows = pl.ds(r * SUB, SUB)
        return xs[c, rows].astype(F32) + xr[i % 2, c, rows].astype(F32)

    def chunk_rows(c):
        return pl.ds(pl.multiple_of(c * CHUNK, CHUNK), CHUNK)

    def sub_rows(c, r):
        return pl.ds(pl.multiple_of(c * CHUNK + r * SUB, SUB), SUB)

    def columns(j, span):
        return pl.ds(pl.multiple_of(j * span, LANES), span)


    def out_copy(l, which, src, dst):
        def away():
            return remote(src, dst.at[core], out_send.at[which], out_recv.at[which], to_core)

        def here():
            return pltpu.make_async_copy(src, dst.at[core], local_sem.at[which])

        return here, away

    def out_start(l, which, src, dst):
        here, away = out_copy(l, which, src, dst)

        @pl.when(core == l)
        def _():
            here().start()

        @pl.when(core != l)
        def _():
            away().start()

    def out_wait(l, which, src, dst):
        here, away = out_copy(l, which, src, dst)

        @pl.when(core == l)
        def _():
            here().wait()
            remote(
                src, dst.at[1 - core], out_send.at[which], out_recv.at[which], to_core
            ).wait_recv()

        @pl.when(core != l)
        def _():
            away().wait_send()


    def weight(l, m):
        if m == QK:
            pair = full[m][l, :, :, 0], full[m][l, :, :, 1]
            return jnp.concatenate([flat_rows(one) for one in pair], 1)
        return flat_rows(full[m][l])

    def project(l, c):
        rows = chunk_rows(c)
        for m, span in ((QK, slice(0, 2 * local)), (V, slice(2 * local, 3 * local))):
            packed[l, rows, span] = dot(zin[l, rows], weight(l, m)).astype(BF)

    low_lane = lax.broadcasted_iota(jnp.int32, (1, LANES), 1) < LANES // 2

    def both_heads(value):
        none = jnp.zeros_like(value)
        return jnp.concatenate(
            [jnp.where(low_lane, value, none), jnp.where(low_lane, none, value)], 0
        )

    def one_head(value):
        half = value.shape[0] // 2
        return jnp.where(low_lane, value[:half], value[half:])

    def head_columns(j):
        return tuple(
            slice(part * local + j * LANES, part * local + (j + 1) * LANES)
            for part in range(3)
        )

    def attend(l, c):
        rows = slice(c * CHUNK, (c + 1) * CHUNK)
        keys = jnp.concatenate([keys_ref[...]] * (2 * CHUNK // LANES), 1)
        groups = jnp.concatenate([groups_ref[l : l + 1, rows]] * 2, 1)
        allowed = keys == groups
        for j in range(local // LANES):
            q_cols, k_cols, v_cols = head_columns(j)
            query = both_heads(packed[l, rows, q_cols] * scale)
            scores = jnp.where(allowed, dot_nt(packed[l, :, k_cols], query), -1e9)
            expo = jnp.exp(scores - jnp.max(scores, 0, keepdims=True))
            low = (expo * (1.0 / jnp.sum(expo, 0, keepdims=True))).astype(BF)
            prob[l, 2 * j, :, rows] = low[:, :CHUNK]
            prob[l, 2 * j + 1, :, rows] = low[:, CHUNK:]
            mixed[l, rows, q_cols] = one_head(dot_tn(low, packed[l, :, v_cols])).astype(BF)

    def send_product(i, l, c, *pairs):
        total = 0.0
        for left, m in pairs:
            total = total + dot_nt(left(), weight(l, m))
        xs[c] = total.astype(BF)
        if i == AHEAD and c == 0:

            @pl.when(core == 1)
            def _():
                pl.semaphore_wait(token, 1)

        send(i, c)

    def attend_out(i, l, c):
        send_product(i, l, c, (lambda: mixed[l, chunk_rows(c)], O))

    def gather_norms(l):
        norms[l] = jnp.sum(flat_rows(full[PIECES][l]).reshape(nz * ny, 8, width), 0)

    def norm_of(l, which):
        return norms[l, which : which + 1], norms[l, 2 + which : 3 + which]

    def normalize(value):
        center = value - jnp.mean(value, -1, keepdims=True)
        inverse = lax.rsqrt(jnp.mean(center * center, -1, keepdims=True) + eps)
        return center * inverse, inverse

    def expand(i, l, c):
        rows = chunk_rows(c)
        arrive(i, c)
        gain, shift = norm_of(l, 0)

        def one(r):
            sub = sub_rows(c, r)
            normed, inverse = normalize(zin[l, sub].astype(F32) + both(i, c, r))
            norm1[l, sub] = normed
            roots[sub, l : l + 1] = inverse
            hid[l, sub] = (normed * gain + shift).astype(BF)

        each(CHUNK // SUB, one)

        for m in (UA, UB):
            for part in range(units // 2 // TILE):
                cols = slice(part * TILE, (part + 1) * TILE)
                pre = dot(hid[l, rows], flat_rows(full[m][l, :, :, :, cols]))
                lower = 0.5 + 0.5 * lax.erf(pre * 0.7071067811865476)
                density = jnp.exp(-0.5 * pre * pre) * 0.3989422804014327
                start = (m - UA) * units // 2 + part * TILE
                act[l, rows, start : start + TILE] = (pre * lower).astype(BF)
                slope[l, rows, start : start + TILE] = (lower + pre * density).astype(BF)

    def halves(ref, l, rows):
        low, high = slice(0, units // 2), slice(units // 2, units)
        return (lambda: ref[l, rows, low]), (lambda: ref[l, rows, high])

    def contract(i, l, c):
        low, high = halves(act, l, chunk_rows(c))
        send_product(i, l, c, (low, DA), (high, DB))

    def second_norm(i, l, c, r):
        sub = sub_rows(c, r)
        gain, shift = norm_of(l, 0)
        hidden = norm1[l, sub] * gain + shift
        return normalize(hidden + both(i, c, r))

    def norm_back(grad, normed, inverse, gain):
        scaled = grad * gain
        inner = (
            scaled
            - jnp.mean(scaled, -1, keepdims=True)
            - normed * jnp.mean(scaled * normed, -1, keepdims=True)
        )
        return inner * inverse

    def count(l, which, grad, normed):
        ng[l, which : which + 1] += jnp.sum(grad * normed, 0, keepdims=True)
        ng[l, 2 + which : 3 + which] += jnp.sum(grad, 0, keepdims=True)

    def top_back(l, c, r, grad, normed, inverse):
        sub = sub_rows(c, r)
        count(l, 1, grad, normed)
        back = norm_back(grad, normed, inverse, norm_of(l, 1)[0])
        gsum[sub] = back
        gtok[sub] = back.astype(BF)

    def expand_back(i, l, c):
        rows = chunk_rows(c)
        for m in (DA, DB):
            cols = slice((m - DA) * units // 2, (m - DA + 1) * units // 2)
            grad = dot(gtok[rows], flat_rows(full[m][l]))
            slope[l, rows, cols] = (grad * slope[l, rows, cols].astype(F32)).astype(BF)

        low, high = halves(slope, l, rows)
        send_product(i, l, c, (low, UA), (high, UB))

    def weight_grad(l, m, source, right, start=0):
        gather_drain(l, m)
        span = 2 * local if m == QK else full[m].shape[-1]
        grad = dot_tn(source[...], right[l, :, start : start + span]).astype(BF)
        grad = grad.reshape(nz, ny, block, span)
        if m == QK:
            full[m][l, :, :, 0] = grad[..., 0:local]
            full[m][l, :, :, 1] = grad[..., local:span]
        else:
            full[m][l] = grad
        sum_start(l, m)

    def attend_back(l):
        for j in range(local // LANES):
            q_cols, k_cols, v_cols = head_columns(j)
            grad = both_heads(gmix[:, q_cols])
            low = jnp.concatenate([prob[l, 2 * j], prob[l, 2 * j + 1]], 1)
            wide = low.astype(F32)
            product = wide * dot_nt(packed[l, :, v_cols], grad)
            total = jnp.sum(product, 0, keepdims=True)
            back = (product - wide * total).astype(BF)
            packed[l, :, v_cols] = dot(low, grad).astype(BF)
            g_key = dot(back, both_heads(packed[l, :, q_cols]))
            g_query = one_head(dot_tn(back, packed[l, :, k_cols]))
            packed[l, :, q_cols] = (g_query * scale).astype(BF)
            packed[l, :, k_cols] = (g_key * scale).astype(BF)

    def middle_back(i, l, c):
        rows = chunk_rows(c)
        arrive(i, c)

        def one(r):
            sub = sub_rows(c, r)
            grad = gsum[sub] + both(i, c, r)
            normed = norm1[l, sub]
            count(l, 0, grad, normed)
            back = norm_back(grad, normed, roots[sub, l : l + 1], norm_of(l, 0)[0])
            gsum[sub] = back
            gtok[sub] = back.astype(BF)

        each(CHUNK // SUB, one)
        gmix[rows] = dot(gtok[rows], flat_rows(full[O][l])).astype(BF)

    def project_back(i, l, c):
        rows = chunk_rows(c)
        send_product(
            i,
            l,
            c,
            (lambda: packed[l, rows, 0 : 2 * local], QK),
            (lambda: packed[l, rows, 2 * local : 3 * local], V),
        )


    barrier = pltpu.get_barrier_semaphore()
    peers = [to_x, to_core, to_y] + [to_z(k) for k in range(1, nz)]
    for peer in peers:
        pl.semaphore_signal(barrier, inc=1, device_id=peer, device_id_type=MESH)
    entry = [
        pltpu.make_async_copy(src, dst, local_sem.at[4 + i])
        for i, (src, dst) in enumerate(
            (
                (x_ref.at[core], zin.at[0]),
                (go_ref.at[core], gtop),
                (segs_ref, segs),
            )
        )
    ]
    first_rows, top_rows, id_rows = entry
    for copy in entry:
        copy.start()
    ng[...] = jnp.zeros_like(ng)
    vectors = jnp.zeros((8, width), F32)
    full[N][core, z, y] = vectors
    full[N][core, z, y, 0:2, 0:block] = gain_ref[0].astype(F32)
    full[N][core, z, y, 2:4, 0:block] = shift_ref[0].astype(F32)
    full[N][core, z, y] = pltpu.roll(full[N][core, z, y], place * block, 1)
    pl.semaphore_wait(barrier, len(peers))

    gather_own(0, QK, V, N, O)
    gather_far(0, QK, V)
    gather_own(0, UA, UB, DA, DB)
    id_rows.wait()
    row = segs[pl.ds(core, 1)]
    mapped = jnp.zeros_like(row)
    for i in range(partner_ref.shape[1]):
        mapped = jnp.where(row == i, partner_ref[core, i], mapped)
    groups_ref[0:1] = row.astype(F32)
    groups_ref[1:2] = mapped.astype(F32)
    keys_ref[...] = jnp.broadcast_to(row.astype(F32), (LANES, length)).T
    gather_pass(0, QK)
    gather_far(0, O, N)
    gather_cross(0, N)
    gather_pass(0, V)
    gather_far(0, UA)
    gather_pass(0, N, O)
    gather_far(0, UB)
    gather_late(0, QK, V, N, O)
    gather_end(0, QK, V, N)
    gather_own(1, QK, V, N, O, UA, UB, DA, DB)
    first_rows.wait()
    gather_norms(0)
    each(chunks, lambda c: project(0, c))
    attend(0, 0)
    gather_pass(0, UA)
    gather_far(0, DA)
    gather_end(0, O)
    attend_out(0, 0, 0)
    attend(0, 1)
    attend_out(0, 0, 1)
    gather_late(0, UA)
    gather_pass(0, UB)
    gather_far(0, DB)
    gather_cross(0, DB)
    gather_end(0, UA)
    gather_late(0, UB)
    gather_pass(0, DA)
    gather_end(0, UB)
    expand(0, 0, 0)
    gather_late(0, DA)
    gather_far(1, QK, V, N, O)
    gather_cross(1, N)
    gather_pass(0, DB)
    expand(0, 0, 1)
    gather_late(0, DB)
    gather_end(0, DA, DB)
    gather_far(1, UA)
    each(chunks, lambda c: contract(1, 0, c))

    def into_second(c):
        arrive(1, c)
        gain, shift = norm_of(0, 1)

        def one(r):
            sub = sub_rows(c, r)
            normed, inverse = second_norm(1, 0, c, r)
            norm2[sub] = normed.astype(BF)
            roots[sub, 2:3] = inverse
            zin[1, sub] = (normed * gain + shift).astype(BF)

        each(CHUNK // SUB, one)

    gather_pass(1, QK, V, N, O)
    gather_far(1, UB)
    into_second(0)
    gather_late(1, QK, V, N, O)
    gather_pass(1, UA)
    gather_far(1, DA)
    into_second(1)
    gather_late(1, UA)
    out_start(0, 0, zin.at[1], lo_ref)
    gather_end(1, QK, V, N)
    gather_norms(1)
    each(chunks, lambda c: project(1, c))
    gather_pass(1, UB)
    gather_far(1, DB)
    gather_cross(1, DB)
    attend(1, 0)
    gather_end(1, O)
    attend_out(2, 1, 0)
    gather_late(1, UB)
    gather_pass(1, DA)
    attend(1, 1)
    attend_out(2, 1, 1)
    gather_late(1, DA)
    gather_pass(1, DB)
    gather_end(1, UA, UB)
    expand(2, 1, 0)
    gather_late(1, DB)
    gather_end(1, DA, DB)
    contract(3, 1, 0)
    expand(2, 1, 1)
    contract(3, 1, 1)
    top_rows.wait()

    def over_top(c):
        arrive(3, c)
        if c == 0 and AHEAD == 3:

            @pl.when(core == 0)
            def _():
                pl.semaphore_signal(token, inc=1, device_id=to_core, device_id_type=MESH)

        gain, shift = norm_of(1, 1)

        def one(r):
            sub = sub_rows(c, r)
            normed, inverse = second_norm(3, 1, c, r)
            top_back(1, c, r, gtop[sub].astype(F32), normed, inverse)
            gtop[sub] = (normed * gain + shift).astype(BF)

        each(CHUNK // SUB, one)

    over_top(0)
    expand_back(4, 1, 0)
    over_top(1)
    expand_back(4, 1, 1)
    out_start(1, 1, gtop, lo_ref)
    weight_grad(1, DA, gtok, act)
    weight_grad(1, DB, gtok, act, units // 2)
    weight_grad(1, UA, hid.at[1], slope)
    weight_grad(1, UB, hid.at[1], slope, units // 2)
    middle_back(4, 1, 0)
    sum_first(1, DA)
    sum_first(1, DB)
    middle_back(4, 1, 1)
    attend_back(1)
    sum_first(1, UA)
    sum_first(1, UB)
    each(chunks, lambda c: project_back(5, 1, c))
    weight_grad(1, O, gtok, mixed)
    weight_grad(1, QK, zin.at[1], packed)
    weight_grad(1, V, zin.at[1], packed, 2 * local)
    vec_start(1)
    sum_second(1, DA)
    sum_second(1, DB)
    sum_first(1, O)
    sum_first(1, QK)
    sum_first(1, V)

    def under(c):
        arrive(5, c)

        def one(r):
            sub = sub_rows(c, r)
            low = (gsum[sub] + both(5, c, r)).astype(BF)
            gin[sub] = low
            top_back(0, c, r, low.astype(F32), norm2[sub].astype(F32), roots[sub, 2:3])

        each(CHUNK // SUB, one)
        expand_back(6, 0, c)

    under(0)
    sum_second(1, UA)
    sum_second(1, UB)
    under(1)
    out_start(1, 3, gin, ig_ref)
    weight_grad(0, DA, gtok, act)
    weight_grad(0, DB, gtok, act, units // 2)
    weight_grad(0, UA, hid.at[0], slope)
    sum_first(0, DA)
    weight_grad(0, UB, hid.at[0], slope, units // 2)
    sum_relay(1, DA)
    sum_relay(1, DB)
    vec_first(1)
    sum_first(0, DB)
    middle_back(6, 0, 0)
    sum_relay(1, UA)
    sum_relay(1, UB)
    sum_second(1, O)
    sum_second(1, QK)
    sum_second(1, V)
    middle_back(6, 0, 1)
    sum_first(0, UA)
    attend_back(0)
    sum_second(0, DA)
    each(chunks, lambda c: project_back(7, 0, c))
    sum_first(0, UB)
    weight_grad(0, O, gtok, mixed)
    weight_grad(0, QK, zin.at[0], packed)
    weight_grad(0, V, zin.at[0], packed, 2 * local)
    vec_start(0)
    sum_first(0, O)
    sum_first(0, QK)
    sum_first(0, V)
    vec_first(0)
    sum_relay(1, O)
    sum_relay(1, QK)
    sum_relay(1, V)
    vec_second(1)
    sum_second(0, DB)
    sum_relay(0, DA)
    sum_second(0, UA)
    sum_relay(0, DB)

    def bottom(c):
        arrive(7, c)

        def one(r):
            sub = sub_rows(c, r)
            gtop[sub] = (gsum[sub] + both(7, c, r)).astype(BF)

        each(CHUNK // SUB, one)

    out_wait(1, 1, gtop, lo_ref)
    bottom(0)
    sum_second(0, UB)
    sum_relay(0, UA)
    sum_second(0, O)
    sum_second(0, QK)
    sum_second(0, V)
    vec_second(0)
    bottom(1)
    out_start(0, 2, gtop, ig_ref)
    sum_relay(0, UB)
    sum_last(0, DA)
    sum_last(0, DB)
    sum_relay(0, O)
    sum_relay(0, QK)
    sum_relay(0, V)
    for m in (DA, DB, UA, UB, O, QK, V):
        sum_last(1, m)
    vec_last(1)
    for m in range(PIECES):
        sum_drain(1, m)
    vec_drain(1)
    for m in (DA, DB, UA, UB):
        sum_drain(0, m)
    gather_drain(0, N)
    gather_drain(1, N)
    sum_last(0, UA)
    sum_last(0, UB)
    vec_last(0)
    sum_last(0, O)
    sum_last(0, QK)
    sum_last(0, V)
    for m in (O, QK, V):
        sum_drain(0, m)
    vec_drain(0)
    for m in range(PIECES):
        result_out(m).wait()
    norm_out().wait()
    out_wait(0, 0, zin.at[1], lo_ref)
    out_wait(0, 2, gtop, ig_ref)
    out_wait(1, 3, gin, ig_ref)


def fused(sizes, x, grad, segments, partner, gains, shifts, shards_in):
    nz, ny, length, width, local, units, eps, scale = sizes
    block = width // (nz * ny)
    chunks = length // CHUNK
    tiles = ((2, block, local),) + ((block, local),) * 2 + ((block, units // 2),) * 4
    dma = pltpu.SemaphoreType.DMA
    vmem = pltpu.VMEM
    scratch = [vmem((2, nz, ny) + tile, BF) for tile in tiles]
    scratch += [vmem((2, nz, ny, 8, width), F32)]
    scratch += [vmem((nz, ny) + tile, BF) for tile in tiles]
    scratch += [vmem((nz,) + tile, BF) for tile in tiles]
    scratch += [vmem((nz,) + tile, BF) for tile in tiles]
    scratch += [vmem(tile, F32) for tile in tiles]
    scratch += [
        vmem((length, LANES), F32),
        vmem((2, length), F32),
        vmem((2, length), jnp.int32),
        vmem((8, LANES), F32),
        vmem((8, width), F32),
        vmem((8, width), F32),
        vmem((nz - 1, 8, width), F32),
        vmem((4, 8, width), F32),
        vmem((2, length, width), BF),
        vmem((2, length, 3 * local), BF),
        vmem((2, local // HEAD, length, length), BF),
        vmem((2, length, local), BF),
        vmem((2, length, width), F32),
        vmem((2, length, width), BF),
        vmem((2, length, units), BF),
        vmem((2, length, units), BF),
        vmem((length, width), BF),
        vmem((length, 4), F32),
        vmem((length, width), F32),
        vmem((length, width), BF),
        vmem((length, local), BF),
        vmem((length, width), BF),
        vmem((length, width), BF),
        vmem((2, 8, width), F32),
        vmem((chunks, CHUNK, width), BF),
        vmem((2, chunks, CHUNK, width), BF),
        pltpu.SemaphoreType.REGULAR,
        dma((10,)),
        dma((PIECES,)),
        dma((PIECES,)),
        dma((4,)),
        dma((4,)),
        dma((chunks,)),
        dma((2, chunks)),
        dma((PIECES + 1, 2, nz)),
        dma((PIECES + 1, 2, nz)),
        dma((PIECES + 1, nz)),
        dma((PIECES + 1, nz)),
        dma((PIECES + 1, 2 * nz)),
        dma((PIECES + 1, 2 * nz)),
        dma((PIECES + 1, 2)),
        dma((PIECES + 1, 2)),
        dma((PIECES + 1, nz)),
        dma((PIECES + 1, nz)),
        dma((PIECES + 1, nz - 1)),
        dma((PIECES + 1, nz)),
    ]
    anywhere = pl.BlockSpec(memory_space=pl.ANY)
    inside = pl.BlockSpec(memory_space=pltpu.VMEM)
    outs = (
        ((2, length, width), BF),
        ((2, length, width), BF),
        ((3, block, local), F32),
        ((block, local), F32),
        ((block, units), F32),
        ((block, units), F32),
        ((8, LANES), F32),
    )
    return pl.pallas_call(
        functools.partial(kernel, sizes),
        out_shape=[jax.ShapeDtypeStruct(*out) for out in outs],
        in_specs=[pl.BlockSpec(memory_space=pltpu.SMEM)] + [inside] * 2 + [anywhere] * 7,
        out_specs=[anywhere] * len(outs),
        scratch_shapes=scratch,
        compiler_params=pltpu.CompilerParams(
            collective_id=0, has_side_effects=True, vmem_limit_bytes=127 << 19
        ),
    )(partner, gains, shifts, x, grad, segments, *shards_in)


def place_results(*refs):
    count = (len(refs) - 2) // 3
    srcs, dsts, held = refs[:count], refs[count : 2 * count], refs[2 * count : 3 * count]
    into, out = refs[3 * count :]
    for i in range(count):
        pltpu.make_async_copy(srcs[i], held[i], into.at[i]).start()
    for i in range(count):
        pltpu.make_async_copy(srcs[i], held[i], into.at[i]).wait()
        pltpu.make_async_copy(held[i], dsts[i], out.at[i]).start()
    for i in range(count):
        pltpu.make_async_copy(held[i], dsts[i], out.at[i]).wait()


def placed_results(*items):
    dma = pltpu.SemaphoreType.DMA
    anywhere = pl.BlockSpec(memory_space=pl.ANY)
    return pl.pallas_call(
        place_results,
        out_shape=[jax.ShapeDtypeStruct(item.shape, item.dtype) for item in items],
        in_specs=[anywhere] * len(items),
        out_specs=[anywhere] * len(items),
        scratch_shapes=[pltpu.VMEM(item.shape, item.dtype) for item in items]
        + [dma((len(items),)), dma((len(items),))],
        compiler_params=pltpu.CompilerParams(vmem_limit_bytes=127 << 19),
    )(*items)


def kernel_shards(
    inputs, segments, partner, grad_output, w_qkv, w_out, w_up, w_down, norm_gain, norm_shift
):
    parts = lax.axis_size("dp")
    length, width = inputs.shape[1:]
    local, units = w_out.shape[1], w_up.shape[2]
    block = width // parts
    sizes = (parts // 2, 2, length, width, local, units, norm_eps, score_scale)
    shards_in = (w_qkv[0].transpose(1, 0, 2), w_out[0].T, w_up[0], w_down[0].T)
    outs = fused(
        sizes, inputs, grad_output, segments, partner, norm_gain, norm_shift, shards_in
    )
    *whole, norm = outs
    layer_outputs, input_grads, g_qkv, g_out, g_up, g_down = placed_results(*whole)
    return (
        layer_outputs[None],
        input_grads[None],
        g_qkv.transpose(1, 0, 2)[None],
        g_out.T[None],
        g_up[None],
        g_down.T[None],
        norm[None, 0:2, 0:block],
        norm[None, 2:4, 0:block],
    )


def solution(mesh):
    placed = (
        P("dp", None, None),
        P("dp", None),
        P("dp", None),
        P("dp", None, None),
        P("section", "dp", None, "tensor"),
        P("section", "tensor", "dp"),
        P("section", "dp", "tensor"),
        P("section", "tensor", "dp"),
        P("section", None, "dp"),
        P("section", None, "dp"),
    )
    block = WIDTH // mesh.shape["dp"]
    whole_tiles = block * mesh.shape["dp"] == WIDTH and block % 16 == 0
    return jax.shard_map(
        kernel_shards if whole_tiles else shards,
        mesh=mesh,
        in_specs=placed,
        out_specs=(
            P("section", "dp", None, None),
            P("section", "dp", None, None),
            P("section", "dp", None, "tensor"),
            P("section", "tensor", "dp"),
            P("section", "dp", "tensor"),
            P("section", "tensor", "dp"),
            P("section", None, "dp"),
            P("section", None, "dp"),
        ),
        check_vma=False,
    )
```
